32 devices in a mesh: cfg: 2 (over core), pipe: 4 (over y, x), seq: 4 (over z).
Axes of the slice: x: 2, y: 2, z: 4, core: 2. Of those that a mesh axis runs over, the one named last changes fastest.
Arguments:
- latent: bfloat16 [4, 32, 2048], P(None, 'seq'), may hold values from -6 to 6
- modulation: float32 [4, 2, 3, 2048], P('pipe', 'cfg'), may hold values from -4 to 4
- qkv_weight: bfloat16 [4, 2048, 6144], P('pipe', None, 'seq'), may hold values from -0.125 to 0.125
- out_weight: bfloat16 [4, 2048, 2048], P('pipe', 'seq'), may hold values from -0.125 to 0.125
- norm_gain: float32 [4, 2, 128], P('pipe'), may hold values from 1.2 to 2
- stale_kv: bfloat16 [4, 2, 2, 4, 4, 4, 8, 512], P('pipe', 'cfg', None, None, 'seq'), may hold values from -2 to 2
Outputs:
- guided: bfloat16 [4, 32, 2048], P('pipe', 'seq', 'cfg')
- next_kv: bfloat16 [4, 2, 2, 4, 4, 4, 8, 512], P('pipe', 'cfg', None, None, 'seq')
The draws below stay inside these ranges and needn't reach their ends.
All inputs are finite; a program needn't handle non-finite values.
Results may differ from the reference program's by a relative error of at most 0.033.
Values may be sent and summed in bfloat16 or wider, within the bound.
No kernel may reach another device: no remote copies, remote signals or barrier semaphores. Data moves between devices by JAX's collectives and lax.ppermute only.
A program may use at most 64 MiB of HBM per device.

```python
import math
import jax
import jax.numpy as jnp
from jax import lax

HEAD_DIM = 128
HEADS = 16
D = 2048
TOK_DEV = 8
PATCHES = 4
TOKP = 32
SLICES = 4
MEMBERS = 1
HEAD_LOCAL = 4
N_PIPE = 4
N_SEQ = 4


def block_scale(key, extent, cuts, low, top_value):
    gain = 1.0
    for axis_at, blocks in cuts:
        steps = jax.random.uniform(jax.random.fold_in(jax.random.fold_in(key, 6), axis_at), (blocks,), jnp.float32, low / len(cuts), top_value / len(cuts))
        gain = gain * jnp.repeat(jnp.exp(steps), extent[axis_at] // blocks).reshape((-1,) + (1,) * (len(extent) - 1 - axis_at))
    return gain


def normal_values(rng, shape, deviation, limit, cuts=(), kind=jnp.bfloat16):
    drawn = jax.random.normal(rng, shape, jnp.float32) * deviation
    if len(cuts) > 0:
        drawn = block_scale(rng, shape, cuts, -0.22, 0.18) * drawn
    return jnp.clip(drawn, min=-limit, max=limit).astype(kind)


def setup_inputs(seed: int = 0) -> dict:
    streams_of = jax.random.split(jax.random.key(seed), 7)
    latent = normal_values(streams_of[0], (PATCHES, TOKP, D), 1.0, 6.0, ((1, 4),))
    modulation = normal_values(streams_of[1], (N_PIPE, 2, 3, D), 1.0, 4.0, ((0, 4), (1, 2)), jnp.float32)
    qkv_weight = normal_values(streams_of[2], (N_PIPE, D, 3 * D), D ** -0.5, 0.125, ((0, 4), (2, 4)))
    out_weight = normal_values(streams_of[3], (N_PIPE, D, D), D ** -0.5, 0.125, ((0, 4), (1, 4)))
    norm_gain = jnp.clip(1.2 + 0.79999995 * jax.random.uniform(streams_of[4], (N_PIPE, 2, HEAD_DIM), jnp.float32) ** block_scale(streams_of[4], (N_PIPE, 2, HEAD_DIM), ((0, 4),), -0.2, 0.2), 1.2, 2.0)
    stale_kv = jnp.clip(jax.random.uniform(streams_of[5], (N_PIPE, 2, 2, PATCHES, N_SEQ, SLICES, TOK_DEV, HEAD_LOCAL * HEAD_DIM), jnp.float32, -2.0, 2.0) * block_scale(streams_of[5], (N_PIPE, 2, 2, PATCHES, N_SEQ, SLICES, TOK_DEV, HEAD_LOCAL * HEAD_DIM), ((0, 4), (1, 2), (4, 4)), -0.4, 0.0), -2.0, 2.0).astype(jnp.bfloat16)
    return dict(latent=latent, modulation=modulation, qkv_weight=qkv_weight, out_weight=out_weight, norm_gain=norm_gain, stale_kv=stale_kv)


GUIDANCE_SCALE = 6.0
EPSILON = 1e-06

def layer_norm(values):
    center = values - lax.optimization_barrier(jnp.mean(values, axis=-1, keepdims=True))
    spread = lax.optimization_barrier(jnp.mean(center * center, axis=-1, keepdims=True))
    return center * lax.rsqrt(spread + EPSILON)

def head_norm(values, gain_row):
    return values * lax.rsqrt(lax.optimization_barrier(jnp.mean(values * values, axis=-1, keepdims=True)) + EPSILON) * gain_row

def attend(queries, key_rows, value_rows):

    def one_head(operands):
        query_head, key_head, value_head = operands
        scores = jnp.dot(query_head, key_head.T, preferred_element_type=jnp.float32) / math.sqrt(HEAD_DIM)
        weights = jnp.exp(scores)
        weight_total = lax.optimization_barrier(jnp.sum(weights, axis=-1, keepdims=True))
        summed = jnp.dot(weights.astype(jnp.bfloat16), value_head, preferred_element_type=jnp.float32)
        return (summed / weight_total).astype(jnp.bfloat16)
    return lax.map(one_head, (queries, key_rows, value_rows))

def reference(latent, modulation, qkv_weight, out_weight, norm_gain, stale_kv):
    stored = stale_kv.reshape(N_PIPE, 2, 2, PATCHES, SLICES, MEMBERS, SLICES, TOK_DEV, HEAD_LOCAL, HEAD_DIM)
    stored = stored.transpose(0, 1, 2, 3, 6, 5, 7, 4, 8, 9).reshape(N_PIPE, 2, 2, PATCHES, TOKP, HEADS, HEAD_DIM)
    member_of = jnp.arange(TOKP, dtype=jnp.int32) // TOK_DEV % MEMBERS
    patch_ids = jnp.arange(PATCHES, dtype=jnp.int32)
    finals = []
    kept_caches = []
    for branch in range(2):
        carried = [latent[patch_index] for patch_index in range(PATCHES)]
        section_caches = []
        for section_index in range(N_PIPE):
            shift_row = modulation[section_index, branch, 0]
            scale_row = modulation[section_index, branch, 1]
            gate_row = modulation[section_index, branch, 2]
            stale_keys = stored[section_index, branch, 0]
            stale_values = stored[section_index, branch, 1]
            fresh_keys = stale_keys
            fresh_values = stale_values
            for patch_index in range(PATCHES):
                hidden_in = carried[patch_index]
                normed = layer_norm(hidden_in.astype(jnp.float32))
                modulated = (normed * (1.0 + scale_row) + shift_row).astype(jnp.bfloat16)
                mixed = jnp.dot(modulated, qkv_weight[section_index], preferred_element_type=jnp.float32)
                mixed = mixed.reshape(TOKP, HEADS, 3, HEAD_DIM)
                queries = head_norm(mixed[:, :, 0], norm_gain[section_index, 0]).astype(jnp.bfloat16)
                new_keys = head_norm(mixed[:, :, 1], norm_gain[section_index, 1]).astype(jnp.bfloat16)
                new_values = mixed[:, :, 2].astype(jnp.bfloat16)
                fresh_keys = fresh_keys.at[patch_index].set(new_keys)
                fresh_values = fresh_values.at[patch_index].set(new_values)
                grouped = queries.reshape(SLICES, MEMBERS, TOK_DEV, HEADS, HEAD_DIM)
                pieces = []
                for member in range(MEMBERS):
                    use_fresh = jnp.logical_and(patch_ids[:, None] <= patch_index, member_of[None, :] == member)
                    key_view = jnp.where(use_fresh[:, :, None, None], fresh_keys, stale_keys)
                    value_view = jnp.where(use_fresh[:, :, None, None], fresh_values, stale_values)
                    key_view = key_view.reshape(PATCHES * TOKP, HEADS, HEAD_DIM).transpose(1, 0, 2)
                    value_view = value_view.reshape(PATCHES * TOKP, HEADS, HEAD_DIM).transpose(1, 0, 2)
                    rows = grouped[:, member].reshape(SLICES * TOK_DEV, HEADS, HEAD_DIM).transpose(1, 0, 2)
                    attended_rows = attend(rows, key_view, value_view)
                    pieces.append(attended_rows.transpose(1, 0, 2).reshape(SLICES, TOK_DEV, D))
                attended = jnp.stack(pieces, axis=1).reshape(TOKP, D)
                projected = jnp.dot(attended, out_weight[section_index], preferred_element_type=jnp.float32)
                carried[patch_index] = (hidden_in.astype(jnp.float32) + gate_row * projected).astype(jnp.bfloat16)
            section_caches.append(jnp.stack((fresh_keys, fresh_values)))
        finals.append(jnp.stack(carried))
        kept_caches.append(jnp.stack(section_caches))
    conditional = finals[0].astype(jnp.float32)
    unconditional = finals[1].astype(jnp.float32)
    guided = (unconditional + GUIDANCE_SCALE * (conditional - unconditional)).astype(jnp.bfloat16)
    next_kv = jnp.stack(kept_caches).transpose(1, 0, 2, 3, 4, 5, 6)
    next_kv = next_kv.reshape(N_PIPE, 2, 2, PATCHES, SLICES, MEMBERS, TOK_DEV, SLICES, HEAD_LOCAL, HEAD_DIM)
    next_kv = next_kv.transpose(0, 1, 2, 3, 7, 5, 4, 6, 8, 9)
    next_kv = next_kv.reshape(N_PIPE, 2, 2, PATCHES, N_SEQ, SLICES, TOK_DEV, HEAD_LOCAL * HEAD_DIM)
    return (guided, next_kv)
```

```python
import math

import jax
import jax.numpy as jnp
from jax import lax
from jax.sharding import PartitionSpec as P

GUIDANCE_SCALE = 6.0
EPSILON = 1e-06
GROUPS = 1


def swapped(value, axis, bit):
    return lax.ppermute(value, axis, [(i, i ^ 1 << bit) for i in range(lax.axis_size(axis))])


def from_behind(value, axis, steps):
    count = lax.axis_size(axis)
    return lax.ppermute(value, axis, [(i, i + steps) for i in range(count - steps)])


def layer_norm(values):
    center = values - jnp.mean(values, axis=-1, keepdims=True)
    spread = jnp.mean(center * center, axis=-1, keepdims=True)
    return center * lax.rsqrt(spread + EPSILON)


def head_norm(values, gain_row):
    return (
        values * lax.rsqrt(jnp.mean(values * values, axis=-1, keepdims=True) + EPSILON) * gain_row
    )


def join_pair(is_upper, mine, theirs, axis_dim):
    return jnp.where(
        is_upper,
        jnp.concatenate((theirs, mine), axis_dim),
        jnp.concatenate((mine, theirs), axis_dim),
    )


def local(latent, modulation, qkv_weight, out_weight, norm_gain, stale_kv):
    seq_count = lax.axis_size("seq")
    seq_rank = lax.axis_index("seq")
    section_count = lax.axis_size("pipe")
    section_rank = lax.axis_index("pipe")
    patches, tok_dev, model_width = latent.shape
    head_dim = norm_gain.shape[2]
    slice_count = min(seq_count, 8)
    member_count = seq_count // slice_count
    member_bits = member_count.bit_length() - 1
    own_member = seq_rank % member_count
    local_width = stale_kv.shape[7]
    local_heads = local_width // head_dim
    group_rows = slice_count * tok_dev
    divisor = math.sqrt(head_dim)
    shift_row = modulation[0, 0, 0]
    scale_row = modulation[0, 0, 1]
    gate_row = modulation[0, 0, 2]
    query_gain = norm_gain[0, 0]
    key_gain = norm_gain[0, 1]
    own_cache = stale_kv[0, 0].reshape(2, patches, group_rows, local_width)
    group_cache = own_cache[None]
    qkv_slice = qkv_weight[0]
    out_slice = out_weight[0]
    for level_index in range(member_bits):
        got_qkv, got_out, got_cache = (
            swapped(qkv_slice, "seq", level_index),
            swapped(out_slice, "seq", level_index),
            swapped(group_cache, "seq", level_index),
        )
        is_upper = own_member >> level_index & 1 == 1
        qkv_slice = join_pair(is_upper, qkv_slice, got_qkv, 1)
        out_slice = join_pair(is_upper, out_slice, got_out, 0)
        group_cache = join_pair(is_upper, group_cache, got_cache, 0)
    stale_rows = group_cache.swapaxes(0, 1).reshape(2, -1, local_width)
    peers = None
    if member_count > 1:
        peers = [
            [a + member_count * b for b in range(slice_count)] for a in range(member_count)
        ]

    def exchange(value):
        return lax.all_to_all(value, "seq", 0, 0, axis_index_groups=peers)

    size = patches // GROUPS
    ticks = GROUPS + section_count - 1
    stale_patch = jnp.tile(jnp.repeat(jnp.arange(patches), group_rows), member_count)
    stale_member = jnp.repeat(jnp.arange(member_count), patches * group_rows)
    row_patch = jnp.repeat(jnp.arange(size), group_rows)
    incoming = None
    fresh_ticks = []
    result_ticks = []
    for tick in range(ticks):
        group = tick - section_rank
        if incoming is None:
            hidden_in = latent[:size]
        elif tick < GROUPS:
            hidden_in = jnp.where(
                section_rank == 0, latent[tick * size : (tick + 1) * size], incoming
            )
        else:
            hidden_in = incoming
        normed = layer_norm(hidden_in.astype(jnp.float32))
        modulated = (normed * (1.0 + scale_row) + shift_row).astype(jnp.bfloat16)
        features = exchange(jnp.broadcast_to(modulated[None], (slice_count,) + modulated.shape))
        features = features.swapaxes(0, 1).reshape(size * group_rows, model_width)
        mixed = jnp.dot(features, qkv_slice, preferred_element_type=jnp.float32)
        mixed = mixed.reshape(size * group_rows, local_heads, 3, head_dim)
        queries = head_norm(mixed[:, :, 0], query_gain).astype(jnp.bfloat16)
        fresh = jnp.stack((head_norm(mixed[:, :, 1], key_gain), mixed[:, :, 2])).astype(
            jnp.bfloat16
        )
        fresh_ticks.append(fresh)
        query_patch = group * size + row_patch
        seen = fresh_ticks[-GROUPS:]
        masks = []
        for back in range(len(seen) - 1, -1, -1):
            key_patch = (group - back) * size + row_patch
            masks.append(
                jnp.logical_and(
                    key_patch[None, :] >= 0, key_patch[None, :] <= query_patch[:, None]
                )
            )
        masks.append(
            jnp.logical_or(
                stale_patch[None, :] > query_patch[:, None], stale_member[None, :] != own_member
            )
        )
        mask = jnp.concatenate(masks, axis=1)
        tables = [f.reshape(2, size * group_rows, local_heads, head_dim) for f in seen]
        tables.append(stale_rows.reshape(2, -1, local_heads, head_dim))
        view = jnp.concatenate(tables, axis=1)
        scores = (
            jnp.einsum("qhd,khd->hqk", queries, view[0], preferred_element_type=jnp.float32)
            / divisor
        )
        weights = jnp.where(mask[None], jnp.exp(scores), 0.0)
        weight_total = jnp.sum(weights, axis=-1)
        summed = jnp.einsum(
            "hqk,khd->qhd",
            weights.astype(jnp.bfloat16),
            view[1],
            preferred_element_type=jnp.float32,
        )
        attended = (
            (summed / weight_total.T[:, :, None])
            .astype(jnp.bfloat16)
            .reshape(size * group_rows, local_width)
        )
        partial_out = jnp.dot(attended, out_slice, preferred_element_type=jnp.float32)
        partial_out = partial_out.astype(jnp.bfloat16).reshape(
            size, slice_count, tok_dev, model_width
        )
        parts = exchange(partial_out.swapaxes(0, 1))
        projected = jnp.sum(parts.astype(jnp.float32), axis=0)
        hidden_out = (hidden_in.astype(jnp.float32) + gate_row * projected).astype(jnp.bfloat16)
        result_ticks.append(hidden_out)
        if tick < ticks - 1:
            incoming = from_behind(hidden_out, "pipe", 1)

    fresh_all = jnp.stack(fresh_ticks)
    next_cache = lax.dynamic_slice_in_dim(fresh_all, section_rank, GROUPS, 0)
    next_cache = next_cache.swapaxes(0, 1).reshape(stale_kv.shape)
    results = jnp.concatenate(result_ticks[section_count - 1 :], axis=0)
    per_section = patches // section_count
    half = model_width // 2
    results = results.reshape(section_count, per_section * tok_dev, 2, half)
    results = results.transpose(2, 0, 1, 3).reshape(2 * section_count, per_section * tok_dev, half)
    got = lax.all_to_all(results, ("cfg", "pipe"), 0, 0)
    got = got.reshape(2, section_count, per_section, tok_dev, half)[:, section_count - 1]
    got = got.astype(jnp.float32)
    guided = (got[1] + GUIDANCE_SCALE * (got[0] - got[1])).astype(jnp.bfloat16)
    return (guided, next_cache)


def solution(mesh):
    placed = (
        P(None, "seq", None),
        P("pipe", "cfg", None, None),
        P("pipe", None, "seq"),
        P("pipe", "seq", None),
        P("pipe", None, None),
        P("pipe", "cfg", None, None, "seq", None, None, None),
    )
    return jax.shard_map(
        local,
        mesh=mesh,
        in_specs=placed,
        out_specs=(P("pipe", "seq", "cfg"), P("pipe", "cfg", None, None, "seq", None, None, None)),
        check_vma=False,
    )
```

```python
import math

import jax
import jax.numpy as jnp
from jax import lax
from jax.sharding import PartitionSpec as P

GUIDANCE_SCALE = 6.0
EPSILON = 1e-06
GROUPS = 1


def swapped(value, axis, bit):
    return lax.ppermute(value, axis, [(i, i ^ 1 << bit) for i in range(lax.axis_size(axis))])


def from_behind(value, axis, steps):
    count = lax.axis_size(axis)
    return lax.ppermute(value, axis, [(i, i + steps) for i in range(count - steps)])


def layer_norm(values):
    center = values - jnp.mean(values, axis=-1, keepdims=True)
    spread = jnp.mean(center * center, axis=-1, keepdims=True)
    return center * lax.rsqrt(spread + EPSILON)


def head_norm(values, gain_row):
    return (
        values * lax.rsqrt(jnp.mean(values * values, axis=-1, keepdims=True) + EPSILON) * gain_row
    )


def join_pair(is_upper, mine, theirs, axis_dim):
    return jnp.where(
        is_upper,
        jnp.concatenate((theirs, mine), axis_dim),
        jnp.concatenate((mine, theirs), axis_dim),
    )


def local(latent, modulation, qkv_weight, out_weight, norm_gain, stale_kv):
    seq_count = lax.axis_size("seq")
    seq_rank = lax.axis_index("seq")
    section_count = lax.axis_size("pipe")
    section_rank = lax.axis_index("pipe")
    patches, tok_dev, model_width = latent.shape
    head_dim = norm_gain.shape[2]
    slice_count = min(seq_count, 8)
    member_count = seq_count // slice_count
    member_bits = member_count.bit_length() - 1
    own_member = seq_rank % member_count
    local_width = stale_kv.shape[7]
    local_heads = local_width // head_dim
    group_rows = slice_count * tok_dev
    divisor = math.sqrt(head_dim)
    shift_row = modulation[0, 0, 0]
    scale_row = modulation[0, 0, 1]
    gate_row = modulation[0, 0, 2]
    query_gain = norm_gain[0, 0]
    key_gain = norm_gain[0, 1]
    own_cache = stale_kv[0, 0].reshape(2, patches, group_rows, local_width)
    group_cache = own_cache[None]
    qkv_slice = qkv_weight[0]
    out_slice = out_weight[0]
    for level_index in range(member_bits):
        got_qkv, got_out, got_cache = (
            swapped(qkv_slice, "seq", level_index),
            swapped(out_slice, "seq", level_index),
            swapped(group_cache, "seq", level_index),
        )
        is_upper = own_member >> level_index & 1 == 1
        qkv_slice = join_pair(is_upper, qkv_slice, got_qkv, 1)
        out_slice = join_pair(is_upper, out_slice, got_out, 0)
        group_cache = join_pair(is_upper, group_cache, got_cache, 0)
    stale_rows = group_cache.swapaxes(0, 1).reshape(2, -1, local_width)
    peers = None
    if member_count > 1:
        peers = [
            [a + member_count * b for b in range(slice_count)] for a in range(member_count)
        ]

    size = patches // GROUPS
    ticks = GROUPS + section_count - 1
    stale_patch = jnp.tile(jnp.repeat(jnp.arange(patches), group_rows), member_count)
    stale_member = jnp.repeat(jnp.arange(member_count), patches * group_rows)
    row_patch = jnp.repeat(jnp.arange(size), group_rows)
    incoming = None
    fresh_ticks = []
    result_ticks = []
    for tick in range(ticks):
        group = tick - section_rank
        if incoming is None:
            hidden_in = latent[:size]
        elif tick < GROUPS:
            hidden_in = jnp.where(
                section_rank == 0, latent[tick * size : (tick + 1) * size], incoming
            )
        else:
            hidden_in = incoming
        normed = layer_norm(hidden_in.astype(jnp.float32))
        modulated = (normed * (1.0 + scale_row) + shift_row).astype(jnp.bfloat16)
        features = lax.all_gather(modulated, "seq", axis_index_groups=peers)
        features = features.swapaxes(0, 1).reshape(size * group_rows, model_width)
        mixed = jnp.dot(features, qkv_slice, preferred_element_type=jnp.float32)
        mixed = mixed.reshape(size * group_rows, local_heads, 3, head_dim)
        queries = head_norm(mixed[:, :, 0], query_gain).astype(jnp.bfloat16)
        fresh = jnp.stack((head_norm(mixed[:, :, 1], key_gain), mixed[:, :, 2])).astype(
            jnp.bfloat16
        )
        fresh_ticks.append(fresh)
        query_patch = group * size + row_patch
        seen = fresh_ticks[-GROUPS:]
        masks = []
        for back in range(len(seen) - 1, -1, -1):
            key_patch = (group - back) * size + row_patch
            masks.append(
                jnp.logical_and(
                    key_patch[None, :] >= 0, key_patch[None, :] <= query_patch[:, None]
                )
            )
        masks.append(
            jnp.logical_or(
                stale_patch[None, :] > query_patch[:, None], stale_member[None, :] != own_member
            )
        )
        mask = jnp.concatenate(masks, axis=1)
        tables = [f.reshape(2, size * group_rows, local_heads, head_dim) for f in seen]
        tables.append(stale_rows.reshape(2, -1, local_heads, head_dim))
        view = jnp.concatenate(tables, axis=1)
        scores = (
            jnp.einsum("qhd,khd->hqk", queries, view[0], preferred_element_type=jnp.float32)
            / divisor
        )
        weights = jnp.where(mask[None], jnp.exp(scores), 0.0)
        weight_total = jnp.sum(weights, axis=-1)
        summed = jnp.einsum(
            "hqk,khd->qhd",
            weights.astype(jnp.bfloat16),
            view[1],
            preferred_element_type=jnp.float32,
        )
        attended = (
            (summed / weight_total.T[:, :, None])
            .astype(jnp.bfloat16)
            .reshape(size * group_rows, local_width)
        )
        partial_out = jnp.dot(attended, out_slice, preferred_element_type=jnp.float32)
        partial_out = partial_out.astype(jnp.bfloat16).reshape(
            size, slice_count, tok_dev, model_width
        )
        projected = lax.psum_scatter(
            partial_out.swapaxes(0, 1), "seq", axis_index_groups=peers
        ).astype(jnp.float32)
        hidden_out = (hidden_in.astype(jnp.float32) + gate_row * projected).astype(jnp.bfloat16)
        result_ticks.append(hidden_out)
        if tick < ticks - 1:
            incoming = from_behind(hidden_out, "pipe", 1)

    fresh_all = jnp.stack(fresh_ticks)
    next_cache = lax.dynamic_slice_in_dim(fresh_all, section_rank, GROUPS, 0)
    next_cache = next_cache.swapaxes(0, 1).reshape(stale_kv.shape)
    results = jnp.concatenate(result_ticks[section_count - 1 :], axis=0)
    per_section = patches // section_count
    half = model_width // 2
    results = results.reshape(section_count, per_section * tok_dev, 2, half)
    results = results.transpose(2, 0, 1, 3).reshape(2 * section_count, per_section * tok_dev, half)
    got = lax.all_to_all(results, ("cfg", "pipe"), 0, 0)
    got = got.reshape(2, section_count, per_section, tok_dev, half)[:, section_count - 1]
    got = got.astype(jnp.float32)
    guided = (got[1] + GUIDANCE_SCALE * (got[0] - got[1])).astype(jnp.bfloat16)
    return (guided, next_cache)


def solution(mesh):
    placed = (
        P(None, "seq", None),
        P("pipe", "cfg", None, None),
        P("pipe", None, "seq"),
        P("pipe", "seq", None),
        P("pipe", None, None),
        P("pipe", "cfg", None, None, "seq", None, None, None),
    )
    return jax.shard_map(
        local,
        mesh=mesh,
        in_specs=placed,
        out_specs=(P("pipe", "seq", "cfg"), P("pipe", "cfg", None, None, "seq", None, None, None)),
        check_vma=False,
    )
```

```python
import math

import jax
import jax.numpy as jnp
from jax import lax
from jax.sharding import PartitionSpec as P

GUIDANCE_SCALE = 6.0
EPSILON = 1e-06


def swapped(value, axis, bit):
    return lax.ppermute(value, axis, [(i, i ^ 1 << bit) for i in range(lax.axis_size(axis))])


def layer_norm(values):
    center = values - jnp.mean(values, axis=-1, keepdims=True)
    spread = jnp.mean(center * center, axis=-1, keepdims=True)
    return center * lax.rsqrt(spread + EPSILON)


def head_norm(values, gain_row):
    return (
        values * lax.rsqrt(jnp.mean(values * values, axis=-1, keepdims=True) + EPSILON) * gain_row
    )


def join_pair(is_upper, mine, theirs, axis_dim):
    return jnp.where(
        is_upper,
        jnp.concatenate((theirs, mine), axis_dim),
        jnp.concatenate((mine, theirs), axis_dim),
    )


def local(latent, modulation, qkv_weight, out_weight, norm_gain, stale_kv):
    seq_count = lax.axis_size("seq")
    seq_rank = lax.axis_index("seq")
    section_count = lax.axis_size("pipe")
    section_rank = lax.axis_index("pipe")
    branch_rank = lax.axis_index("cfg")
    patches, tok_dev, model_width = latent.shape
    head_dim = norm_gain.shape[2]
    slice_count = min(seq_count, 8)
    member_count = seq_count // slice_count
    member_bits = member_count.bit_length() - 1
    own_member = seq_rank % member_count
    local_width = stale_kv.shape[7]
    local_heads = local_width // head_dim
    group_rows = slice_count * tok_dev
    divisor = math.sqrt(head_dim)
    shift_row = modulation[0, 0, 0]
    scale_row = modulation[0, 0, 1]
    gate_row = modulation[0, 0, 2]
    query_gain = norm_gain[0, 0]
    key_gain = norm_gain[0, 1]
    own_cache = stale_kv[0, 0].reshape(2, patches, group_rows, local_width)
    group_cache = own_cache[None]
    qkv_slice = qkv_weight[0]
    out_slice = out_weight[0]
    for level_index in range(member_bits):
        got_qkv, got_out, got_cache = (
            swapped(qkv_slice, "seq", level_index),
            swapped(out_slice, "seq", level_index),
            swapped(group_cache, "seq", level_index),
        )
        is_upper = own_member >> level_index & 1 == 1
        qkv_slice = join_pair(is_upper, qkv_slice, got_qkv, 1)
        out_slice = join_pair(is_upper, out_slice, got_out, 0)
        group_cache = join_pair(is_upper, group_cache, got_cache, 0)
    stale_rows = group_cache.swapaxes(0, 1).reshape(2, -1, local_width)
    homes = section_count * slice_count
    per_home = patches // section_count
    rows = patches * group_rows
    peers = None
    if member_count > 1:
        peers = [
            [
                q * seq_count + a + member_count * b
                for q in range(section_count)
                for b in range(slice_count)
            ]
            for a in range(member_count)
        ]

    def exchange(value):
        return lax.all_to_all(value, ("pipe", "seq"), 0, 0, axis_index_groups=peers)

    patch_of = jnp.repeat(jnp.arange(patches), group_rows)
    stale_patch = jnp.tile(patch_of, member_count)
    stale_member = jnp.repeat(jnp.arange(member_count), rows)
    mask = jnp.concatenate(
        (
            patch_of[None, :] <= patch_of[:, None],
            jnp.logical_or(
                stale_patch[None, :] > patch_of[:, None], stale_member[None, :] != own_member
            ),
        ),
        axis=1,
    )
    hidden = lax.dynamic_slice_in_dim(latent, section_rank * per_home, per_home, 0)
    next_cache = None
    for section in range(section_count):
        features = exchange(jnp.broadcast_to(hidden[None], (homes,) + hidden.shape))
        features = features.reshape(section_count, slice_count, per_home, tok_dev, model_width)
        features = features.swapaxes(1, 2).reshape(rows, model_width)
        normed = layer_norm(features.astype(jnp.float32))
        modulated = (normed * (1.0 + scale_row) + shift_row).astype(jnp.bfloat16)
        mixed = jnp.dot(modulated, qkv_slice, preferred_element_type=jnp.float32)
        mixed = mixed.reshape(rows, local_heads, 3, head_dim)
        queries = head_norm(mixed[:, :, 0], query_gain).astype(jnp.bfloat16)
        fresh = jnp.stack((head_norm(mixed[:, :, 1], key_gain), mixed[:, :, 2])).astype(
            jnp.bfloat16
        )
        next_cache = (
            fresh if next_cache is None else jnp.where(section_rank == section, fresh, next_cache)
        )
        view = jnp.concatenate(
            (fresh, stale_rows.reshape(2, -1, local_heads, head_dim)), axis=1
        )
        scores = (
            jnp.einsum("qhd,khd->hqk", queries, view[0], preferred_element_type=jnp.float32)
            / divisor
        )
        weights = jnp.where(mask[None], jnp.exp(scores), 0.0)
        weight_total = jnp.sum(weights, axis=-1)
        summed = jnp.einsum(
            "hqk,khd->qhd",
            weights.astype(jnp.bfloat16),
            view[1],
            preferred_element_type=jnp.float32,
        )
        attended = (
            (summed / weight_total.T[:, :, None]).astype(jnp.bfloat16).reshape(rows, local_width)
        )
        partial_out = jnp.dot(attended, out_slice, preferred_element_type=jnp.float32)
        partial_out = (gate_row * partial_out).astype(jnp.bfloat16)
        partial_out = partial_out.reshape(
            section_count, per_home, slice_count, tok_dev, model_width
        )
        partial_out = partial_out.swapaxes(1, 2).reshape(homes, per_home, tok_dev, model_width)
        parts = exchange(partial_out)
        parts = parts[section * slice_count : (section + 1) * slice_count].astype(jnp.float32)
        hidden = (hidden.astype(jnp.float32) + jnp.sum(parts, axis=0)).astype(jnp.bfloat16)

    next_cache = next_cache.reshape(stale_kv.shape)
    half = model_width // 2
    kept = lax.dynamic_slice_in_dim(hidden, branch_rank * half, half, 2)
    sent = lax.dynamic_slice_in_dim(hidden, (1 - branch_rank) * half, half, 2)
    got = swapped(sent, "cfg", 0)
    conditional = jnp.where(branch_rank == 0, kept, got).astype(jnp.float32)
    unconditional = jnp.where(branch_rank == 0, got, kept).astype(jnp.float32)
    guided = (unconditional + GUIDANCE_SCALE * (conditional - unconditional)).astype(jnp.bfloat16)
    return (guided, next_cache)


def solution(mesh):
    placed = (
        P(None, "seq", None),
        P("pipe", "cfg", None, None),
        P("pipe", None, "seq"),
        P("pipe", "seq", None),
        P("pipe", None, None),
        P("pipe", "cfg", None, None, "seq", None, None, None),
    )
    return jax.shard_map(
        local,
        mesh=mesh,
        in_specs=placed,
        out_specs=(P("pipe", "seq", "cfg"), P("pipe", "cfg", None, None, "seq", None, None, None)),
        check_vma=False,
    )
```

```python
import functools
import math

import jax
import jax.numpy as jnp
from jax import lax
from jax.experimental import pallas as pl
from jax.experimental.pallas import tpu as pltpu
from jax.sharding import PartitionSpec as P

GUIDANCE_SCALE = 6.0
EPSILON = 1e-06
GROUPS = 2


def swapped(value, axis, bit):
    return lax.ppermute(value, axis, [(i, i ^ 1 << bit) for i in range(lax.axis_size(axis))])


def head_norm(values, gain_row):
    return (
        values * lax.rsqrt(jnp.mean(values * values, axis=-1, keepdims=True) + EPSILON) * gain_row
    )


def join_pair(is_upper, mine, theirs, axis_dim):
    return jnp.where(
        is_upper,
        jnp.concatenate((theirs, mine), axis_dim),
        jnp.concatenate((mine, theirs), axis_dim),
    )


def section_kernel(sizes, where_ref, rows_ref, mod_ref, qkv_ref, out_ref, gain_ref, stale_ref, *refs):
    *prev_refs, partial_ref, fresh_ref = refs
    patches, tok_dev, group_rows, head_dim = sizes
    blocks, slices, block_rows, block_cols = rows_ref.shape
    rows = slices * block_rows
    width = blocks * block_cols
    in_group = block_rows // tok_dev
    heads = stale_ref.shape[2] // head_dim
    group, own_member = where_ref[0], where_ref[1]
    parts = [rows_ref[q].reshape(rows, block_cols).astype(jnp.float32) for q in range(blocks)]
    mean = sum(jnp.sum(x, axis=-1, keepdims=True) for x in parts) / width
    parts = [x - mean for x in parts]
    spread = sum(jnp.sum(x * x, axis=-1, keepdims=True) for x in parts) / width
    inverse = lax.rsqrt(spread + EPSILON)
    modulated = []
    for q, x in enumerate(parts):
        at = pl.ds(q * block_cols, block_cols)
        modulated.append(
            (x * inverse * (1.0 + mod_ref[1:2, at]) + mod_ref[0:1, at]).astype(jnp.bfloat16)
        )
    modulated = jnp.concatenate(modulated, axis=1)
    mixed = jnp.dot(modulated, qkv_ref[...], preferred_element_type=jnp.float32)

    def patch_in_group(shape, axis):
        return lax.broadcasted_iota(jnp.int32, shape, axis) // tok_dev % in_group

    square = (rows, rows)
    masks = []
    for back in range(len(prev_refs), 0, -1):
        masks.append(jnp.broadcast_to(group >= back, square))
    masks.append(patch_in_group(square, 1) <= patch_in_group(square, 0))
    wide = (rows, stale_ref.shape[1])
    key_at = lax.broadcasted_iota(jnp.int32, wide, 1)
    masks.append(
        jnp.logical_or(
            key_at // group_rows % patches > group * in_group + patch_in_group(wide, 0),
            key_at // (group_rows * patches) != own_member,
        )
    )
    attended = []
    for head in range(heads):
        at = slice(head * head_dim, (head + 1) * head_dim)
        query, key, value = (
            mixed[:, (3 * head + j) * head_dim : (3 * head + j + 1) * head_dim] for j in range(3)
        )
        query = head_norm(query, gain_ref[0:1, :]).astype(jnp.bfloat16)
        key = head_norm(key, gain_ref[1:2, :]).astype(jnp.bfloat16)
        value = value.astype(jnp.bfloat16)
        fresh_ref[0, :, at] = key
        fresh_ref[1, :, at] = value
        keys = [ref[0, :, at] for ref in prev_refs] + [key, stale_ref[0, :, at]]
        values = [ref[1, :, at] for ref in prev_refs] + [value, stale_ref[1, :, at]]
        total = 0.0
        summed = 0.0
        for mask, key_rows, value_rows in zip(masks, keys, values):
            scores = lax.dot_general(
                query, key_rows, (((1,), (1,)), ((), ())), preferred_element_type=jnp.float32
            )
            weights = jnp.where(mask, jnp.exp(scores / math.sqrt(head_dim)), 0.0)
            total = total + jnp.sum(weights, axis=-1, keepdims=True)
            summed = summed + jnp.dot(
                weights.astype(jnp.bfloat16), value_rows, preferred_element_type=jnp.float32
            )
        attended.append((summed / total).astype(jnp.bfloat16))
    attended = jnp.concatenate(attended, axis=1)
    projected = jnp.dot(attended, out_ref[...], preferred_element_type=jnp.float32)
    projected = (mod_ref[2:3, :] * projected).astype(jnp.bfloat16)
    for q in range(blocks):
        partial_ref[q] = projected[:, q * block_cols : (q + 1) * block_cols].reshape(
            slices, block_rows, block_cols
        )


def local(latent, modulation, qkv_weight, out_weight, norm_gain, stale_kv):
    seq_count = lax.axis_size("seq")
    seq_rank = lax.axis_index("seq")
    section_count = lax.axis_size("pipe")
    section_rank = lax.axis_index("pipe")
    branch_rank = lax.axis_index("cfg")
    patches, tok_dev, model_width = latent.shape
    head_dim = norm_gain.shape[2]
    slice_count = min(seq_count, 8)
    member_count = seq_count // slice_count
    member_bits = member_count.bit_length() - 1
    own_member = seq_rank % member_count
    local_width = stale_kv.shape[7]
    group_rows = slice_count * tok_dev
    own_cache = stale_kv[0, 0].reshape(2, patches, group_rows, local_width)
    group_cache = own_cache[None]
    qkv_slice = qkv_weight[0]
    out_slice = out_weight[0]
    for level_index in range(member_bits):
        got_qkv, got_out, got_cache = (
            swapped(qkv_slice, "seq", level_index),
            swapped(out_slice, "seq", level_index),
            swapped(group_cache, "seq", level_index),
        )
        is_upper = own_member >> level_index & 1 == 1
        qkv_slice = join_pair(is_upper, qkv_slice, got_qkv, 1)
        out_slice = join_pair(is_upper, out_slice, got_out, 0)
        group_cache = join_pair(is_upper, group_cache, got_cache, 0)
    stale_rows = group_cache.swapaxes(0, 1).reshape(2, -1, local_width)
    homes = section_count * slice_count
    in_group = patches // GROUPS
    block_rows = in_group * tok_dev
    block_cols = model_width // section_count
    rows = slice_count * block_rows
    peers = None
    if member_count > 1:
        peers = [
            [
                q * seq_count + a + member_count * b
                for q in range(section_count)
                for b in range(slice_count)
            ]
            for a in range(member_count)
        ]

    def exchange(value):
        value = value.reshape(homes, block_rows, block_cols)
        value = lax.all_to_all(value, ("pipe", "seq"), 0, 0, axis_index_groups=peers)
        return value.reshape(section_count, slice_count, block_rows, block_cols)

    in_vmem = functools.partial(pltpu.with_memory_space_constraint, memory_space=pltpu.VMEM)
    qkv_slice, out_slice = in_vmem(qkv_slice), in_vmem(out_slice)

    def attend(group, features, prev):
        vmem = pl.BlockSpec(memory_space=pltpu.VMEM)
        return pl.pallas_call(
            functools.partial(section_kernel, (patches, tok_dev, group_rows, head_dim)),
            out_shape=(
                jax.ShapeDtypeStruct(features.shape, jnp.bfloat16),
                jax.ShapeDtypeStruct((2, rows, local_width), jnp.bfloat16),
            ),
            in_specs=[pl.BlockSpec(memory_space=pltpu.SMEM)] + [vmem] * (6 + len(prev)),
            out_specs=(vmem, vmem),
            compiler_params=pltpu.CompilerParams(vmem_limit_bytes=24 * 1024 * 1024),
        )(
            jnp.stack((group, own_member)).astype(jnp.int32),
            features,
            modulation[0, 0],
            qkv_slice,
            out_slice,
            norm_gain[0],
            stale_rows,
            *prev,
        )

    sources = lax.dynamic_slice_in_dim(
        latent.reshape(GROUPS, block_rows, model_width), section_rank * block_cols, block_cols, 2
    )
    zeros = jnp.zeros_like(sources[0])
    streams = jnp.stack([sources[0]] + [zeros] * (section_count - 1))
    fresh_ticks = []
    finals = []
    for tick in range(GROUPS + section_count - 1):
        features = exchange(
            jnp.broadcast_to(
                streams[:, None], (section_count, slice_count, block_rows, block_cols)
            )
        )
        prev = fresh_ticks[-(GROUPS - 1) :] if GROUPS > 1 else []
        partial_out, fresh = attend(tick - section_rank, features, prev)
        fresh_ticks.append(fresh)
        parts = exchange(partial_out).astype(jnp.float32)
        results = (streams.astype(jnp.float32) + jnp.sum(parts, axis=1)).astype(jnp.bfloat16)
        finals.append(results[-1])
        entering = sources[tick + 1] if tick + 1 < GROUPS else zeros
        streams = jnp.concatenate((entering[None], results[:-1]))

    next_cache = lax.dynamic_slice_in_dim(jnp.stack(fresh_ticks), section_rank, GROUPS, 0)
    next_cache = next_cache.reshape(GROUPS, 2, slice_count, in_group, tok_dev, local_width)
    next_cache = next_cache.transpose(1, 0, 3, 2, 4, 5).reshape(stale_kv.shape)
    per_home = patches // section_count
    finals = jnp.stack(finals[section_count - 1 :])
    finals = finals.reshape(1, section_count, per_home, tok_dev, block_cols)
    finals = jnp.broadcast_to(finals, (2,) + finals.shape[1:])
    got = lax.all_to_all(
        finals.reshape((-1,) + finals.shape[2:]), ("cfg", "pipe"), 0, 0
    ).reshape(finals.shape)
    half = section_count // 2
    got = lax.dynamic_slice_in_dim(got, branch_rank * half, half, 1).astype(jnp.float32)
    guided = (got[1] + GUIDANCE_SCALE * (got[0] - got[1])).astype(jnp.bfloat16)
    guided = guided.transpose(1, 2, 0, 3).reshape(per_home, tok_dev, half * block_cols)
    return (guided, next_cache)


def solution(mesh):
    placed = (
        P(None, "seq", None),
        P("pipe", "cfg", None, None),
        P("pipe", None, "seq"),
        P("pipe", "seq", None),
        P("pipe", None, None),
        P("pipe", "cfg", None, None, "seq", None, None, None),
    )
    return jax.shard_map(
        local,
        mesh=mesh,
        in_specs=placed,
        out_specs=(P("pipe", "seq", "cfg"), P("pipe", "cfg", None, None, "seq", None, None, None)),
        check_vma=False,
    )
```

```python
import functools
import math

import jax
import jax.numpy as jnp
from jax import lax
from jax.experimental import pallas as pl
from jax.experimental.pallas import tpu as pltpu
from jax.sharding import PartitionSpec as P

GUIDANCE_SCALE = 6.0
EPSILON = 1e-06
GROUPS = 2


def swapped(value, axis, bit):
    return lax.ppermute(value, axis, [(i, i ^ 1 << bit) for i in range(lax.axis_size(axis))])


def head_norm(values, gain_row):
    return (
        values * lax.rsqrt(jnp.mean(values * values, axis=-1, keepdims=True) + EPSILON) * gain_row
    )


def join_pair(is_upper, mine, theirs, axis_dim):
    return jnp.where(
        is_upper,
        jnp.concatenate((theirs, mine), axis_dim),
        jnp.concatenate((mine, theirs), axis_dim),
    )


def section_kernel(sizes, where_ref, rows_ref, mod_ref, qkv_ref, out_ref, gain_ref, stale_ref, *refs):
    *prev_refs, partial_ref, fresh_ref = refs
    patches, tok_dev, group_rows, head_dim = sizes
    blocks, slices, block_rows, block_cols = rows_ref.shape
    rows = slices * block_rows
    width = blocks * block_cols
    in_group = block_rows // tok_dev
    heads = stale_ref.shape[2] // head_dim
    group, own_member = where_ref[0], where_ref[1]
    parts = [rows_ref[q].reshape(rows, block_cols).astype(jnp.float32) for q in range(blocks)]
    mean = sum(jnp.sum(x, axis=-1, keepdims=True) for x in parts) / width
    parts = [x - mean for x in parts]
    spread = sum(jnp.sum(x * x, axis=-1, keepdims=True) for x in parts) / width
    inverse = lax.rsqrt(spread + EPSILON)
    modulated = []
    for q, x in enumerate(parts):
        at = pl.ds(q * block_cols, block_cols)
        modulated.append(
            (x * inverse * (1.0 + mod_ref[1:2, at]) + mod_ref[0:1, at]).astype(jnp.bfloat16)
        )
    modulated = jnp.concatenate(modulated, axis=1)
    mixed = jnp.dot(modulated, qkv_ref[...], preferred_element_type=jnp.float32)

    def patch_in_group(shape, axis):
        return lax.broadcasted_iota(jnp.int32, shape, axis) // tok_dev % in_group

    square = (rows, rows)
    masks = []
    for back in range(len(prev_refs), 0, -1):
        masks.append(jnp.broadcast_to(group >= back, square))
    masks.append(patch_in_group(square, 1) <= patch_in_group(square, 0))
    wide = (rows, stale_ref.shape[1])
    key_at = lax.broadcasted_iota(jnp.int32, wide, 1)
    masks.append(
        jnp.logical_or(
            key_at // group_rows % patches > group * in_group + patch_in_group(wide, 0),
            key_at // (group_rows * patches) != own_member,
        )
    )
    attended = []
    for head in range(heads):
        at = slice(head * head_dim, (head + 1) * head_dim)
        query, key, value = (
            mixed[:, (3 * head + j) * head_dim : (3 * head + j + 1) * head_dim] for j in range(3)
        )
        query = head_norm(query, gain_ref[0:1, :]).astype(jnp.bfloat16)
        key = head_norm(key, gain_ref[1:2, :]).astype(jnp.bfloat16)
        value = value.astype(jnp.bfloat16)
        fresh_ref[0, :, at] = key
        fresh_ref[1, :, at] = value
        keys = [ref[0, :, at] for ref in prev_refs] + [key, stale_ref[0, :, at]]
        values = [ref[1, :, at] for ref in prev_refs] + [value, stale_ref[1, :, at]]
        total = 0.0
        summed = 0.0
        for mask, key_rows, value_rows in zip(masks, keys, values):
            scores = lax.dot_general(
                query, key_rows, (((1,), (1,)), ((), ())), preferred_element_type=jnp.float32
            )
            weights = jnp.where(mask, jnp.exp(scores / math.sqrt(head_dim)), 0.0)
            total = total + jnp.sum(weights, axis=-1, keepdims=True)
            summed = summed + jnp.dot(
                weights.astype(jnp.bfloat16), value_rows, preferred_element_type=jnp.float32
            )
        attended.append((summed / total).astype(jnp.bfloat16))
    attended = jnp.concatenate(attended, axis=1)
    projected = jnp.dot(attended, out_ref[...], preferred_element_type=jnp.float32)
    projected = (mod_ref[2:3, :] * projected).astype(jnp.bfloat16)
    for q in range(blocks):
        partial_ref[q] = projected[:, q * block_cols : (q + 1) * block_cols].reshape(
            slices, block_rows, block_cols
        )


def load_kernel(qkv_ref, out_ref, qkv_to, out_to, sems):
    copies = (
        pltpu.make_async_copy(qkv_ref, qkv_to, sems.at[0]),
        pltpu.make_async_copy(out_ref, out_to, sems.at[1]),
    )
    for copy in copies:
        copy.start()
    for copy in copies:
        copy.wait()


def settle_kernel(parts_ref, streams_ref, entering_ref, streams_to, spread_to, last_to):
    count, slices = parts_ref.shape[:2]
    for section in range(count):
        total = streams_ref[section].astype(jnp.float32)
        for piece in range(slices):
            total = total + parts_ref[section, piece].astype(jnp.float32)
        total = total.astype(jnp.bfloat16)
        if section == count - 1:
            last_to[...] = total
        else:
            streams_to[section + 1] = total
            for piece in range(slices):
                spread_to[section + 1, piece] = total
    streams_to[0] = entering_ref[...]
    for piece in range(slices):
        spread_to[0, piece] = entering_ref[...]


def local(latent, modulation, qkv_weight, out_weight, norm_gain, stale_kv):
    seq_count = lax.axis_size("seq")
    seq_rank = lax.axis_index("seq")
    section_count = lax.axis_size("pipe")
    section_rank = lax.axis_index("pipe")
    branch_rank = lax.axis_index("cfg")
    patches, tok_dev, model_width = latent.shape
    head_dim = norm_gain.shape[2]
    slice_count = min(seq_count, 8)
    member_count = seq_count // slice_count
    member_bits = member_count.bit_length() - 1
    own_member = seq_rank % member_count
    local_width = stale_kv.shape[7]
    group_rows = slice_count * tok_dev
    own_cache = stale_kv[0, 0].reshape(2, patches, group_rows, local_width)
    group_cache = own_cache[None]
    qkv_slice = qkv_weight[0]
    out_slice = out_weight[0]
    for level_index in range(member_bits):
        got_qkv, got_out, got_cache = (
            swapped(qkv_slice, "seq", level_index),
            swapped(out_slice, "seq", level_index),
            swapped(group_cache, "seq", level_index),
        )
        is_upper = own_member >> level_index & 1 == 1
        qkv_slice = join_pair(is_upper, qkv_slice, got_qkv, 1)
        out_slice = join_pair(is_upper, out_slice, got_out, 0)
        group_cache = join_pair(is_upper, group_cache, got_cache, 0)
    stale_rows = group_cache.swapaxes(0, 1).reshape(2, -1, local_width)
    homes = section_count * slice_count
    in_group = patches // GROUPS
    block_rows = in_group * tok_dev
    block_cols = model_width // section_count
    rows = slice_count * block_rows
    peers = None
    if member_count > 1:
        peers = [
            [
                q * seq_count + a + member_count * b
                for q in range(section_count)
                for b in range(slice_count)
            ]
            for a in range(member_count)
        ]

    def exchange(value):
        value = value.reshape(homes, block_rows, block_cols)
        value = lax.all_to_all(value, ("pipe", "seq"), 0, 0, axis_index_groups=peers)
        return value.reshape(section_count, slice_count, block_rows, block_cols)

    vmem = pl.BlockSpec(memory_space=pltpu.VMEM)
    in_vmem = functools.partial(pltpu.with_memory_space_constraint, memory_space=pltpu.VMEM)
    qkv_slice, out_slice = pl.pallas_call(
        load_kernel,
        out_shape=(
            pltpu.VMEM(qkv_slice.shape, jnp.bfloat16),
            pltpu.VMEM(out_slice.shape, jnp.bfloat16),
        ),
        in_specs=[pl.BlockSpec(memory_space=pltpu.HBM)] * 2,
        out_specs=(vmem, vmem),
        scratch_shapes=[pltpu.SemaphoreType.DMA((2,))],
        compiler_params=pltpu.CompilerParams(vmem_limit_bytes=1024 * 1024),
        cost_estimate=pl.CostEstimate(
            flops=0, bytes_accessed=4 * (qkv_slice.size + out_slice.size), transcendentals=0
        ),
    )(*(pltpu.with_memory_space_constraint(w, pltpu.HBM) for w in (qkv_slice, out_slice)))

    def attend(group, features, prev):
        return pl.pallas_call(
            functools.partial(section_kernel, (patches, tok_dev, group_rows, head_dim)),
            out_shape=(
                jax.ShapeDtypeStruct(features.shape, jnp.bfloat16),
                jax.ShapeDtypeStruct((2, rows, local_width), jnp.bfloat16),
            ),
            in_specs=[pl.BlockSpec(memory_space=pltpu.SMEM)] + [vmem] * (6 + len(prev)),
            out_specs=(vmem, vmem),
            compiler_params=pltpu.CompilerParams(vmem_limit_bytes=24 * 1024 * 1024),
        )(
            jnp.stack((group, own_member)).astype(jnp.int32),
            features,
            modulation[0, 0],
            in_vmem(qkv_slice),
            in_vmem(out_slice),
            norm_gain[0],
            stale_rows,
            *prev,
        )

    sources = lax.dynamic_slice_in_dim(
        latent.reshape(GROUPS, block_rows, model_width), section_rank * block_cols, block_cols, 2
    )
    spread_shape = (section_count, slice_count, block_rows, block_cols)
    zeros = jnp.zeros_like(sources[0])
    streams = jnp.stack([sources[0]] + [zeros] * (section_count - 1))
    spread = jnp.broadcast_to(streams[:, None], spread_shape)

    def settle(parts, streams, entering):
        return pl.pallas_call(
            settle_kernel,
            out_shape=tuple(
                jax.ShapeDtypeStruct(shape, jnp.bfloat16)
                for shape in (streams.shape, spread_shape, entering.shape)
            ),
            in_specs=[vmem] * 3,
            out_specs=(vmem,) * 3,
            compiler_params=pltpu.CompilerParams(vmem_limit_bytes=8 * 1024 * 1024),
        )(parts, streams, entering)

    fresh_ticks = []
    finals = []
    for tick in range(GROUPS + section_count - 1):
        features = exchange(spread)
        prev = fresh_ticks[-(GROUPS - 1) :] if GROUPS > 1 else []
        partial_out, fresh = attend(tick - section_rank, features, prev)
        fresh_ticks.append(fresh)
        entering = sources[tick + 1] if tick + 1 < GROUPS else zeros
        streams, spread, last = settle(exchange(partial_out), streams, entering)
        finals.append(last)

    next_cache = lax.dynamic_slice_in_dim(jnp.stack(fresh_ticks), section_rank, GROUPS, 0)
    next_cache = next_cache.reshape(GROUPS, 2, slice_count, in_group, tok_dev, local_width)
    next_cache = next_cache.transpose(1, 0, 3, 2, 4, 5).reshape(stale_kv.shape)
    per_home = patches // section_count
    finals = jnp.stack(finals[section_count - 1 :])
    finals = finals.reshape(1, section_count, per_home, tok_dev, block_cols)
    finals = jnp.broadcast_to(finals, (2,) + finals.shape[1:])
    got = lax.all_to_all(
        finals.reshape((-1,) + finals.shape[2:]), ("cfg", "pipe"), 0, 0
    ).reshape(finals.shape)
    half = section_count // 2
    got = lax.dynamic_slice_in_dim(got, branch_rank * half, half, 1).astype(jnp.float32)
    guided = (got[1] + GUIDANCE_SCALE * (got[0] - got[1])).astype(jnp.bfloat16)
    guided = guided.transpose(1, 2, 0, 3).reshape(per_home, tok_dev, half * block_cols)
    return (guided, next_cache)


def solution(mesh):
    placed = (
        P(None, "seq", None),
        P("pipe", "cfg", None, None),
        P("pipe", None, "seq"),
        P("pipe", "seq", None),
        P("pipe", None, None),
        P("pipe", "cfg", None, None, "seq", None, None, None),
    )
    return jax.shard_map(
        local,
        mesh=mesh,
        in_specs=placed,
        out_specs=(P("pipe", "seq", "cfg"), P("pipe", "cfg", None, None, "seq", None, None, None)),
        check_vma=False,
    )
```

```python
import functools
import math

import jax
import jax.numpy as jnp
from jax import lax
from jax.experimental import pallas as pl
from jax.experimental.pallas import tpu as pltpu
from jax.sharding import PartitionSpec as P

GUIDANCE_SCALE = 6.0
EPSILON = 1e-06
GROUPS = 2


def swapped(value, axis, bit):
    return lax.ppermute(value, axis, [(i, i ^ 1 << bit) for i in range(lax.axis_size(axis))])


def head_norm(values, gain_row):
    return (
        values * lax.rsqrt(jnp.mean(values * values, axis=-1, keepdims=True) + EPSILON) * gain_row
    )


def join_pair(is_upper, mine, theirs, axis_dim):
    return jnp.where(
        is_upper,
        jnp.concatenate((theirs, mine), axis_dim),
        jnp.concatenate((mine, theirs), axis_dim),
    )


def section_kernel(tick, sizes, where_ref, rows_ref, mod_ref, qkv_ref, out_ref, gain_ref, *refs):
    *stale_refs, old_table_ref, partial_ref, table_ref = refs
    tok_dev, head_dim = sizes
    blocks, slices, block_rows, block_cols = rows_ref.shape
    rows = slices * block_rows
    width = blocks * block_cols
    in_group = block_rows // tok_dev
    group_rows = slices * tok_dev
    groups, local_width = table_ref.shape[1], table_ref.shape[3]
    heads = local_width // head_dim
    section, own_member = where_ref[0], where_ref[1]
    group = tick - section
    parts = [rows_ref[q].reshape(rows, block_cols).astype(jnp.float32) for q in range(blocks)]
    mean = sum(jnp.sum(x, axis=-1, keepdims=True) for x in parts) / width
    parts = [x - mean for x in parts]
    spread = sum(jnp.sum(x * x, axis=-1, keepdims=True) for x in parts) / width
    inverse = lax.rsqrt(spread + EPSILON)
    modulated = []
    for q, x in enumerate(parts):
        at = pl.ds(q * block_cols, block_cols)
        modulated.append(
            (x * inverse * (1.0 + mod_ref[1:2, at]) + mod_ref[0:1, at]).astype(jnp.bfloat16)
        )
    modulated = jnp.concatenate(modulated, axis=1)
    mixed = jnp.dot(modulated, qkv_ref[...], preferred_element_type=jnp.float32)

    def by_patch(values):
        values = values.reshape(slices, in_group, tok_dev, head_dim).swapaxes(0, 1)
        return values.reshape(rows, head_dim).astype(jnp.bfloat16)

    def query_patch(shape):
        return lax.broadcasted_iota(jnp.int32, shape, 0) // tok_dev % in_group

    square, wide = (rows, rows), (rows, groups * rows)
    fresh_patch = lax.broadcasted_iota(jnp.int32, square, 1) // group_rows
    old_patch = lax.broadcasted_iota(jnp.int32, wide, 1) // group_rows - group * in_group
    masks = [
        fresh_patch <= query_patch(square),
        jnp.logical_or(old_patch < 0, old_patch > query_patch(wide)),
    ]
    for ref in stale_refs:
        at = lax.broadcasted_iota(jnp.int32, (rows, ref.shape[1]), 1)
        masks.append(at // (groups * rows) != own_member)
    attended = []
    fresh = []
    for head in range(heads):
        at = slice(head * head_dim, (head + 1) * head_dim)
        query, key, value = (
            mixed[:, (3 * head + j) * head_dim : (3 * head + j + 1) * head_dim] for j in range(3)
        )
        query = head_norm(query, gain_ref[0:1, :]).astype(jnp.bfloat16)
        key = by_patch(head_norm(key, gain_ref[1:2, :]))
        value = by_patch(value)
        fresh.append((key, value))
        keys, values = (
            [new, old_table_ref[j, :, :, at].reshape(groups * rows, head_dim)]
            + [ref[j, :, at] for ref in stale_refs]
            for j, new in enumerate((key, value))
        )
        total = 0.0
        summed = 0.0
        for mask, key_rows, value_rows in zip(masks, keys, values):
            scores = lax.dot_general(
                query, key_rows, (((1,), (1,)), ((), ())), preferred_element_type=jnp.float32
            )
            weights = jnp.where(mask, jnp.exp(scores / math.sqrt(head_dim)), 0.0)
            total = total + jnp.sum(weights, axis=-1, keepdims=True)
            summed = summed + jnp.dot(
                weights.astype(jnp.bfloat16), value_rows, preferred_element_type=jnp.float32
            )
        attended.append((summed / total).astype(jnp.bfloat16))
    attended = jnp.concatenate(attended, axis=1)

    for at in range(groups):

        @pl.when(group == at)
        def _():
            for j in range(2):
                table_ref[j, at] = jnp.concatenate([pair[j] for pair in fresh], axis=1)

        @pl.when(group != at)
        def _():
            for j in range(2):
                table_ref[j, at] = old_table_ref[j, at]

    projected = jnp.dot(attended, out_ref[...], preferred_element_type=jnp.float32)
    projected = (mod_ref[2:3, :] * projected).astype(jnp.bfloat16)
    for q in range(blocks):
        partial_ref[q] = projected[:, q * block_cols : (q + 1) * block_cols].reshape(
            slices, block_rows, block_cols
        )


def start_kernel(where_ref, latent_ref, qkv_ref, out_ref, qkv_to, out_to, sources_to, streams_to, spread_to, sems):
    copies = (
        pltpu.make_async_copy(qkv_ref, qkv_to, sems.at[0]),
        pltpu.make_async_copy(out_ref, out_to, sems.at[1]),
    )
    for copy in copies:
        copy.start()
    sections, slices, _, block_cols = spread_to.shape
    for q in range(sections):

        @pl.when(where_ref[0] == q)
        def _():
            sources_to[...] = latent_ref[:, :, q * block_cols : (q + 1) * block_cols]

    first = sources_to[0]
    for section in range(sections):
        held = first if section == 0 else jnp.zeros_like(first)
        streams_to[section] = held
        for piece in range(slices):
            spread_to[section, piece] = held
    for copy in copies:
        copy.wait()


def settle_kernel(parts_ref, streams_ref, entering_ref, streams_to, spread_to, last_to):
    count, slices = parts_ref.shape[:2]
    for section in range(count):
        total = streams_ref[section].astype(jnp.float32)
        for piece in range(slices):
            total = total + parts_ref[section, piece].astype(jnp.float32)
        total = total.astype(jnp.bfloat16)
        if section == count - 1:
            last_to[...] = total
        else:
            streams_to[section + 1] = total
            for piece in range(slices):
                spread_to[section + 1, piece] = total
    streams_to[0] = entering_ref[...]
    for piece in range(slices):
        spread_to[0, piece] = entering_ref[...]


def local(latent, modulation, qkv_weight, out_weight, norm_gain, stale_kv):
    seq_count = lax.axis_size("seq")
    seq_rank = lax.axis_index("seq")
    section_count = lax.axis_size("pipe")
    section_rank = lax.axis_index("pipe")
    branch_rank = lax.axis_index("cfg")
    patches, tok_dev, model_width = latent.shape
    head_dim = norm_gain.shape[2]
    slice_count = min(seq_count, 8)
    member_count = seq_count // slice_count
    member_bits = member_count.bit_length() - 1
    own_member = seq_rank % member_count
    local_width = stale_kv.shape[7]
    group_rows = slice_count * tok_dev
    own_cache = stale_kv[0, 0].reshape(2, patches, group_rows, local_width)
    group_cache = own_cache[None]
    qkv_slice = qkv_weight[0]
    out_slice = out_weight[0]
    for level_index in range(member_bits):
        got_qkv, got_out, got_cache = (
            swapped(qkv_slice, "seq", level_index),
            swapped(out_slice, "seq", level_index),
            swapped(group_cache, "seq", level_index),
        )
        is_upper = own_member >> level_index & 1 == 1
        qkv_slice = join_pair(is_upper, qkv_slice, got_qkv, 1)
        out_slice = join_pair(is_upper, out_slice, got_out, 0)
        group_cache = join_pair(is_upper, group_cache, got_cache, 0)
    homes = section_count * slice_count
    in_group = patches // GROUPS
    block_rows = in_group * tok_dev
    block_cols = model_width // section_count
    rows = slice_count * block_rows
    peers = None
    if member_count > 1:
        peers = [
            [
                q * seq_count + a + member_count * b
                for q in range(section_count)
                for b in range(slice_count)
            ]
            for a in range(member_count)
        ]

    def exchange(value):
        value = value.reshape(homes, block_rows, block_cols)
        value = lax.all_to_all(value, ("pipe", "seq"), 0, 0, axis_index_groups=peers)
        return value.reshape(section_count, slice_count, block_rows, block_cols)

    vmem = pl.BlockSpec(memory_space=pltpu.VMEM)
    smem = pl.BlockSpec(memory_space=pltpu.SMEM)
    in_hbm = functools.partial(pltpu.with_memory_space_constraint, memory_space=pltpu.HBM)
    in_vmem = functools.partial(pltpu.with_memory_space_constraint, memory_space=pltpu.VMEM)
    where = jnp.stack((section_rank, own_member)).astype(jnp.int32)
    sources = latent.reshape(GROUPS, block_rows, model_width)
    stream_shape = (section_count, block_rows, block_cols)
    spread_shape = (section_count, slice_count, block_rows, block_cols)
    qkv_slice, out_slice, sources, streams, spread = pl.pallas_call(
        start_kernel,
        out_shape=(
            pltpu.VMEM(qkv_slice.shape, jnp.bfloat16),
            pltpu.VMEM(out_slice.shape, jnp.bfloat16),
            jax.ShapeDtypeStruct((GROUPS, block_rows, block_cols), jnp.bfloat16),
            jax.ShapeDtypeStruct(stream_shape, jnp.bfloat16),
            jax.ShapeDtypeStruct(spread_shape, jnp.bfloat16),
        ),
        in_specs=[smem, vmem] + [pl.BlockSpec(memory_space=pltpu.HBM)] * 2,
        out_specs=(vmem,) * 5,
        scratch_shapes=[pltpu.SemaphoreType.DMA((2,))],
        compiler_params=pltpu.CompilerParams(vmem_limit_bytes=4 * 1024 * 1024),
    )(where, sources, in_hbm(qkv_slice), in_hbm(out_slice))
    stale_rows = []
    if member_count > 1:
        stale_rows = [group_cache.swapaxes(0, 1).reshape(2, -1, local_width)]
    table = own_cache.reshape(2, GROUPS, rows, local_width)

    def attend(tick, features, table):
        operands = (
            where,
            features,
            modulation[0, 0],
            in_vmem(qkv_slice),
            in_vmem(out_slice),
            norm_gain[0],
            *stale_rows,
            table,
        )
        return pl.pallas_call(
            functools.partial(section_kernel, tick, (tok_dev, head_dim)),
            out_shape=(
                jax.ShapeDtypeStruct(features.shape, jnp.bfloat16),
                jax.ShapeDtypeStruct(table.shape, jnp.bfloat16),
            ),
            in_specs=[smem] + [vmem] * (len(operands) - 1),
            out_specs=(vmem, vmem),
            input_output_aliases={len(operands) - 1: 1},
            compiler_params=pltpu.CompilerParams(vmem_limit_bytes=24 * 1024 * 1024),
        )(*operands)

    def settle(parts, streams, entering):
        return pl.pallas_call(
            settle_kernel,
            out_shape=tuple(
                jax.ShapeDtypeStruct(shape, jnp.bfloat16)
                for shape in (stream_shape, spread_shape, entering.shape)
            ),
            in_specs=[vmem] * 3,
            out_specs=(vmem,) * 3,
            compiler_params=pltpu.CompilerParams(vmem_limit_bytes=8 * 1024 * 1024),
        )(parts, streams, entering)

    finals = []
    for tick in range(GROUPS + section_count - 1):
        partial_out, table = attend(tick, exchange(spread), table)
        streams, spread, last = settle(
            exchange(partial_out), streams, sources[min(tick + 1, GROUPS - 1)]
        )
        finals.append(last)

    next_cache = table.reshape(stale_kv.shape)
    per_home = patches // section_count
    finals = jnp.stack(finals[section_count - 1 :])
    finals = finals.reshape(1, section_count, per_home, tok_dev, block_cols)
    finals = jnp.broadcast_to(finals, (2,) + finals.shape[1:])
    got = lax.all_to_all(
        finals.reshape((-1,) + finals.shape[2:]), ("cfg", "pipe"), 0, 0
    ).reshape(finals.shape)
    half = section_count // 2
    got = lax.dynamic_slice_in_dim(got, branch_rank * half, half, 1).astype(jnp.float32)
    guided = (got[1] + GUIDANCE_SCALE * (got[0] - got[1])).astype(jnp.bfloat16)
    guided = guided.transpose(1, 2, 0, 3).reshape(per_home, tok_dev, half * block_cols)
    return (guided, next_cache)


def solution(mesh):
    placed = (
        P(None, "seq", None),
        P("pipe", "cfg", None, None),
        P("pipe", None, "seq"),
        P("pipe", "seq", None),
        P("pipe", None, None),
        P("pipe", "cfg", None, None, "seq", None, None, None),
    )
    return jax.shard_map(
        local,
        mesh=mesh,
        in_specs=placed,
        out_specs=(P("pipe", "seq", "cfg"), P("pipe", "cfg", None, None, "seq", None, None, None)),
        check_vma=False,
    )
```

```python
import functools
import math

import jax
import jax.numpy as jnp
from jax import lax
from jax.experimental import pallas as pl
from jax.experimental.pallas import tpu as pltpu
from jax.sharding import PartitionSpec as P

GUIDANCE_SCALE = 6.0
EPSILON = 1e-06
GROUPS = 2


def swapped(value, axis, bit):
    return lax.ppermute(value, axis, [(i, i ^ 1 << bit) for i in range(lax.axis_size(axis))])


def head_norm(values, gain_row):
    return (
        values * lax.rsqrt(jnp.mean(values * values, axis=-1, keepdims=True) + EPSILON) * gain_row
    )


def join_pair(is_upper, mine, theirs, axis_dim):
    return jnp.where(
        is_upper,
        jnp.concatenate((theirs, mine), axis_dim),
        jnp.concatenate((mine, theirs), axis_dim),
    )


def section_kernel(tick, sizes, where_ref, rows_ref, mod_ref, qkv_ref, out_ref, gain_ref, *refs):
    *stale_refs, old_table_ref, partial_ref, table_ref = refs
    tok_dev, head_dim = sizes
    blocks, slices, block_rows, block_cols = rows_ref.shape
    rows = slices * block_rows
    width = blocks * block_cols
    in_group = block_rows // tok_dev
    group_rows = slices * tok_dev
    groups, local_width = table_ref.shape[1], table_ref.shape[3]
    heads = local_width // head_dim
    section, own_member = where_ref[0], where_ref[1]
    group = tick - section
    parts = [rows_ref[q].reshape(rows, block_cols).astype(jnp.float32) for q in range(blocks)]
    mean = sum(jnp.sum(x, axis=-1, keepdims=True) for x in parts) / width
    parts = [x - mean for x in parts]
    spread = sum(jnp.sum(x * x, axis=-1, keepdims=True) for x in parts) / width
    inverse = lax.rsqrt(spread + EPSILON)
    modulated = []
    for q, x in enumerate(parts):
        at = slice(q * block_cols, (q + 1) * block_cols)
        modulated.append(
            (x * inverse * (1.0 + mod_ref[1, :, at]) + mod_ref[0, :, at]).astype(jnp.bfloat16)
        )
    modulated = jnp.concatenate(modulated, axis=1)
    mixed = jnp.dot(modulated, qkv_ref[...], preferred_element_type=jnp.float32)

    def by_patch(values):
        values = values.reshape(slices, in_group, tok_dev, head_dim).swapaxes(0, 1)
        return values.reshape(rows, head_dim).astype(jnp.bfloat16)

    def query_patch(shape):
        return lax.broadcasted_iota(jnp.int32, shape, 0) // tok_dev % in_group

    square, wide = (rows, rows), (rows, groups * rows)
    fresh_patch = lax.broadcasted_iota(jnp.int32, square, 1) // group_rows
    old_patch = lax.broadcasted_iota(jnp.int32, wide, 1) // group_rows - group * in_group
    masks = [
        fresh_patch <= query_patch(square),
        jnp.logical_or(old_patch < 0, old_patch > query_patch(wide)),
    ]
    for ref in stale_refs:
        at = lax.broadcasted_iota(jnp.int32, (rows, ref.shape[1]), 1)
        masks.append(at // (groups * rows) != own_member)
    attended = []
    fresh = []
    for head in range(heads):
        at = slice(head * head_dim, (head + 1) * head_dim)
        query, key, value = (
            mixed[:, (3 * head + j) * head_dim : (3 * head + j + 1) * head_dim] for j in range(3)
        )
        query = head_norm(query, gain_ref[0:1, :]).astype(jnp.bfloat16)
        key = by_patch(head_norm(key, gain_ref[1:2, :]))
        value = by_patch(value)
        fresh.append((key, value))
        keys, values = (
            [new, old_table_ref[j, :, :, at].reshape(groups * rows, head_dim)]
            + [ref[j, :, at] for ref in stale_refs]
            for j, new in enumerate((key, value))
        )
        total = 0.0
        summed = 0.0
        for mask, key_rows, value_rows in zip(masks, keys, values):
            scores = lax.dot_general(
                query, key_rows, (((1,), (1,)), ((), ())), preferred_element_type=jnp.float32
            )
            weights = jnp.where(mask, jnp.exp(scores / math.sqrt(head_dim)), 0.0)
            total = total + jnp.sum(weights, axis=-1, keepdims=True)
            summed = summed + jnp.dot(
                weights.astype(jnp.bfloat16), value_rows, preferred_element_type=jnp.float32
            )
        attended.append((summed / total).astype(jnp.bfloat16))
    attended = jnp.concatenate(attended, axis=1)

    projected = jnp.dot(attended, out_ref[...], preferred_element_type=jnp.float32)
    projected = (mod_ref[2] * projected).astype(jnp.bfloat16)
    for q in range(blocks):
        partial_ref[q] = projected[:, q * block_cols : (q + 1) * block_cols].reshape(
            slices, block_rows, block_cols
        )

    for at in range(groups):

        @pl.when(group == at)
        def _():
            for j in range(2):
                table_ref[j, at] = jnp.concatenate([pair[j] for pair in fresh], axis=1)

        @pl.when(group != at)
        def _():
            for j in range(2):
                table_ref[j, at] = old_table_ref[j, at]


def start_kernel(where_ref, latent_ref, *refs):
    loads = (len(refs) - 4) // 2
    from_refs, to_refs = refs[:loads], refs[loads : 2 * loads]
    sources_to, streams_to, spread_to, sems = refs[2 * loads :]
    copies = [
        pltpu.make_async_copy(from_ref, to_ref, sems.at[at])
        for at, (from_ref, to_ref) in enumerate(zip(from_refs, to_refs))
    ]
    for copy in copies:
        copy.start()
    sections, slices, _, block_cols = spread_to.shape
    for q in range(sections):

        @pl.when(where_ref[0] == q)
        def _():
            sources_to[...] = latent_ref[:, :, q * block_cols : (q + 1) * block_cols]

    first = sources_to[0]
    for section in range(sections):
        held = first if section == 0 else jnp.zeros_like(first)
        streams_to[section] = held
        for piece in range(slices):
            spread_to[section, piece] = held
    for copy in copies:
        copy.wait()


def added(parts_ref, streams_ref, section):
    total = streams_ref[section].astype(jnp.float32)
    for piece in range(parts_ref.shape[1]):
        total = total + parts_ref[section, piece].astype(jnp.float32)
    return total.astype(jnp.bfloat16)


def settle_kernel(entering, parts_ref, streams_ref, sources_ref, streams_to, spread_to, last_to):
    count, slices = parts_ref.shape[:2]
    for section in range(count):
        if section == 0:
            held = sources_ref[entering]
        else:
            held = added(parts_ref, streams_ref, section - 1)
        streams_to[section] = held
        for piece in range(slices):
            spread_to[section, piece] = held
    last_to[...] = added(parts_ref, streams_ref, count - 1)


def close_kernel(parts_ref, streams_ref, *refs):
    *last_refs, finals_to = refs
    lasts = [ref[...] for ref in last_refs]
    lasts.append(added(parts_ref, streams_ref, parts_ref.shape[0] - 1))
    finals = jnp.concatenate(lasts).reshape(finals_to.shape[1:])
    for branch in range(finals_to.shape[0]):
        finals_to[branch] = finals


def local(latent, modulation, qkv_weight, out_weight, norm_gain, stale_kv):
    seq_count = lax.axis_size("seq")
    seq_rank = lax.axis_index("seq")
    section_count = lax.axis_size("pipe")
    section_rank = lax.axis_index("pipe")
    branch_rank = lax.axis_index("cfg")
    patches, tok_dev, model_width = latent.shape
    head_dim = norm_gain.shape[2]
    slice_count = min(seq_count, 8)
    member_count = seq_count // slice_count
    member_bits = member_count.bit_length() - 1
    own_member = seq_rank % member_count
    local_width = stale_kv.shape[7]
    group_rows = slice_count * tok_dev
    own_cache = stale_kv[0, 0].reshape(2, patches, group_rows, local_width)
    group_cache = own_cache[None]
    qkv_slice = qkv_weight[0]
    out_slice = out_weight[0]
    for level_index in range(member_bits):
        got_qkv, got_out, got_cache = (
            swapped(qkv_slice, "seq", level_index),
            swapped(out_slice, "seq", level_index),
            swapped(group_cache, "seq", level_index),
        )
        is_upper = own_member >> level_index & 1 == 1
        qkv_slice = join_pair(is_upper, qkv_slice, got_qkv, 1)
        out_slice = join_pair(is_upper, out_slice, got_out, 0)
        group_cache = join_pair(is_upper, group_cache, got_cache, 0)
    homes = section_count * slice_count
    in_group = patches // GROUPS
    block_rows = in_group * tok_dev
    block_cols = model_width // section_count
    rows = slice_count * block_rows
    peers = None
    if member_count > 1:
        peers = [
            [
                q * seq_count + a + member_count * b
                for q in range(section_count)
                for b in range(slice_count)
            ]
            for a in range(member_count)
        ]

    def exchange(value):
        value = value.reshape(homes, block_rows, block_cols)
        value = lax.all_to_all(value, ("pipe", "seq"), 0, 0, axis_index_groups=peers)
        return value.reshape(section_count, slice_count, block_rows, block_cols)

    vmem = pl.BlockSpec(memory_space=pltpu.VMEM)
    smem = pl.BlockSpec(memory_space=pltpu.SMEM)
    in_hbm = functools.partial(pltpu.with_memory_space_constraint, memory_space=pltpu.HBM)
    in_vmem = functools.partial(pltpu.with_memory_space_constraint, memory_space=pltpu.VMEM)
    where = jnp.stack((section_rank, own_member)).astype(jnp.int32)
    sources = latent.reshape(GROUPS, block_rows, model_width)
    stream_shape = (section_count, block_rows, block_cols)
    spread_shape = (section_count, slice_count, block_rows, block_cols)
    loads = (
        qkv_slice,
        out_slice,
        modulation.reshape(3, 1, model_width),
        norm_gain[0],
        own_cache.reshape(2, GROUPS, rows, local_width),
    )
    qkv_slice, out_slice, modulation, norm_gain, table, sources, streams, spread = pl.pallas_call(
        start_kernel,
        out_shape=tuple(pltpu.VMEM(value.shape, value.dtype) for value in loads)
        + (
            pltpu.VMEM((GROUPS, block_rows, block_cols), jnp.bfloat16),
            jax.ShapeDtypeStruct(stream_shape, jnp.bfloat16),
            jax.ShapeDtypeStruct(spread_shape, jnp.bfloat16),
        ),
        in_specs=[smem, vmem] + [pl.BlockSpec(memory_space=pltpu.HBM)] * len(loads),
        out_specs=(vmem,) * (len(loads) + 3),
        scratch_shapes=[pltpu.SemaphoreType.DMA((len(loads),))],
        compiler_params=pltpu.CompilerParams(vmem_limit_bytes=4 * 1024 * 1024),
    )(where, sources, *map(in_hbm, loads))
    stale_rows = []
    if member_count > 1:
        stale_rows = [group_cache.swapaxes(0, 1).reshape(2, -1, local_width)]

    def attend(tick, features, table):
        operands = (
            where,
            features,
            in_vmem(modulation),
            in_vmem(qkv_slice),
            in_vmem(out_slice),
            in_vmem(norm_gain),
            *stale_rows,
            table,
        )
        return pl.pallas_call(
            functools.partial(section_kernel, tick, (tok_dev, head_dim)),
            out_shape=(
                jax.ShapeDtypeStruct(features.shape, jnp.bfloat16),
                jax.ShapeDtypeStruct(table.shape, jnp.bfloat16),
            ),
            in_specs=[smem] + [vmem] * (len(operands) - 1),
            out_specs=(vmem, vmem),
            input_output_aliases={len(operands) - 1: 1},
            compiler_params=pltpu.CompilerParams(vmem_limit_bytes=24 * 1024 * 1024),
        )(*operands)

    def settle(entering, parts, streams):
        return pl.pallas_call(
            functools.partial(settle_kernel, entering),
            out_shape=tuple(
                jax.ShapeDtypeStruct(shape, jnp.bfloat16)
                for shape in (stream_shape, spread_shape, stream_shape[1:])
            ),
            in_specs=[vmem] * 3,
            out_specs=(vmem,) * 3,
            compiler_params=pltpu.CompilerParams(vmem_limit_bytes=8 * 1024 * 1024),
        )(parts, streams, in_vmem(sources))

    lasts = []
    ticks = GROUPS + section_count - 1
    for tick in range(ticks):
        partial_out, table = attend(tick, exchange(spread), table)
        parts = exchange(partial_out)
        if tick < ticks - 1:
            streams, spread, last = settle(min(tick + 1, GROUPS - 1), parts, streams)
            lasts.append(last)

    next_cache = table.reshape(stale_kv.shape)
    per_home = patches // section_count
    finals = pl.pallas_call(
        close_kernel,
        out_shape=jax.ShapeDtypeStruct((2, patches, tok_dev, block_cols), jnp.bfloat16),
        in_specs=[vmem] * (GROUPS + 1),
        out_specs=vmem,
        compiler_params=pltpu.CompilerParams(vmem_limit_bytes=8 * 1024 * 1024),
    )(parts, streams, *lasts[section_count - 1 :])
    finals = finals.reshape(2, section_count, per_home, tok_dev, block_cols)
    got = lax.all_to_all(
        finals.reshape((-1,) + finals.shape[2:]), ("cfg", "pipe"), 0, 0
    ).reshape(finals.shape)
    half = section_count // 2
    got = lax.dynamic_slice_in_dim(got, branch_rank * half, half, 1).astype(jnp.float32)
    guided = (got[1] + GUIDANCE_SCALE * (got[0] - got[1])).astype(jnp.bfloat16)
    guided = guided.transpose(1, 2, 0, 3).reshape(per_home, tok_dev, half * block_cols)
    return (guided, next_cache)


def solution(mesh):
    placed = (
        P(None, "seq", None),
        P("pipe", "cfg", None, None),
        P("pipe", None, "seq"),
        P("pipe", "seq", None),
        P("pipe", None, None),
        P("pipe", "cfg", None, None, "seq", None, None, None),
    )
    return jax.shard_map(
        local,
        mesh=mesh,
        in_specs=placed,
        out_specs=(P("pipe", "seq", "cfg"), P("pipe", "cfg", None, None, "seq", None, None, None)),
        check_vma=False,
    )
```

```python
import functools
import math

import jax
import jax.numpy as jnp
from jax import lax
from jax.experimental import pallas as pl
from jax.experimental.pallas import tpu as pltpu
from jax.sharding import PartitionSpec as P

GUIDANCE_SCALE = 6.0
EPSILON = 1e-06
GROUPS = 2
PIECES = 8


def swapped(value, axis, bit):
    return lax.ppermute(value, axis, [(i, i ^ 1 << bit) for i in range(lax.axis_size(axis))])


def head_norm(values, gain_row):
    return (
        values * lax.rsqrt(jnp.mean(values * values, axis=-1, keepdims=True) + EPSILON) * gain_row
    )


def join_pair(is_upper, mine, theirs, axis_dim):
    return jnp.where(
        is_upper,
        jnp.concatenate((theirs, mine), axis_dim),
        jnp.concatenate((mine, theirs), axis_dim),
    )


def section_kernel(tick, sizes, where_ref, rows_ref, mod_ref, qkv_ref, out_ref, gain_ref, *refs):
    *stale_refs, old_table_ref, partial_ref, table_ref = refs
    tok_dev, head_dim = sizes
    blocks, slices, block_rows, block_cols = rows_ref.shape
    rows = slices * block_rows
    width = blocks * block_cols
    in_group = block_rows // tok_dev
    group_rows = slices * tok_dev
    groups, local_width = table_ref.shape[1], table_ref.shape[3]
    heads = local_width // head_dim
    section, own_member = where_ref[0], where_ref[1]
    group = tick - section
    parts = [rows_ref[q].reshape(rows, block_cols).astype(jnp.float32) for q in range(blocks)]
    mean = sum(jnp.sum(x, axis=-1, keepdims=True) for x in parts) / width
    parts = [x - mean for x in parts]
    spread = sum(jnp.sum(x * x, axis=-1, keepdims=True) for x in parts) / width
    inverse = lax.rsqrt(spread + EPSILON)
    modulated = []
    for q, x in enumerate(parts):
        at = slice(q * block_cols, (q + 1) * block_cols)
        modulated.append(
            (x * inverse * (1.0 + mod_ref[1, :, at]) + mod_ref[0, :, at]).astype(jnp.bfloat16)
        )
    modulated = jnp.concatenate(modulated, axis=1)
    mixed = jnp.dot(modulated, qkv_ref[...], preferred_element_type=jnp.float32)

    def by_patch(values):
        values = values.reshape(slices, in_group, tok_dev, head_dim).swapaxes(0, 1)
        return values.reshape(rows, head_dim).astype(jnp.bfloat16)

    def query_patch(shape):
        return lax.broadcasted_iota(jnp.int32, shape, 0) // tok_dev % in_group

    square, wide = (rows, rows), (rows, groups * rows)
    fresh_patch = lax.broadcasted_iota(jnp.int32, square, 1) // group_rows
    old_patch = lax.broadcasted_iota(jnp.int32, wide, 1) // group_rows - group * in_group
    masks = [
        fresh_patch <= query_patch(square),
        jnp.logical_or(old_patch < 0, old_patch > query_patch(wide)),
    ]
    for ref in stale_refs:
        at = lax.broadcasted_iota(jnp.int32, (rows, ref.shape[1]), 1)
        masks.append(at // (groups * rows) != own_member)
    attended = []
    fresh = []
    for head in range(heads):
        at = slice(head * head_dim, (head + 1) * head_dim)
        query, key, value = (
            mixed[:, (3 * head + j) * head_dim : (3 * head + j + 1) * head_dim] for j in range(3)
        )
        query = head_norm(query, gain_ref[0:1, :]).astype(jnp.bfloat16)
        key = by_patch(head_norm(key, gain_ref[1:2, :]))
        value = by_patch(value)
        fresh.append((key, value))
        keys, values = (
            [new, old_table_ref[j, :, :, at].reshape(groups * rows, head_dim)]
            + [ref[j, :, at] for ref in stale_refs]
            for j, new in enumerate((key, value))
        )
        total = 0.0
        summed = 0.0
        for mask, key_rows, value_rows in zip(masks, keys, values):
            scores = lax.dot_general(
                query, key_rows, (((1,), (1,)), ((), ())), preferred_element_type=jnp.float32
            )
            weights = jnp.where(mask, jnp.exp(scores / math.sqrt(head_dim)), 0.0)
            total = total + jnp.sum(weights, axis=-1, keepdims=True)
            summed = summed + jnp.dot(
                weights.astype(jnp.bfloat16), value_rows, preferred_element_type=jnp.float32
            )
        attended.append((summed / total).astype(jnp.bfloat16))
    attended = jnp.concatenate(attended, axis=1)

    projected = jnp.dot(attended, out_ref[...], preferred_element_type=jnp.float32)
    projected = (mod_ref[2] * projected).astype(jnp.bfloat16)
    for q in range(blocks):
        partial_ref[q] = projected[:, q * block_cols : (q + 1) * block_cols].reshape(
            slices, block_rows, block_cols
        )

    for at in range(groups):

        @pl.when(group == at)
        def _():
            for j in range(2):
                table_ref[j, at] = jnp.concatenate([pair[j] for pair in fresh], axis=1)

        @pl.when(group != at)
        def _():
            for j in range(2):
                table_ref[j, at] = old_table_ref[j, at]


def start_kernel(where_ref, latent_ref, *refs):
    loads = (len(refs) - 4) // 2
    from_refs, to_refs = refs[:loads], refs[loads : 2 * loads]
    sources_to, streams_to, spread_to, sems = refs[2 * loads :]
    copies = [
        pltpu.make_async_copy(from_ref, to_ref, sems.at[at])
        for at, (from_ref, to_ref) in enumerate(zip(from_refs, to_refs))
    ]
    for copy in copies[1:]:
        copy.start()
    piece_rows = from_refs[0].shape[0] // PIECES

    @pl.when(where_ref[2] == 0)
    def _():
        copies[0].start()
        copies[0].wait()

    @pl.when(where_ref[2] == 1)
    def _():
        @pl.loop(0, PIECES)
        def _(step):
            at = pl.ds(step * piece_rows, piece_rows)
            piece = pltpu.make_async_copy(from_refs[0].at[at], to_refs[0].at[at], sems.at[0])
            piece.start()
            piece.wait()

    sections, slices, _, block_cols = spread_to.shape
    for q in range(sections):

        @pl.when(where_ref[0] == q)
        def _():
            sources_to[...] = latent_ref[:, :, q * block_cols : (q + 1) * block_cols]

    first = sources_to[0]
    for section in range(sections):
        held = first if section == 0 else jnp.zeros_like(first)
        streams_to[section] = held
        for piece in range(slices):
            spread_to[section, piece] = held
    for copy in copies[1:]:
        copy.wait()


def added(parts_ref, streams_ref, section):
    total = streams_ref[section].astype(jnp.float32)
    for piece in range(parts_ref.shape[1]):
        total = total + parts_ref[section, piece].astype(jnp.float32)
    return total.astype(jnp.bfloat16)


def settle_kernel(entering, parts_ref, streams_ref, sources_ref, streams_to, spread_to, last_to):
    count, slices = parts_ref.shape[:2]
    for section in range(count):
        if section == 0:
            held = sources_ref[entering]
        else:
            held = added(parts_ref, streams_ref, section - 1)
        streams_to[section] = held
        for piece in range(slices):
            spread_to[section, piece] = held
    last_to[...] = added(parts_ref, streams_ref, count - 1)


def close_kernel(parts_ref, streams_ref, *refs):
    *last_refs, finals_to = refs
    lasts = [ref[...] for ref in last_refs]
    lasts.append(added(parts_ref, streams_ref, parts_ref.shape[0] - 1))
    finals = jnp.concatenate(lasts).reshape(finals_to.shape[1:])
    for branch in range(finals_to.shape[0]):
        finals_to[branch] = finals


def local(latent, modulation, qkv_weight, out_weight, norm_gain, stale_kv):
    seq_count = lax.axis_size("seq")
    seq_rank = lax.axis_index("seq")
    section_count = lax.axis_size("pipe")
    section_rank = lax.axis_index("pipe")
    branch_rank = lax.axis_index("cfg")
    patches, tok_dev, model_width = latent.shape
    head_dim = norm_gain.shape[2]
    slice_count = min(seq_count, 8)
    member_count = seq_count // slice_count
    member_bits = member_count.bit_length() - 1
    own_member = seq_rank % member_count
    local_width = stale_kv.shape[7]
    group_rows = slice_count * tok_dev
    own_cache = stale_kv[0, 0].reshape(2, patches, group_rows, local_width)
    group_cache = own_cache[None]
    qkv_slice = qkv_weight[0]
    out_slice = out_weight[0]
    for level_index in range(member_bits):
        got_qkv, got_out, got_cache = (
            swapped(qkv_slice, "seq", level_index),
            swapped(out_slice, "seq", level_index),
            swapped(group_cache, "seq", level_index),
        )
        is_upper = own_member >> level_index & 1 == 1
        qkv_slice = join_pair(is_upper, qkv_slice, got_qkv, 1)
        out_slice = join_pair(is_upper, out_slice, got_out, 0)
        group_cache = join_pair(is_upper, group_cache, got_cache, 0)
    homes = section_count * slice_count
    in_group = patches // GROUPS
    block_rows = in_group * tok_dev
    block_cols = model_width // section_count
    rows = slice_count * block_rows
    peers = None
    if member_count > 1:
        peers = [
            [
                q * seq_count + a + member_count * b
                for q in range(section_count)
                for b in range(slice_count)
            ]
            for a in range(member_count)
        ]

    def exchange(value):
        value = value.reshape(homes, block_rows, block_cols)
        value = lax.all_to_all(value, ("pipe", "seq"), 0, 0, axis_index_groups=peers)
        return value.reshape(section_count, slice_count, block_rows, block_cols)

    vmem = pl.BlockSpec(memory_space=pltpu.VMEM)
    smem = pl.BlockSpec(memory_space=pltpu.SMEM)
    in_hbm = functools.partial(pltpu.with_memory_space_constraint, memory_space=pltpu.HBM)
    in_vmem = functools.partial(pltpu.with_memory_space_constraint, memory_space=pltpu.VMEM)
    where = jnp.stack((section_rank, own_member, branch_rank)).astype(jnp.int32)
    sources = latent.reshape(GROUPS, block_rows, model_width)
    stream_shape = (section_count, block_rows, block_cols)
    spread_shape = (section_count, slice_count, block_rows, block_cols)
    loads = (
        qkv_slice,
        out_slice,
        modulation.reshape(3, 1, model_width),
        norm_gain[0],
        own_cache.reshape(2, GROUPS, rows, local_width),
    )
    qkv_slice, out_slice, modulation, norm_gain, table, sources, streams, spread = pl.pallas_call(
        start_kernel,
        out_shape=tuple(pltpu.VMEM(value.shape, value.dtype) for value in loads)
        + (
            pltpu.VMEM((GROUPS, block_rows, block_cols), jnp.bfloat16),
            jax.ShapeDtypeStruct(stream_shape, jnp.bfloat16),
            jax.ShapeDtypeStruct(spread_shape, jnp.bfloat16),
        ),
        in_specs=[smem, vmem] + [pl.BlockSpec(memory_space=pltpu.HBM)] * len(loads),
        out_specs=(vmem,) * (len(loads) + 3),
        scratch_shapes=[pltpu.SemaphoreType.DMA((len(loads),))],
        compiler_params=pltpu.CompilerParams(vmem_limit_bytes=4 * 1024 * 1024),
    )(where, sources, *map(in_hbm, loads))
    stale_rows = []
    if member_count > 1:
        stale_rows = [group_cache.swapaxes(0, 1).reshape(2, -1, local_width)]

    def attend(tick, features, table):
        operands = (
            where,
            features,
            in_vmem(modulation),
            in_vmem(qkv_slice),
            in_vmem(out_slice),
            in_vmem(norm_gain),
            *stale_rows,
            table,
        )
        return pl.pallas_call(
            functools.partial(section_kernel, tick, (tok_dev, head_dim)),
            out_shape=(
                jax.ShapeDtypeStruct(features.shape, jnp.bfloat16),
                jax.ShapeDtypeStruct(table.shape, jnp.bfloat16),
            ),
            in_specs=[smem] + [vmem] * (len(operands) - 1),
            out_specs=(vmem, vmem),
            input_output_aliases={len(operands) - 1: 1},
            compiler_params=pltpu.CompilerParams(vmem_limit_bytes=24 * 1024 * 1024),
        )(*operands)

    def settle(entering, parts, streams):
        return pl.pallas_call(
            functools.partial(settle_kernel, entering),
            out_shape=tuple(
                jax.ShapeDtypeStruct(shape, jnp.bfloat16)
                for shape in (stream_shape, spread_shape, stream_shape[1:])
            ),
            in_specs=[vmem] * 3,
            out_specs=(vmem,) * 3,
            compiler_params=pltpu.CompilerParams(vmem_limit_bytes=8 * 1024 * 1024),
        )(parts, streams, in_vmem(sources))

    lasts = []
    ticks = GROUPS + section_count - 1
    for tick in range(ticks):
        partial_out, table = attend(tick, exchange(spread), table)
        parts = exchange(partial_out)
        if tick < ticks - 1:
            streams, spread, last = settle(min(tick + 1, GROUPS - 1), parts, streams)
            lasts.append(last)

    next_cache = table.reshape(stale_kv.shape)
    per_home = patches // section_count
    finals = pl.pallas_call(
        close_kernel,
        out_shape=jax.ShapeDtypeStruct((2, patches, tok_dev, block_cols), jnp.bfloat16),
        in_specs=[vmem] * (GROUPS + 1),
        out_specs=vmem,
        compiler_params=pltpu.CompilerParams(vmem_limit_bytes=8 * 1024 * 1024),
    )(parts, streams, *lasts[section_count - 1 :])
    finals = finals.reshape(2, section_count, per_home, tok_dev, block_cols)
    got = lax.all_to_all(
        finals.reshape((-1,) + finals.shape[2:]), ("cfg", "pipe"), 0, 0
    ).reshape(finals.shape)
    half = section_count // 2
    got = lax.dynamic_slice_in_dim(got, branch_rank * half, half, 1).astype(jnp.float32)
    guided = (got[1] + GUIDANCE_SCALE * (got[0] - got[1])).astype(jnp.bfloat16)
    guided = guided.transpose(1, 2, 0, 3).reshape(per_home, tok_dev, half * block_cols)
    return (guided, next_cache)


def solution(mesh):
    placed = (
        P(None, "seq", None),
        P("pipe", "cfg", None, None),
        P("pipe", None, "seq"),
        P("pipe", "seq", None),
        P("pipe", None, None),
        P("pipe", "cfg", None, None, "seq", None, None, None),
    )
    return jax.shard_map(
        local,
        mesh=mesh,
        in_specs=placed,
        out_specs=(P("pipe", "seq", "cfg"), P("pipe", "cfg", None, None, "seq", None, None, None)),
        check_vma=False,
    )
```

```python
import functools
import math

import jax
import jax.numpy as jnp
from jax import lax
from jax.experimental import pallas as pl
from jax.experimental.pallas import tpu as pltpu
from jax.sharding import PartitionSpec as P

GUIDANCE_SCALE = 6.0
EPSILON = 1e-06
GROUPS = 2


def swapped(value, axis, bit):
    return lax.ppermute(value, axis, [(i, i ^ 1 << bit) for i in range(lax.axis_size(axis))])


def head_norm(values, gain_row):
    return (
        values * lax.rsqrt(jnp.mean(values * values, axis=-1, keepdims=True) + EPSILON) * gain_row
    )


def join_pair(is_upper, mine, theirs, axis_dim):
    return jnp.where(
        is_upper,
        jnp.concatenate((theirs, mine), axis_dim),
        jnp.concatenate((mine, theirs), axis_dim),
    )


def section_kernel(tick, sizes, where_ref, rows_ref, mod_ref, qkv_ref, out_ref, gain_ref, *refs):
    *stale_refs, old_table_ref, partial_ref, table_ref = refs
    closing = len(partial_ref.shape) == 5
    tok_dev, head_dim = sizes
    blocks, slices, block_rows, block_cols = rows_ref.shape
    rows = slices * block_rows
    width = blocks * block_cols
    in_group = block_rows // tok_dev
    group_rows = slices * tok_dev
    groups, local_width = table_ref.shape[1], table_ref.shape[3]
    heads = local_width // head_dim
    section, own_member, own_slice = where_ref[0], where_ref[1], where_ref[2]
    group = tick - section
    parts = [rows_ref[q].reshape(rows, block_cols).astype(jnp.float32) for q in range(blocks)]
    mean = sum(jnp.sum(x, axis=-1, keepdims=True) for x in parts) / width
    parts = [x - mean for x in parts]
    spread = sum(jnp.sum(x * x, axis=-1, keepdims=True) for x in parts) / width
    inverse = lax.rsqrt(spread + EPSILON)
    modulated = []
    for q, x in enumerate(parts):
        at = slice(q * block_cols, (q + 1) * block_cols)
        modulated.append(
            (x * inverse * (1.0 + mod_ref[1, :, at]) + mod_ref[0, :, at]).astype(jnp.bfloat16)
        )
    modulated = jnp.concatenate(modulated, axis=1)
    mixed = jnp.dot(modulated, qkv_ref[...], preferred_element_type=jnp.float32)

    def by_patch(values):
        values = values.reshape(slices, in_group, tok_dev, head_dim).swapaxes(0, 1)
        return values.reshape(rows, head_dim).astype(jnp.bfloat16)

    def query_patch(shape):
        return lax.broadcasted_iota(jnp.int32, shape, 0) // tok_dev % in_group

    square, wide = (rows, rows), (rows, groups * rows)
    fresh_patch = lax.broadcasted_iota(jnp.int32, square, 1) // group_rows
    old_patch = lax.broadcasted_iota(jnp.int32, wide, 1) // group_rows - group * in_group
    masks = [
        fresh_patch <= query_patch(square),
        jnp.logical_or(old_patch < 0, old_patch > query_patch(wide)),
    ]
    for ref in stale_refs:
        at = lax.broadcasted_iota(jnp.int32, (rows, ref.shape[1]), 1)
        masks.append(at // (groups * rows) != own_member)
    attended = []
    fresh = []
    for head in range(heads):
        at = slice(head * head_dim, (head + 1) * head_dim)
        query, key, value = (
            mixed[:, (3 * head + j) * head_dim : (3 * head + j + 1) * head_dim] for j in range(3)
        )
        query = head_norm(query, gain_ref[0:1, :]).astype(jnp.bfloat16)
        key = by_patch(head_norm(key, gain_ref[1:2, :]))
        value = by_patch(value)
        fresh.append((key, value))
        keys, values = (
            [new, old_table_ref[j, :, :, at].reshape(groups * rows, head_dim)]
            + [ref[j, :, at] for ref in stale_refs]
            for j, new in enumerate((key, value))
        )
        total = 0.0
        summed = 0.0
        for mask, key_rows, value_rows in zip(masks, keys, values):
            scores = lax.dot_general(
                query, key_rows, (((1,), (1,)), ((), ())), preferred_element_type=jnp.float32
            )
            weights = jnp.where(mask, jnp.exp(scores / math.sqrt(head_dim)), 0.0)
            total = total + jnp.sum(weights, axis=-1, keepdims=True)
            summed = summed + jnp.dot(
                weights.astype(jnp.bfloat16), value_rows, preferred_element_type=jnp.float32
            )
        attended.append((summed / total).astype(jnp.bfloat16))
    attended = jnp.concatenate(attended, axis=1)

    projected = jnp.dot(attended, out_ref[...], preferred_element_type=jnp.float32)
    projected = mod_ref[2] * projected
    if closing:
        close_into(partial_ref, projected, rows_ref, section, own_slice, in_group)
    else:
        out_cols = partial_ref.shape[3]
        for q in range(partial_ref.shape[0]):
            piece = projected[:, q * out_cols : (q + 1) * out_cols].astype(jnp.bfloat16)
            partial_ref[q] = piece.reshape(slices, block_rows, out_cols)

    for at in range(groups):

        @pl.when(group == at)
        def _():
            for j in range(2):
                table_ref[j, at] = jnp.concatenate([pair[j] for pair in fresh], axis=1)

        @pl.when(group != at)
        def _():
            for j in range(2):
                table_ref[j, at] = old_table_ref[j, at]


def close_into(closing_ref, projected, rows_ref, section, own_slice, in_group):
    branches, patches, slices = closing_ref.shape[:3]
    blocks, _, block_rows, block_cols = rows_ref.shape
    tok_dev = block_rows // in_group
    per_branch = blocks // branches

    @pl.when(section >= patches)
    def _():
        for piece in range(slices):
            own = (own_slice == piece).astype(jnp.float32)
            by_block = []
            for q in range(blocks):
                rows = projected[
                    piece * block_rows : (piece + 1) * block_rows,
                    q * block_cols : (q + 1) * block_cols,
                ]
                rows = rows + own * rows_ref[q, piece].astype(jnp.float32)
                by_block.append(rows.reshape(in_group, tok_dev, block_cols))
            for branch in range(branches):
                for patch in range(patches):
                    held = [by_block[branch * per_branch + k][patch] for k in range(per_branch)]
                    closing_ref[branch, patch, piece] = jnp.concatenate(held).astype(jnp.bfloat16)

    @pl.when(section < patches)
    def _():
        finished = [rows_ref[q, own_slice].astype(jnp.float32)[:tok_dev] for q in range(blocks)]
        for branch in range(branches):
            held = jnp.concatenate(finished[branch * per_branch : (branch + 1) * per_branch])
            held = held.astype(jnp.bfloat16)
            for patch in range(patches):
                for piece in range(slices):
                    closing_ref[branch, patch, piece] = held


def start_kernel(where_ref, latent_ref, *refs):
    loads = (len(refs) - 4) // 2
    from_refs, to_refs = refs[:loads], refs[loads : 2 * loads]
    sources_to, streams_to, spread_to, sems = refs[2 * loads :]
    copies = [
        pltpu.make_async_copy(from_ref, to_ref, sems.at[at])
        for at, (from_ref, to_ref) in enumerate(zip(from_refs, to_refs))
    ]
    for copy in copies:
        copy.start()
    sections, _, block_cols = streams_to.shape
    for piece in range(spread_to.shape[0]):
        spread_to[piece] = latent_ref[0]
    for q in range(sections):

        @pl.when(where_ref[0] == q)
        def _():
            sources_to[...] = latent_ref[:, :, q * block_cols : (q + 1) * block_cols]

    streams_to[0] = sources_to[0]
    for section in range(1, sections):
        streams_to[section] = jnp.zeros(streams_to.shape[1:], streams_to.dtype)
    for copy in copies:
        copy.wait()


def added(parts_ref, streams_ref, section):
    total = streams_ref[section].astype(jnp.float32)
    for piece in range(parts_ref.shape[1]):
        total = total + parts_ref[section, piece].astype(jnp.float32)
    return total


def settle_kernel(entering, parts_ref, streams_ref, sources_ref, streams_to, spread_to):
    count, slices = parts_ref.shape[:2]
    for section in range(count):
        if section == 0:
            held = sources_ref[entering]
        else:
            held = added(parts_ref, streams_ref, section - 1).astype(jnp.bfloat16)
        streams_to[section] = held
        for piece in range(slices):
            spread_to[section, piece] = held


def settle_last_kernel(in_group, parts_ref, streams_ref, spread_to):
    count, slices = parts_ref.shape[:2]
    finished = added(parts_ref, streams_ref, count - 1)
    tok_dev = finished.shape[0] // in_group
    last = added(parts_ref, streams_ref, count - 2).astype(jnp.bfloat16)
    for section in range(count):
        held = last
        if section < in_group:
            held = finished[section * tok_dev : (section + 1) * tok_dev]
            held = jnp.concatenate([held] * in_group).astype(jnp.bfloat16)
        for piece in range(slices):
            spread_to[section, piece] = held


def guide_kernel(where_ref, closing_ref, guided_ref):
    branches, patches, slices, block_rows, block_cols = closing_ref.shape
    tok_dev = guided_ref.shape[0]
    section, own_slice = where_ref[0], where_ref[2]

    def combine(pair):
        conditional, unconditional = pair
        rows = unconditional + GUIDANCE_SCALE * (conditional - unconditional)
        for at in range(block_rows // tok_dev):
            guided_ref[:, at * block_cols : (at + 1) * block_cols] = rows[
                at * tok_dev : (at + 1) * tok_dev
            ].astype(jnp.bfloat16)

    @pl.when(section >= patches)
    def _():
        pair = []
        for branch in range(branches):
            total = 0.0
            for piece in range(slices):
                total = total + closing_ref[branch, patches - 1, piece].astype(jnp.float32)
            pair.append(total.astype(jnp.bfloat16).astype(jnp.float32))
        combine(pair)

    @pl.when(section < patches)
    def _():
        combine(
            [closing_ref[branch, section, own_slice].astype(jnp.float32) for branch in range(branches)]
        )


def local(latent, modulation, qkv_weight, out_weight, norm_gain, stale_kv):
    seq_count = lax.axis_size("seq")
    seq_rank = lax.axis_index("seq")
    section_count = lax.axis_size("pipe")
    section_rank = lax.axis_index("pipe")
    patches, tok_dev, model_width = latent.shape
    head_dim = norm_gain.shape[2]
    slice_count = min(seq_count, 8)
    member_count = seq_count // slice_count
    member_bits = member_count.bit_length() - 1
    own_member = seq_rank % member_count
    local_width = stale_kv.shape[7]
    group_rows = slice_count * tok_dev
    own_cache = stale_kv[0, 0].reshape(2, patches, group_rows, local_width)
    group_cache = own_cache[None]
    qkv_slice = qkv_weight[0]
    out_slice = out_weight[0]
    for level_index in range(member_bits):
        got_qkv, got_out, got_cache = (
            swapped(qkv_slice, "seq", level_index),
            swapped(out_slice, "seq", level_index),
            swapped(group_cache, "seq", level_index),
        )
        is_upper = own_member >> level_index & 1 == 1
        qkv_slice = join_pair(is_upper, qkv_slice, got_qkv, 1)
        out_slice = join_pair(is_upper, out_slice, got_out, 0)
        group_cache = join_pair(is_upper, group_cache, got_cache, 0)
    homes = section_count * slice_count
    in_group = patches // GROUPS
    block_rows = in_group * tok_dev
    block_cols = model_width // section_count
    rows = slice_count * block_rows
    half = section_count // 2
    groups_of = range(member_count)
    in_slices = [[a + member_count * b for b in range(slice_count)] for a in groups_of]
    peers = [[q * seq_count + at for q in range(section_count) for at in g] for g in in_slices]
    closing_peers = [
        [
            (c * section_count + q) * seq_count + at
            for c in range(2)
            for q in range(h * half, (h + 1) * half)
            for at in g
        ]
        for h in range(2)
        for g in in_slices
    ]

    def exchange(value):
        value = value.reshape(homes, block_rows, block_cols)
        value = lax.all_to_all(value, ("pipe", "seq"), 0, 0, axis_index_groups=peers)
        return value.reshape(section_count, slice_count, block_rows, block_cols)

    vmem = pl.BlockSpec(memory_space=pltpu.VMEM)
    smem = pl.BlockSpec(memory_space=pltpu.SMEM)
    in_hbm = functools.partial(pltpu.with_memory_space_constraint, memory_space=pltpu.HBM)
    in_vmem = functools.partial(pltpu.with_memory_space_constraint, memory_space=pltpu.VMEM)
    where = jnp.stack((section_rank, own_member, seq_rank // member_count)).astype(jnp.int32)
    sources = latent.reshape(GROUPS, block_rows, model_width)
    stream_shape = (section_count, block_rows, block_cols)
    spread_shape = (section_count, slice_count, block_rows, block_cols)
    loads = (
        qkv_slice,
        out_slice,
        modulation.reshape(3, 1, model_width),
        norm_gain[0],
        own_cache.reshape(2, GROUPS, rows, local_width),
    )
    qkv_slice, out_slice, modulation, norm_gain, table, sources, streams, spread = pl.pallas_call(
        start_kernel,
        out_shape=tuple(pltpu.VMEM(value.shape, value.dtype) for value in loads)
        + (
            pltpu.VMEM((GROUPS, block_rows, block_cols), jnp.bfloat16),
            jax.ShapeDtypeStruct(stream_shape, jnp.bfloat16),
            jax.ShapeDtypeStruct((slice_count, block_rows, model_width), jnp.bfloat16),
        ),
        in_specs=[smem, vmem] + [pl.BlockSpec(memory_space=pltpu.HBM)] * len(loads),
        out_specs=(vmem,) * (len(loads) + 3),
        scratch_shapes=[pltpu.SemaphoreType.DMA((len(loads),))],
        compiler_params=pltpu.CompilerParams(vmem_limit_bytes=4 * 1024 * 1024),
    )(where, sources, *map(in_hbm, loads))
    stale_rows = []
    if member_count > 1:
        stale_rows = [group_cache.swapaxes(0, 1).reshape(2, -1, local_width)]

    def attend(tick, features, table, partial_shape):
        operands = (
            where,
            features,
            in_vmem(modulation),
            in_vmem(qkv_slice),
            in_vmem(out_slice),
            in_vmem(norm_gain),
            *stale_rows,
            table,
        )
        return pl.pallas_call(
            functools.partial(section_kernel, tick, (tok_dev, head_dim)),
            out_shape=(
                jax.ShapeDtypeStruct(partial_shape, jnp.bfloat16),
                jax.ShapeDtypeStruct(table.shape, jnp.bfloat16),
            ),
            in_specs=[smem] + [vmem] * (len(operands) - 1),
            out_specs=(vmem, vmem),
            input_output_aliases={len(operands) - 1: 1},
            compiler_params=pltpu.CompilerParams(vmem_limit_bytes=24 * 1024 * 1024),
        )(*operands)

    def small(kernel, in_specs, *out_shapes):
        return pl.pallas_call(
            kernel,
            out_shape=tuple(jax.ShapeDtypeStruct(shape, jnp.bfloat16) for shape in out_shapes),
            in_specs=in_specs,
            out_specs=(vmem,) * len(out_shapes),
            compiler_params=pltpu.CompilerParams(vmem_limit_bytes=8 * 1024 * 1024),
        )

    ticks = GROUPS + section_count - 1
    closing_shape = (2, half, slice_count, block_rows, block_cols)
    features = lax.all_to_all(spread, "seq", 0, 0, axis_index_groups=in_slices)[None]
    for tick in range(ticks - 1):
        partial_out, table = attend(tick, features, table, spread_shape)
        parts = exchange(partial_out)
        if tick < ticks - 2:
            streams, spread = small(
                functools.partial(settle_kernel, min(tick + 1, GROUPS - 1)),
                [vmem] * 3,
                stream_shape,
                spread_shape,
            )(parts, streams, in_vmem(sources))
        else:
            (spread,) = small(
                functools.partial(settle_last_kernel, in_group), [vmem] * 2, spread_shape
            )(parts, streams)
        features = exchange(spread)
    closing, table = attend(ticks - 1, features, table, closing_shape)
    closing = lax.all_to_all(
        closing.reshape((-1,) + closing_shape[3:]),
        ("cfg", "pipe", "seq"),
        0,
        0,
        axis_index_groups=closing_peers,
    ).reshape(closing_shape)
    (guided,) = small(guide_kernel, [smem, vmem], (tok_dev, model_width // 2))(where, closing)
    return (guided[None], table.reshape(stale_kv.shape))


def solution(mesh):
    placed = (
        P(None, "seq", None),
        P("pipe", "cfg", None, None),
        P("pipe", None, "seq"),
        P("pipe", "seq", None),
        P("pipe", None, None),
        P("pipe", "cfg", None, None, "seq", None, None, None),
    )
    return jax.shard_map(
        local,
        mesh=mesh,
        in_specs=placed,
        out_specs=(P("pipe", "seq", "cfg"), P("pipe", "cfg", None, None, "seq", None, None, None)),
        check_vma=False,
    )
```

```python
import functools
import math

import jax
import jax.numpy as jnp
from jax import lax
from jax.experimental import pallas as pl
from jax.experimental.pallas import tpu as pltpu
from jax.sharding import PartitionSpec as P

GUIDANCE_SCALE = 6.0
EPSILON = 1e-06
GROUPS = 2
PIECES = 4


def swapped(value, axis, bit):
    return lax.ppermute(value, axis, [(i, i ^ 1 << bit) for i in range(lax.axis_size(axis))])


def head_norm(values, gain_row):
    return (
        values * lax.rsqrt(jnp.mean(values * values, axis=-1, keepdims=True) + EPSILON) * gain_row
    )


def join_pair(is_upper, mine, theirs, axis_dim):
    return jnp.where(
        is_upper,
        jnp.concatenate((theirs, mine), axis_dim),
        jnp.concatenate((mine, theirs), axis_dim),
    )


def section_kernel(tick, sizes, where_ref, rows_ref, mod_ref, qkv_ref, out_ref, gain_ref, *refs):
    loading = tick == 0
    weights_from = (qkv_ref, out_ref)
    if loading:
        *refs, qkv_ref, out_ref, sems = refs
    *stale_refs, old_table_ref, partial_ref, table_ref = refs
    closing = len(partial_ref.shape) == 5
    tok_dev, head_dim = sizes
    blocks, slices, block_rows, block_cols = rows_ref.shape
    rows = slices * block_rows
    width = blocks * block_cols
    in_group = block_rows // tok_dev
    group_rows = slices * tok_dev
    groups, local_width = table_ref.shape[1], table_ref.shape[3]
    heads = local_width // head_dim
    section, own_member, own_slice = where_ref[0], where_ref[1], where_ref[2]
    group = tick - section
    copies = []
    if loading:
        piece_rows = qkv_ref.shape[0] // PIECES
        for at in range(PIECES):
            piece = pl.ds(at * piece_rows, piece_rows)
            copies.append(
                pltpu.make_async_copy(
                    weights_from[0].at[piece], qkv_ref.at[piece], sems.at[at]
                )
            )
        copies.append(pltpu.make_async_copy(weights_from[1], out_ref, sems.at[PIECES]))
        for copy in copies:
            copy.start()
    parts = [rows_ref[q].reshape(rows, block_cols).astype(jnp.float32) for q in range(blocks)]
    mean = sum(jnp.sum(x, axis=-1, keepdims=True) for x in parts) / width
    parts = [x - mean for x in parts]
    spread = sum(jnp.sum(x * x, axis=-1, keepdims=True) for x in parts) / width
    inverse = lax.rsqrt(spread + EPSILON)
    modulated = []
    for q, x in enumerate(parts):
        at = slice(q * block_cols, (q + 1) * block_cols)
        modulated.append(
            (x * inverse * (1.0 + mod_ref[1, :, at]) + mod_ref[0, :, at]).astype(jnp.bfloat16)
        )
    modulated = jnp.concatenate(modulated, axis=1)
    if loading:
        mixed = 0.0
        for at in range(PIECES):
            copies[at].wait()
            piece = slice(at * piece_rows, (at + 1) * piece_rows)
            mixed = mixed + jnp.dot(
                modulated[:, piece], qkv_ref[piece, :], preferred_element_type=jnp.float32
            )
    else:
        mixed = jnp.dot(modulated, qkv_ref[...], preferred_element_type=jnp.float32)

    def by_patch(values):
        values = values.reshape(slices, in_group, tok_dev, head_dim).swapaxes(0, 1)
        return values.reshape(rows, head_dim).astype(jnp.bfloat16)

    def query_patch(shape):
        return lax.broadcasted_iota(jnp.int32, shape, 0) // tok_dev % in_group

    square, wide = (rows, rows), (rows, groups * rows)
    fresh_patch = lax.broadcasted_iota(jnp.int32, square, 1) // group_rows
    old_patch = lax.broadcasted_iota(jnp.int32, wide, 1) // group_rows - group * in_group
    masks = [
        fresh_patch <= query_patch(square),
        jnp.logical_or(old_patch < 0, old_patch > query_patch(wide)),
    ]
    for ref in stale_refs:
        at = lax.broadcasted_iota(jnp.int32, (rows, ref.shape[1]), 1)
        masks.append(at // (groups * rows) != own_member)
    attended = []
    fresh = []
    for head in range(heads):
        at = slice(head * head_dim, (head + 1) * head_dim)
        query, key, value = (
            mixed[:, (3 * head + j) * head_dim : (3 * head + j + 1) * head_dim] for j in range(3)
        )
        query = head_norm(query, gain_ref[0:1, :]).astype(jnp.bfloat16)
        key = by_patch(head_norm(key, gain_ref[1:2, :]))
        value = by_patch(value)
        fresh.append((key, value))
        keys, values = (
            [new, old_table_ref[j, :, :, at].reshape(groups * rows, head_dim)]
            + [ref[j, :, at] for ref in stale_refs]
            for j, new in enumerate((key, value))
        )
        total = 0.0
        summed = 0.0
        for mask, key_rows, value_rows in zip(masks, keys, values):
            scores = lax.dot_general(
                query, key_rows, (((1,), (1,)), ((), ())), preferred_element_type=jnp.float32
            )
            weights = jnp.where(mask, jnp.exp(scores / math.sqrt(head_dim)), 0.0)
            total = total + jnp.sum(weights, axis=-1, keepdims=True)
            summed = summed + jnp.dot(
                weights.astype(jnp.bfloat16), value_rows, preferred_element_type=jnp.float32
            )
        attended.append((summed / total).astype(jnp.bfloat16))
    attended = jnp.concatenate(attended, axis=1)

    if loading:
        copies[PIECES].wait()
    projected = jnp.dot(attended, out_ref[...], preferred_element_type=jnp.float32)
    projected = mod_ref[2] * projected
    if closing:
        close_into(partial_ref, projected, rows_ref, section, own_slice, in_group)
    else:
        out_cols = partial_ref.shape[3]
        for q in range(partial_ref.shape[0]):
            piece = projected[:, q * out_cols : (q + 1) * out_cols].astype(jnp.bfloat16)
            partial_ref[q] = piece.reshape(slices, block_rows, out_cols)

    for at in range(groups):

        @pl.when(group == at)
        def _():
            for j in range(2):
                table_ref[j, at] = jnp.concatenate([pair[j] for pair in fresh], axis=1)

        @pl.when(group != at)
        def _():
            for j in range(2):
                table_ref[j, at] = old_table_ref[j, at]


def close_into(closing_ref, projected, rows_ref, section, own_slice, in_group):
    branches, patches, slices = closing_ref.shape[:3]
    blocks, _, block_rows, block_cols = rows_ref.shape
    tok_dev = block_rows // in_group
    per_branch = blocks // branches

    @pl.when(section >= patches)
    def _():
        for piece in range(slices):
            own = (own_slice == piece).astype(jnp.float32)
            by_block = []
            for q in range(blocks):
                rows = projected[
                    piece * block_rows : (piece + 1) * block_rows,
                    q * block_cols : (q + 1) * block_cols,
                ]
                rows = rows + own * rows_ref[q, piece].astype(jnp.float32)
                by_block.append(rows.reshape(in_group, tok_dev, block_cols))
            for branch in range(branches):
                for patch in range(patches):
                    held = [by_block[branch * per_branch + k][patch] for k in range(per_branch)]
                    closing_ref[branch, patch, piece] = jnp.concatenate(held).astype(jnp.bfloat16)

    @pl.when(section < patches)
    def _():
        finished = [rows_ref[q, own_slice].astype(jnp.float32)[:tok_dev] for q in range(blocks)]
        for branch in range(branches):
            held = jnp.concatenate(finished[branch * per_branch : (branch + 1) * per_branch])
            held = held.astype(jnp.bfloat16)
            for patch in range(patches):
                for piece in range(slices):
                    closing_ref[branch, patch, piece] = held


def start_kernel(where_ref, latent_ref, *refs):
    loads = (len(refs) - 4) // 2
    from_refs, to_refs = refs[:loads], refs[loads : 2 * loads]
    sources_to, streams_to, spread_to, sems = refs[2 * loads :]
    sections, _, block_cols = streams_to.shape
    own_cols = pl.ds(pl.multiple_of(where_ref[0] * block_cols, block_cols), block_cols)
    pairs = [(latent_ref.at[0], spread_to.at[piece]) for piece in range(spread_to.shape[0])]
    pairs.append((latent_ref.at[:, :, own_cols], sources_to))
    pairs.extend(zip(from_refs, to_refs))
    copies = [
        pltpu.make_async_copy(from_ref, to_ref, sems.at[at])
        for at, (from_ref, to_ref) in enumerate(pairs)
    ]
    for copy in copies:
        copy.start()
    for section in range(1, sections):
        streams_to[section] = jnp.zeros(streams_to.shape[1:], streams_to.dtype)
    for copy in copies:
        copy.wait()
    streams_to[0] = sources_to[0]


def added(parts_ref, streams_ref, section):
    total = streams_ref[section].astype(jnp.float32)
    for piece in range(parts_ref.shape[1]):
        total = total + parts_ref[section, piece].astype(jnp.float32)
    return total


def settle_kernel(entering, parts_ref, streams_ref, sources_ref, streams_to, spread_to):
    count, slices = parts_ref.shape[:2]
    for section in range(count):
        if section == 0:
            held = sources_ref[entering]
        else:
            held = added(parts_ref, streams_ref, section - 1).astype(jnp.bfloat16)
        streams_to[section] = held
        for piece in range(slices):
            spread_to[section, piece] = held


def settle_last_kernel(in_group, parts_ref, streams_ref, spread_to):
    count, slices = parts_ref.shape[:2]
    finished = added(parts_ref, streams_ref, count - 1)
    tok_dev = finished.shape[0] // in_group
    last = added(parts_ref, streams_ref, count - 2).astype(jnp.bfloat16)
    for section in range(count):
        held = last
        if section < in_group:
            held = finished[section * tok_dev : (section + 1) * tok_dev]
            held = jnp.concatenate([held] * in_group).astype(jnp.bfloat16)
        for piece in range(slices):
            spread_to[section, piece] = held


def guide_kernel(where_ref, closing_ref, guided_ref):
    branches, patches, slices, block_rows, block_cols = closing_ref.shape
    tok_dev = guided_ref.shape[0]
    section, own_slice = where_ref[0], where_ref[2]

    def combine(pair):
        conditional, unconditional = pair
        rows = unconditional + GUIDANCE_SCALE * (conditional - unconditional)
        for at in range(block_rows // tok_dev):
            guided_ref[:, at * block_cols : (at + 1) * block_cols] = rows[
                at * tok_dev : (at + 1) * tok_dev
            ].astype(jnp.bfloat16)

    @pl.when(section >= patches)
    def _():
        pair = []
        for branch in range(branches):
            total = 0.0
            for piece in range(slices):
                total = total + closing_ref[branch, patches - 1, piece].astype(jnp.float32)
            pair.append(total.astype(jnp.bfloat16).astype(jnp.float32))
        combine(pair)

    @pl.when(section < patches)
    def _():
        combine(
            [closing_ref[branch, section, own_slice].astype(jnp.float32) for branch in range(branches)]
        )


def local(latent, modulation, qkv_weight, out_weight, norm_gain, stale_kv):
    seq_count = lax.axis_size("seq")
    seq_rank = lax.axis_index("seq")
    section_count = lax.axis_size("pipe")
    section_rank = lax.axis_index("pipe")
    patches, tok_dev, model_width = latent.shape
    head_dim = norm_gain.shape[2]
    slice_count = min(seq_count, 8)
    member_count = seq_count // slice_count
    member_bits = member_count.bit_length() - 1
    own_member = seq_rank % member_count
    local_width = stale_kv.shape[7]
    group_rows = slice_count * tok_dev
    own_cache = stale_kv[0, 0].reshape(2, patches, group_rows, local_width)
    group_cache = own_cache[None]
    qkv_slice = qkv_weight[0]
    out_slice = out_weight[0]
    for level_index in range(member_bits):
        got_qkv, got_out, got_cache = (
            swapped(qkv_slice, "seq", level_index),
            swapped(out_slice, "seq", level_index),
            swapped(group_cache, "seq", level_index),
        )
        is_upper = own_member >> level_index & 1 == 1
        qkv_slice = join_pair(is_upper, qkv_slice, got_qkv, 1)
        out_slice = join_pair(is_upper, out_slice, got_out, 0)
        group_cache = join_pair(is_upper, group_cache, got_cache, 0)
    homes = section_count * slice_count
    in_group = patches // GROUPS
    block_rows = in_group * tok_dev
    block_cols = model_width // section_count
    rows = slice_count * block_rows
    half = section_count // 2
    groups_of = range(member_count)
    in_slices = [[a + member_count * b for b in range(slice_count)] for a in groups_of]
    peers = [[q * seq_count + at for q in range(section_count) for at in g] for g in in_slices]
    closing_peers = [
        [
            (c * section_count + q) * seq_count + at
            for c in range(2)
            for q in range(h * half, (h + 1) * half)
            for at in g
        ]
        for h in range(2)
        for g in in_slices
    ]

    def exchange(value):
        value = value.reshape(homes, block_rows, block_cols)
        value = lax.all_to_all(value, ("pipe", "seq"), 0, 0, axis_index_groups=peers)
        return value.reshape(section_count, slice_count, block_rows, block_cols)

    vmem = pl.BlockSpec(memory_space=pltpu.VMEM)
    smem = pl.BlockSpec(memory_space=pltpu.SMEM)
    hbm = pl.BlockSpec(memory_space=pltpu.HBM)
    in_hbm = functools.partial(pltpu.with_memory_space_constraint, memory_space=pltpu.HBM)
    in_vmem = functools.partial(pltpu.with_memory_space_constraint, memory_space=pltpu.VMEM)
    where = jnp.stack((section_rank, own_member, seq_rank // member_count)).astype(jnp.int32)
    sources = latent.reshape(GROUPS, block_rows, model_width)
    stream_shape = (section_count, block_rows, block_cols)
    spread_shape = (section_count, slice_count, block_rows, block_cols)
    loads = (
        modulation.reshape(3, 1, model_width),
        norm_gain[0],
        own_cache.reshape(2, GROUPS, rows, local_width),
    )
    modulation, norm_gain, table, sources, streams, spread = pl.pallas_call(
        start_kernel,
        out_shape=tuple(pltpu.VMEM(value.shape, value.dtype) for value in loads)
        + (
            pltpu.VMEM((GROUPS, block_rows, block_cols), jnp.bfloat16),
            jax.ShapeDtypeStruct(stream_shape, jnp.bfloat16),
            jax.ShapeDtypeStruct((slice_count, block_rows, model_width), jnp.bfloat16),
        ),
        in_specs=[smem] + [hbm] * (len(loads) + 1),
        out_specs=(vmem,) * (len(loads) + 3),
        scratch_shapes=[pltpu.SemaphoreType.DMA((len(loads) + slice_count + 1,))],
        compiler_params=pltpu.CompilerParams(vmem_limit_bytes=4 * 1024 * 1024),
    )(where, in_hbm(sources), *map(in_hbm, loads))
    stale_rows = []
    if member_count > 1:
        stale_rows = [group_cache.swapaxes(0, 1).reshape(2, -1, local_width)]

    def attend(tick, features, table, weights, partial_shape):
        loading = tick == 0
        operands = (
            where,
            features,
            in_vmem(modulation),
            *map(in_hbm if loading else in_vmem, weights),
            in_vmem(norm_gain),
            *stale_rows,
            table,
        )
        in_specs = [smem] + [vmem] * (len(operands) - 1)
        out_shape = (
            jax.ShapeDtypeStruct(partial_shape, jnp.bfloat16),
            jax.ShapeDtypeStruct(table.shape, jnp.bfloat16),
        )
        scratch = []
        if loading:
            in_specs[3:5] = [hbm, hbm]
            out_shape += tuple(pltpu.VMEM(w.shape, jnp.bfloat16) for w in weights)
            scratch = [pltpu.SemaphoreType.DMA((PIECES + 1,))]
        return pl.pallas_call(
            functools.partial(section_kernel, tick, (tok_dev, head_dim)),
            out_shape=out_shape,
            in_specs=in_specs,
            out_specs=(vmem,) * len(out_shape),
            scratch_shapes=scratch,
            input_output_aliases={len(operands) - 1: 1},
            compiler_params=pltpu.CompilerParams(vmem_limit_bytes=24 * 1024 * 1024),
        )(*operands)

    def small(kernel, in_specs, *out_shapes):
        return pl.pallas_call(
            kernel,
            out_shape=tuple(jax.ShapeDtypeStruct(shape, jnp.bfloat16) for shape in out_shapes),
            in_specs=in_specs,
            out_specs=(vmem,) * len(out_shapes),
            compiler_params=pltpu.CompilerParams(vmem_limit_bytes=8 * 1024 * 1024),
        )

    ticks = GROUPS + section_count - 1
    closing_shape = (2, half, slice_count, block_rows, block_cols)
    features = lax.all_to_all(spread, "seq", 0, 0, axis_index_groups=in_slices)[None]
    weights = [qkv_slice, out_slice]
    for tick in range(ticks - 1):
        partial_out, table, *loaded = attend(tick, features, table, weights, spread_shape)
        weights = loaded or weights
        parts = exchange(partial_out)
        if tick < ticks - 2:
            streams, spread = small(
                functools.partial(settle_kernel, min(tick + 1, GROUPS - 1)),
                [vmem] * 3,
                stream_shape,
                spread_shape,
            )(parts, streams, in_vmem(sources))
        else:
            (spread,) = small(
                functools.partial(settle_last_kernel, in_group), [vmem] * 2, spread_shape
            )(parts, streams)
        features = exchange(spread)
    closing, table = attend(ticks - 1, features, table, weights, closing_shape)
    closing = lax.all_to_all(
        closing.reshape((-1,) + closing_shape[3:]),
        ("cfg", "pipe", "seq"),
        0,
        0,
        axis_index_groups=closing_peers,
    ).reshape(closing_shape)
    (guided,) = small(guide_kernel, [smem, vmem], (tok_dev, model_width // 2))(where, closing)
    return (guided[None], table.reshape(stale_kv.shape))


def solution(mesh):
    placed = (
        P(None, "seq", None),
        P("pipe", "cfg", None, None),
        P("pipe", None, "seq"),
        P("pipe", "seq", None),
        P("pipe", None, None),
        P("pipe", "cfg", None, None, "seq", None, None, None),
    )
    return jax.shard_map(
        local,
        mesh=mesh,
        in_specs=placed,
        out_specs=(P("pipe", "seq", "cfg"), P("pipe", "cfg", None, None, "seq", None, None, None)),
        check_vma=False,
    )
```

```python
import functools
import math

import jax
import jax.numpy as jnp
from jax import lax
from jax.experimental import pallas as pl
from jax.experimental.pallas import tpu as pltpu
from jax.sharding import PartitionSpec as P

GUIDANCE_SCALE = 6.0
EPSILON = 1e-06
GROUPS = 2
PIECES = 8
IN_FLIGHT = 3


def swapped(value, axis, bit):
    return lax.ppermute(value, axis, [(i, i ^ 1 << bit) for i in range(lax.axis_size(axis))])


def head_norm(values, gain_row):
    return (
        values * lax.rsqrt(jnp.mean(values * values, axis=-1, keepdims=True) + EPSILON) * gain_row
    )


def join_pair(is_upper, mine, theirs, axis_dim):
    return jnp.where(
        is_upper,
        jnp.concatenate((theirs, mine), axis_dim),
        jnp.concatenate((mine, theirs), axis_dim),
    )


def section_kernel(tick, sizes, where_ref, rows_ref, mod_ref, qkv_ref, out_ref, gain_ref, *refs):
    loading = tick == 0
    weights_from = (qkv_ref, out_ref)
    if loading:
        *refs, qkv_ref, out_ref, sems = refs
    *stale_refs, old_table_ref, partial_ref, table_ref = refs
    closing = len(partial_ref.shape) == 5
    tok_dev, head_dim = sizes
    blocks, slices, block_rows, block_cols = rows_ref.shape
    rows = slices * block_rows
    width = blocks * block_cols
    in_group = block_rows // tok_dev
    group_rows = slices * tok_dev
    groups, local_width = table_ref.shape[1], table_ref.shape[3]
    heads = local_width // head_dim
    section, own_member, own_slice = where_ref[0], where_ref[1], where_ref[2]
    group = tick - section
    copies = []
    if loading:
        piece_rows = qkv_ref.shape[0] // PIECES
        for at in range(PIECES):
            piece = pl.ds(at * piece_rows, piece_rows)
            copies.append(
                pltpu.make_async_copy(
                    weights_from[0].at[piece], qkv_ref.at[piece], sems.at[at]
                )
            )
        copies.append(pltpu.make_async_copy(weights_from[1], out_ref, sems.at[PIECES]))
        for copy in copies[:IN_FLIGHT]:
            copy.start()
    parts = [rows_ref[q].reshape(rows, block_cols).astype(jnp.float32) for q in range(blocks)]
    mean = sum(jnp.sum(x, axis=-1, keepdims=True) for x in parts) / width
    parts = [x - mean for x in parts]
    spread = sum(jnp.sum(x * x, axis=-1, keepdims=True) for x in parts) / width
    inverse = lax.rsqrt(spread + EPSILON)
    modulated = []
    for q, x in enumerate(parts):
        at = slice(q * block_cols, (q + 1) * block_cols)
        modulated.append(
            (x * inverse * (1.0 + mod_ref[1, :, at]) + mod_ref[0, :, at]).astype(jnp.bfloat16)
        )
    modulated = jnp.concatenate(modulated, axis=1)
    if loading:
        mixed = 0.0
        for at in range(PIECES):
            copies[at].wait()
            if at + IN_FLIGHT < len(copies):
                copies[at + IN_FLIGHT].start()
            piece = slice(at * piece_rows, (at + 1) * piece_rows)
            mixed = mixed + jnp.dot(
                modulated[:, piece], qkv_ref[piece, :], preferred_element_type=jnp.float32
            )
    else:
        mixed = jnp.dot(modulated, qkv_ref[...], preferred_element_type=jnp.float32)

    def by_patch(values):
        values = values.reshape(slices, in_group, tok_dev, head_dim).swapaxes(0, 1)
        return values.reshape(rows, head_dim).astype(jnp.bfloat16)

    def query_patch(shape):
        return lax.broadcasted_iota(jnp.int32, shape, 0) // tok_dev % in_group

    fresh_shape, old_shape = (rows, rows), (rows, groups * rows)
    fresh_patch = lax.broadcasted_iota(jnp.int32, fresh_shape, 1) // group_rows
    old_patch = lax.broadcasted_iota(jnp.int32, old_shape, 1) // group_rows - group * in_group
    masks = [
        (fresh_patch <= query_patch(fresh_shape)).astype(jnp.float32),
        jnp.logical_or(old_patch < 0, old_patch > query_patch(old_shape)).astype(jnp.float32),
    ]
    for ref in stale_refs:
        at = lax.broadcasted_iota(jnp.int32, (rows, ref.shape[1]), 1)
        masks.append((at // (groups * rows) != own_member).astype(jnp.float32))
    mask = jnp.concatenate(masks, axis=1)

    def column(head, kind):
        at = (3 * head + kind) * head_dim
        return mixed[:, at : at + head_dim]

    every = range(heads)
    at_head = [slice(head * head_dim, (head + 1) * head_dim) for head in every]
    queries = [head_norm(column(h, 0), gain_ref[0:1, :]).astype(jnp.bfloat16) for h in every]
    fresh = [
        (by_patch(head_norm(column(h, 1), gain_ref[1:2, :])), by_patch(column(h, 2))) for h in every
    ]

    def entries(head, kind):
        old = old_table_ref[kind, :, :, at_head[head]].reshape(groups * rows, head_dim)
        stale = [ref[kind, :, at_head[head]] for ref in stale_refs]
        return jnp.concatenate([fresh[head][kind], old] + stale)

    scores = [
        lax.dot_general(
            queries[h],
            entries(h, 0),
            (((1,), (1,)), ((), ())),
            preferred_element_type=jnp.float32,
        )
        for h in every
    ]
    weights = [mask * jnp.exp(s / math.sqrt(head_dim)) for s in scores]
    totals = [jnp.sum(w, axis=-1, keepdims=True) for w in weights]
    summed = [
        jnp.dot(weights[h].astype(jnp.bfloat16), entries(h, 1), preferred_element_type=jnp.float32)
        for h in every
    ]
    attended = [(a / t).astype(jnp.bfloat16) for a, t in zip(summed, totals)]
    attended = jnp.concatenate(attended, axis=1)

    if loading:
        copies[PIECES].wait()
    projected = jnp.dot(attended, out_ref[...], preferred_element_type=jnp.float32)
    projected = mod_ref[2] * projected
    if closing:
        close_into(partial_ref, projected, rows_ref, section, own_slice, in_group)
    else:
        out_cols = partial_ref.shape[3]
        for q in range(partial_ref.shape[0]):
            piece = projected[:, q * out_cols : (q + 1) * out_cols].astype(jnp.bfloat16)
            partial_ref[q] = piece.reshape(slices, block_rows, out_cols)

    for at in range(groups):

        @pl.when(group == at)
        def _():
            for j in range(2):
                table_ref[j, at] = jnp.concatenate([pair[j] for pair in fresh], axis=1)

        @pl.when(group != at)
        def _():
            for j in range(2):
                table_ref[j, at] = old_table_ref[j, at]


def close_into(closing_ref, projected, rows_ref, section, own_slice, in_group):
    branches, patches, slices = closing_ref.shape[:3]
    blocks, _, block_rows, block_cols = rows_ref.shape
    tok_dev = block_rows // in_group
    per_branch = blocks // branches

    @pl.when(section >= patches)
    def _():
        for piece in range(slices):
            own = (own_slice == piece).astype(jnp.float32)
            by_block = []
            for q in range(blocks):
                rows = projected[
                    piece * block_rows : (piece + 1) * block_rows,
                    q * block_cols : (q + 1) * block_cols,
                ]
                rows = rows + own * rows_ref[q, piece].astype(jnp.float32)
                by_block.append(rows.reshape(in_group, tok_dev, block_cols))
            for branch in range(branches):
                for patch in range(patches):
                    held = [by_block[branch * per_branch + k][patch] for k in range(per_branch)]
                    closing_ref[branch, patch, piece] = jnp.concatenate(held).astype(jnp.bfloat16)

    @pl.when(section < patches)
    def _():
        finished = [rows_ref[q, own_slice].astype(jnp.float32)[:tok_dev] for q in range(blocks)]
        for branch in range(branches):
            held = jnp.concatenate(finished[branch * per_branch : (branch + 1) * per_branch])
            held = held.astype(jnp.bfloat16)
            for patch in range(patches):
                for piece in range(slices):
                    closing_ref[branch, patch, piece] = held


def start_kernel(where_ref, latent_ref, *refs):
    loads = (len(refs) - 4) // 2
    from_refs, to_refs = refs[:loads], refs[loads : 2 * loads]
    sources_to, streams_to, spread_to, sems = refs[2 * loads :]
    sections, _, block_cols = streams_to.shape
    own_cols = pl.ds(pl.multiple_of(where_ref[0] * block_cols, block_cols), block_cols)
    pairs = [(latent_ref.at[0], spread_to.at[piece]) for piece in range(spread_to.shape[0])]
    pairs.append((latent_ref.at[:, :, own_cols], sources_to))
    pairs.extend(zip(from_refs, to_refs))
    copies = [
        pltpu.make_async_copy(from_ref, to_ref, sems.at[at])
        for at, (from_ref, to_ref) in enumerate(pairs)
    ]
    for copy in copies:
        copy.start()
    for section in range(1, sections):
        streams_to[section] = jnp.zeros(streams_to.shape[1:], streams_to.dtype)
    for copy in copies:
        copy.wait()
    streams_to[0] = sources_to[0]


def added(parts_ref, streams_ref, section):
    total = streams_ref[section].astype(jnp.float32)
    for piece in range(parts_ref.shape[1]):
        total = total + parts_ref[section, piece].astype(jnp.float32)
    return total


def settle_kernel(entering, parts_ref, streams_ref, sources_ref, streams_to, spread_to):
    count, slices = parts_ref.shape[:2]
    for section in range(count):
        if section == 0:
            held = sources_ref[entering]
        else:
            held = added(parts_ref, streams_ref, section - 1).astype(jnp.bfloat16)
        streams_to[section] = held
        for piece in range(slices):
            spread_to[section, piece] = held


def settle_last_kernel(in_group, parts_ref, streams_ref, spread_to):
    count, slices = parts_ref.shape[:2]
    finished = added(parts_ref, streams_ref, count - 1)
    tok_dev = finished.shape[0] // in_group
    last = added(parts_ref, streams_ref, count - 2).astype(jnp.bfloat16)
    for section in range(count):
        held = last
        if section < in_group:
            held = finished[section * tok_dev : (section + 1) * tok_dev]
            held = jnp.concatenate([held] * in_group).astype(jnp.bfloat16)
        for piece in range(slices):
            spread_to[section, piece] = held


def guide_kernel(where_ref, closing_ref, table_ref, guided_ref, table_to, sem):
    copy = pltpu.make_async_copy(table_ref, table_to, sem)
    copy.start()
    branches, patches, slices, block_rows, block_cols = closing_ref.shape
    tok_dev = guided_ref.shape[0]
    section, own_slice = where_ref[0], where_ref[2]

    def combine(pair):
        conditional, unconditional = pair
        rows = unconditional + GUIDANCE_SCALE * (conditional - unconditional)
        for at in range(block_rows // tok_dev):
            guided_ref[:, at * block_cols : (at + 1) * block_cols] = rows[
                at * tok_dev : (at + 1) * tok_dev
            ].astype(jnp.bfloat16)

    @pl.when(section >= patches)
    def _():
        pair = []
        for branch in range(branches):
            total = 0.0
            for piece in range(slices):
                total = total + closing_ref[branch, patches - 1, piece].astype(jnp.float32)
            pair.append(total.astype(jnp.bfloat16).astype(jnp.float32))
        combine(pair)

    @pl.when(section < patches)
    def _():
        combine(
            [closing_ref[branch, section, own_slice].astype(jnp.float32) for branch in range(branches)]
        )

    copy.wait()


def local(latent, modulation, qkv_weight, out_weight, norm_gain, stale_kv):
    seq_count = lax.axis_size("seq")
    seq_rank = lax.axis_index("seq")
    section_count = lax.axis_size("pipe")
    section_rank = lax.axis_index("pipe")
    patches, tok_dev, model_width = latent.shape
    head_dim = norm_gain.shape[2]
    slice_count = min(seq_count, 8)
    member_count = seq_count // slice_count
    member_bits = member_count.bit_length() - 1
    own_member = seq_rank % member_count
    local_width = stale_kv.shape[7]
    group_rows = slice_count * tok_dev
    own_cache = stale_kv[0, 0].reshape(2, patches, group_rows, local_width)
    group_cache = own_cache[None]
    qkv_slice = qkv_weight[0]
    out_slice = out_weight[0]
    for level_index in range(member_bits):
        got_qkv, got_out, got_cache = (
            swapped(qkv_slice, "seq", level_index),
            swapped(out_slice, "seq", level_index),
            swapped(group_cache, "seq", level_index),
        )
        is_upper = own_member >> level_index & 1 == 1
        qkv_slice = join_pair(is_upper, qkv_slice, got_qkv, 1)
        out_slice = join_pair(is_upper, out_slice, got_out, 0)
        group_cache = join_pair(is_upper, group_cache, got_cache, 0)
    homes = section_count * slice_count
    in_group = patches // GROUPS
    block_rows = in_group * tok_dev
    block_cols = model_width // section_count
    rows = slice_count * block_rows
    half = section_count // 2
    groups_of = range(member_count)
    in_slices = [[a + member_count * b for b in range(slice_count)] for a in groups_of]
    peers = [[q * seq_count + at for q in range(section_count) for at in g] for g in in_slices]
    closing_peers = [
        [
            (c * section_count + q) * seq_count + at
            for c in range(2)
            for q in range(h * half, (h + 1) * half)
            for at in g
        ]
        for h in range(2)
        for g in in_slices
    ]

    def exchange(value):
        value = value.reshape(homes, block_rows, block_cols)
        value = lax.all_to_all(value, ("pipe", "seq"), 0, 0, axis_index_groups=peers)
        return value.reshape(section_count, slice_count, block_rows, block_cols)

    vmem = pl.BlockSpec(memory_space=pltpu.VMEM)
    smem = pl.BlockSpec(memory_space=pltpu.SMEM)
    hbm = pl.BlockSpec(memory_space=pltpu.HBM)
    in_hbm = functools.partial(pltpu.with_memory_space_constraint, memory_space=pltpu.HBM)
    in_vmem = functools.partial(pltpu.with_memory_space_constraint, memory_space=pltpu.VMEM)
    where = jnp.stack((section_rank, own_member, seq_rank // member_count)).astype(jnp.int32)
    sources = latent.reshape(GROUPS, block_rows, model_width)
    stream_shape = (section_count, block_rows, block_cols)
    spread_shape = (section_count, slice_count, block_rows, block_cols)
    loads = (
        modulation.reshape(3, 1, model_width),
        norm_gain[0],
        own_cache.reshape(2, GROUPS, rows, local_width),
    )
    modulation, norm_gain, table, sources, streams, spread = pl.pallas_call(
        start_kernel,
        out_shape=tuple(pltpu.VMEM(value.shape, value.dtype) for value in loads)
        + (
            pltpu.VMEM((GROUPS, block_rows, block_cols), jnp.bfloat16),
            jax.ShapeDtypeStruct(stream_shape, jnp.bfloat16),
            jax.ShapeDtypeStruct((slice_count, block_rows, model_width), jnp.bfloat16),
        ),
        in_specs=[smem] + [hbm] * (len(loads) + 1),
        out_specs=(vmem,) * (len(loads) + 3),
        scratch_shapes=[pltpu.SemaphoreType.DMA((len(loads) + slice_count + 1,))],
        compiler_params=pltpu.CompilerParams(vmem_limit_bytes=4 * 1024 * 1024),
    )(where, in_hbm(sources), *map(in_hbm, loads))
    stale_rows = []
    if member_count > 1:
        stale_rows = [group_cache.swapaxes(0, 1).reshape(2, -1, local_width)]

    def attend(tick, features, table, weights, partial_shape):
        loading = tick == 0
        operands = (
            where,
            features,
            in_vmem(modulation),
            *map(in_hbm if loading else in_vmem, weights),
            in_vmem(norm_gain),
            *stale_rows,
            table,
        )
        in_specs = [smem] + [vmem] * (len(operands) - 1)
        out_shape = (
            jax.ShapeDtypeStruct(partial_shape, jnp.bfloat16),
            jax.ShapeDtypeStruct(table.shape, jnp.bfloat16),
        )
        scratch = []
        if loading:
            in_specs[3:5] = [hbm, hbm]
            out_shape += tuple(pltpu.VMEM(w.shape, jnp.bfloat16) for w in weights)
            scratch = [pltpu.SemaphoreType.DMA((PIECES + 1,))]
        return pl.pallas_call(
            functools.partial(section_kernel, tick, (tok_dev, head_dim)),
            out_shape=out_shape,
            in_specs=in_specs,
            out_specs=(vmem,) * len(out_shape),
            scratch_shapes=scratch,
            input_output_aliases={len(operands) - 1: 1},
            compiler_params=pltpu.CompilerParams(vmem_limit_bytes=24 * 1024 * 1024),
        )(*operands)

    def small(kernel, in_specs, *out_shapes):
        return pl.pallas_call(
            kernel,
            out_shape=tuple(jax.ShapeDtypeStruct(shape, jnp.bfloat16) for shape in out_shapes),
            in_specs=in_specs,
            out_specs=(vmem,) * len(out_shapes),
            compiler_params=pltpu.CompilerParams(vmem_limit_bytes=8 * 1024 * 1024),
        )

    ticks = GROUPS + section_count - 1
    closing_shape = (2, half, slice_count, block_rows, block_cols)
    features = lax.all_to_all(spread, "seq", 0, 0, axis_index_groups=in_slices)[None]
    weights = [qkv_slice, out_slice]
    for tick in range(ticks - 1):
        partial_out, table, *loaded = attend(tick, features, table, weights, spread_shape)
        weights = loaded or weights
        parts = exchange(partial_out)
        if tick < ticks - 2:
            streams, spread = small(
                functools.partial(settle_kernel, min(tick + 1, GROUPS - 1)),
                [vmem] * 3,
                stream_shape,
                spread_shape,
            )(parts, streams, in_vmem(sources))
        else:
            (spread,) = small(
                functools.partial(settle_last_kernel, in_group), [vmem] * 2, spread_shape
            )(parts, streams)
        features = exchange(spread)
    closing, table = attend(ticks - 1, features, table, weights, closing_shape)
    closing = lax.all_to_all(
        closing.reshape((-1,) + closing_shape[3:]),
        ("cfg", "pipe", "seq"),
        0,
        0,
        axis_index_groups=closing_peers,
    ).reshape(closing_shape)
    guided, table = pl.pallas_call(
        guide_kernel,
        out_shape=(
            jax.ShapeDtypeStruct((tok_dev, model_width // 2), jnp.bfloat16),
            jax.ShapeDtypeStruct(table.shape, jnp.bfloat16),
        ),
        in_specs=[smem, vmem, vmem],
        out_specs=(vmem, hbm),
        scratch_shapes=[pltpu.SemaphoreType.DMA],
        compiler_params=pltpu.CompilerParams(vmem_limit_bytes=8 * 1024 * 1024),
    )(where, closing, table)
    return (guided[None], table.reshape(stale_kv.shape))


def solution(mesh):
    placed = (
        P(None, "seq", None),
        P("pipe", "cfg", None, None),
        P("pipe", None, "seq"),
        P("pipe", "seq", None),
        P("pipe", None, None),
        P("pipe", "cfg", None, None, "seq", None, None, None),
    )
    return jax.shard_map(
        local,
        mesh=mesh,
        in_specs=placed,
        out_specs=(P("pipe", "seq", "cfg"), P("pipe", "cfg", None, None, "seq", None, None, None)),
        check_vma=False,
    )
```

```python
import functools
import math

import jax
import jax.numpy as jnp
from jax import lax
from jax.experimental import pallas as pl
from jax.experimental.pallas import tpu as pltpu
from jax.sharding import PartitionSpec as P

GUIDANCE_SCALE = 6.0
EPSILON = 1e-06
GROUPS = 2


def swapped(value, axis, bit):
    return lax.ppermute(value, axis, [(i, i ^ 1 << bit) for i in range(lax.axis_size(axis))])


def head_norm(values, gain_row):
    return (
        values * lax.rsqrt(jnp.mean(values * values, axis=-1, keepdims=True) + EPSILON) * gain_row
    )


def join_pair(is_upper, mine, theirs, axis_dim):
    return jnp.where(
        is_upper,
        jnp.concatenate((theirs, mine), axis_dim),
        jnp.concatenate((mine, theirs), axis_dim),
    )


def section_kernel(tick, sizes, where_ref, rows_ref, mod_ref, qkv_ref, out_ref, gain_ref, *refs):
    *stale_refs, old_table_ref, partial_ref, table_ref = refs
    closing = len(partial_ref.shape) == 5
    tok_dev, head_dim = sizes
    blocks, slices, block_rows, block_cols = rows_ref.shape
    rows = slices * block_rows
    width = blocks * block_cols
    in_group = block_rows // tok_dev
    group_rows = slices * tok_dev
    groups, local_width = table_ref.shape[1], table_ref.shape[3]
    heads = local_width // head_dim
    section, own_member, own_slice = where_ref[0], where_ref[1], where_ref[2]
    group = tick - section
    parts = [rows_ref[q].reshape(rows, block_cols).astype(jnp.float32) for q in range(blocks)]
    mean = sum(jnp.sum(x, axis=-1, keepdims=True) for x in parts) / width
    parts = [x - mean for x in parts]
    spread = sum(jnp.sum(x * x, axis=-1, keepdims=True) for x in parts) / width
    inverse = lax.rsqrt(spread + EPSILON)
    modulated = []
    for q, x in enumerate(parts):
        at = slice(q * block_cols, (q + 1) * block_cols)
        modulated.append(
            (x * inverse * (1.0 + mod_ref[1, :, at]) + mod_ref[0, :, at]).astype(jnp.bfloat16)
        )
    modulated = jnp.concatenate(modulated, axis=1)
    mixed = jnp.dot(modulated, qkv_ref[...], preferred_element_type=jnp.float32)

    def by_patch(values):
        values = values.reshape(slices, in_group, tok_dev, head_dim).swapaxes(0, 1)
        return values.reshape(rows, head_dim).astype(jnp.bfloat16)

    def query_patch(shape):
        return lax.broadcasted_iota(jnp.int32, shape, 0) // tok_dev % in_group

    fresh_shape, old_shape = (rows, rows), (rows, groups * rows)
    fresh_patch = lax.broadcasted_iota(jnp.int32, fresh_shape, 1) // group_rows
    old_patch = lax.broadcasted_iota(jnp.int32, old_shape, 1) // group_rows - group * in_group
    masks = [
        (fresh_patch <= query_patch(fresh_shape)).astype(jnp.float32),
        jnp.logical_or(old_patch < 0, old_patch > query_patch(old_shape)).astype(jnp.float32),
    ]
    for ref in stale_refs:
        at = lax.broadcasted_iota(jnp.int32, (rows, ref.shape[1]), 1)
        masks.append((at // (groups * rows) != own_member).astype(jnp.float32))
    mask = jnp.concatenate(masks, axis=1)

    def column(head, kind):
        at = (3 * head + kind) * head_dim
        return mixed[:, at : at + head_dim]

    every = range(heads)
    at_head = [slice(head * head_dim, (head + 1) * head_dim) for head in every]
    queries = [head_norm(column(h, 0), gain_ref[0:1, :]).astype(jnp.bfloat16) for h in every]
    fresh = [
        (by_patch(head_norm(column(h, 1), gain_ref[1:2, :])), by_patch(column(h, 2))) for h in every
    ]

    def entries(head, kind):
        old = old_table_ref[kind, :, :, at_head[head]].reshape(groups * rows, head_dim)
        stale = [ref[kind, :, at_head[head]] for ref in stale_refs]
        return jnp.concatenate([fresh[head][kind], old] + stale)

    scores = [
        lax.dot_general(
            queries[h],
            entries(h, 0),
            (((1,), (1,)), ((), ())),
            preferred_element_type=jnp.float32,
        )
        for h in every
    ]
    weights = [mask * jnp.exp(s / math.sqrt(head_dim)) for s in scores]
    totals = [jnp.sum(w, axis=-1, keepdims=True) for w in weights]
    summed = [
        jnp.dot(weights[h].astype(jnp.bfloat16), entries(h, 1), preferred_element_type=jnp.float32)
        for h in every
    ]
    attended = [(a / t).astype(jnp.bfloat16) for a, t in zip(summed, totals)]
    attended = jnp.concatenate(attended, axis=1)

    projected = jnp.dot(attended, out_ref[...], preferred_element_type=jnp.float32)
    projected = mod_ref[2] * projected
    if closing:
        close_into(partial_ref, projected, rows_ref, section, own_slice, in_group)
    else:
        out_cols = partial_ref.shape[3]
        for q in range(partial_ref.shape[0]):
            piece = projected[:, q * out_cols : (q + 1) * out_cols].astype(jnp.bfloat16)
            partial_ref[q] = piece.reshape(slices, block_rows, out_cols)

    for at in range(groups):

        @pl.when(group == at)
        def _():
            for j in range(2):
                table_ref[j, at] = jnp.concatenate([pair[j] for pair in fresh], axis=1)

        @pl.when(group != at)
        def _():
            for j in range(2):
                table_ref[j, at] = old_table_ref[j, at]


def close_into(closing_ref, projected, rows_ref, section, own_slice, in_group):
    branches, patches, slices = closing_ref.shape[:3]
    blocks, _, block_rows, block_cols = rows_ref.shape
    tok_dev = block_rows // in_group
    per_branch = blocks // branches

    @pl.when(section >= patches)
    def _():
        for piece in range(slices):
            own = (own_slice == piece).astype(jnp.float32)
            by_block = []
            for q in range(blocks):
                rows = projected[
                    piece * block_rows : (piece + 1) * block_rows,
                    q * block_cols : (q + 1) * block_cols,
                ]
                rows = rows + own * rows_ref[q, piece].astype(jnp.float32)
                by_block.append(rows.reshape(in_group, tok_dev, block_cols))
            for branch in range(branches):
                for patch in range(patches):
                    held = [by_block[branch * per_branch + k][patch] for k in range(per_branch)]
                    closing_ref[branch, patch, piece] = jnp.concatenate(held).astype(jnp.bfloat16)

    @pl.when(section < patches)
    def _():
        finished = [rows_ref[q, own_slice].astype(jnp.float32)[:tok_dev] for q in range(blocks)]
        for branch in range(branches):
            held = jnp.concatenate(finished[branch * per_branch : (branch + 1) * per_branch])
            held = held.astype(jnp.bfloat16)
            for patch in range(patches):
                for piece in range(slices):
                    closing_ref[branch, patch, piece] = held


def start_kernel(where_ref, latent_ref, qkv_ref, out_ref, *refs):
    del qkv_ref, out_ref
    loads = (len(refs) - 4) // 2
    from_refs, to_refs = refs[:loads], refs[loads : 2 * loads]
    sources_to, streams_to, spread_to, sems = refs[2 * loads :]
    sections, _, block_cols = streams_to.shape
    own_cols = pl.ds(pl.multiple_of(where_ref[0] * block_cols, block_cols), block_cols)
    pairs = [(latent_ref.at[0], spread_to.at[piece]) for piece in range(spread_to.shape[0])]
    pairs.append((latent_ref.at[:, :, own_cols], sources_to))
    pairs.extend(zip(from_refs, to_refs))
    copies = [
        pltpu.make_async_copy(from_ref, to_ref, sems.at[at])
        for at, (from_ref, to_ref) in enumerate(pairs)
    ]
    for copy in copies:
        copy.start()
    for section in range(1, sections):
        streams_to[section] = jnp.zeros(streams_to.shape[1:], streams_to.dtype)
    for copy in copies:
        copy.wait()
    streams_to[0] = sources_to[0]


def added(parts_ref, streams_ref, section):
    total = streams_ref[section].astype(jnp.float32)
    for piece in range(parts_ref.shape[1]):
        total = total + parts_ref[section, piece].astype(jnp.float32)
    return total


def settle_kernel(entering, parts_ref, streams_ref, sources_ref, streams_to, spread_to):
    count, slices = parts_ref.shape[:2]
    for section in range(count):
        if section == 0:
            held = sources_ref[entering]
        else:
            held = added(parts_ref, streams_ref, section - 1).astype(jnp.bfloat16)
        streams_to[section] = held
        for piece in range(slices):
            spread_to[section, piece] = held


def settle_last_kernel(in_group, parts_ref, streams_ref, spread_to):
    count, slices = parts_ref.shape[:2]
    finished = added(parts_ref, streams_ref, count - 1)
    tok_dev = finished.shape[0] // in_group
    last = added(parts_ref, streams_ref, count - 2).astype(jnp.bfloat16)
    for section in range(count):
        held = last
        if section < in_group:
            held = finished[section * tok_dev : (section + 1) * tok_dev]
            held = jnp.concatenate([held] * in_group).astype(jnp.bfloat16)
        for piece in range(slices):
            spread_to[section, piece] = held


def guide_kernel(where_ref, closing_ref, table_ref, guided_ref, table_to, sem):
    copy = pltpu.make_async_copy(table_ref, table_to, sem)
    copy.start()
    branches, patches, slices, block_rows, block_cols = closing_ref.shape
    tok_dev = guided_ref.shape[0]
    section, own_slice = where_ref[0], where_ref[2]

    def combine(pair):
        conditional, unconditional = pair
        rows = unconditional + GUIDANCE_SCALE * (conditional - unconditional)
        for at in range(block_rows // tok_dev):
            guided_ref[:, at * block_cols : (at + 1) * block_cols] = rows[
                at * tok_dev : (at + 1) * tok_dev
            ].astype(jnp.bfloat16)

    @pl.when(section >= patches)
    def _():
        pair = []
        for branch in range(branches):
            total = 0.0
            for piece in range(slices):
                total = total + closing_ref[branch, patches - 1, piece].astype(jnp.float32)
            pair.append(total.astype(jnp.bfloat16).astype(jnp.float32))
        combine(pair)

    @pl.when(section < patches)
    def _():
        combine(
            [closing_ref[branch, section, own_slice].astype(jnp.float32) for branch in range(branches)]
        )

    copy.wait()


def local(latent, modulation, qkv_weight, out_weight, norm_gain, stale_kv):
    seq_count = lax.axis_size("seq")
    seq_rank = lax.axis_index("seq")
    section_count = lax.axis_size("pipe")
    section_rank = lax.axis_index("pipe")
    patches, tok_dev, model_width = latent.shape
    head_dim = norm_gain.shape[2]
    slice_count = min(seq_count, 8)
    member_count = seq_count // slice_count
    member_bits = member_count.bit_length() - 1
    own_member = seq_rank % member_count
    local_width = stale_kv.shape[7]
    group_rows = slice_count * tok_dev
    own_cache = stale_kv[0, 0].reshape(2, patches, group_rows, local_width)
    group_cache = own_cache[None]
    qkv_slice = qkv_weight[0]
    out_slice = out_weight[0]
    for level_index in range(member_bits):
        got_qkv, got_out, got_cache = (
            swapped(qkv_slice, "seq", level_index),
            swapped(out_slice, "seq", level_index),
            swapped(group_cache, "seq", level_index),
        )
        is_upper = own_member >> level_index & 1 == 1
        qkv_slice = join_pair(is_upper, qkv_slice, got_qkv, 1)
        out_slice = join_pair(is_upper, out_slice, got_out, 0)
        group_cache = join_pair(is_upper, group_cache, got_cache, 0)
    homes = section_count * slice_count
    in_group = patches // GROUPS
    block_rows = in_group * tok_dev
    block_cols = model_width // section_count
    rows = slice_count * block_rows
    half = section_count // 2
    groups_of = range(member_count)
    in_slices = [[a + member_count * b for b in range(slice_count)] for a in groups_of]
    peers = [[q * seq_count + at for q in range(section_count) for at in g] for g in in_slices]
    closing_peers = [
        [
            (c * section_count + q) * seq_count + at
            for c in range(2)
            for q in range(h * half, (h + 1) * half)
            for at in g
        ]
        for h in range(2)
        for g in in_slices
    ]

    def exchange(value):
        value = value.reshape(homes, block_rows, block_cols)
        value = lax.all_to_all(value, ("pipe", "seq"), 0, 0, axis_index_groups=peers)
        return value.reshape(section_count, slice_count, block_rows, block_cols)

    vmem = pl.BlockSpec(memory_space=pltpu.VMEM)
    smem = pl.BlockSpec(memory_space=pltpu.SMEM)
    hbm = pl.BlockSpec(memory_space=pltpu.HBM)
    in_hbm = functools.partial(pltpu.with_memory_space_constraint, memory_space=pltpu.HBM)
    in_vmem = functools.partial(pltpu.with_memory_space_constraint, memory_space=pltpu.VMEM)
    where = jnp.stack((section_rank, own_member, seq_rank // member_count)).astype(jnp.int32)
    sources = latent.reshape(GROUPS, block_rows, model_width)
    stream_shape = (section_count, block_rows, block_cols)
    spread_shape = (section_count, slice_count, block_rows, block_cols)
    loads = (
        modulation.reshape(3, 1, model_width),
        norm_gain[0],
        own_cache.reshape(2, GROUPS, rows, local_width),
    )
    modulation, norm_gain, table, sources, streams, spread = pl.pallas_call(
        start_kernel,
        out_shape=tuple(pltpu.VMEM(value.shape, value.dtype) for value in loads)
        + (
            pltpu.VMEM((GROUPS, block_rows, block_cols), jnp.bfloat16),
            jax.ShapeDtypeStruct(stream_shape, jnp.bfloat16),
            jax.ShapeDtypeStruct((slice_count, block_rows, model_width), jnp.bfloat16),
        ),
        in_specs=[smem] + [hbm] * (len(loads) + 3),
        out_specs=(vmem,) * (len(loads) + 3),
        scratch_shapes=[pltpu.SemaphoreType.DMA((len(loads) + slice_count + 1,))],
        compiler_params=pltpu.CompilerParams(vmem_limit_bytes=4 * 1024 * 1024),
    )(where, in_hbm(sources), in_hbm(qkv_slice), in_hbm(out_slice), *map(in_hbm, loads))
    stale_rows = []
    if member_count > 1:
        stale_rows = [group_cache.swapaxes(0, 1).reshape(2, -1, local_width)]

    def attend(tick, features, table, partial_shape):
        operands = (
            where,
            features,
            in_vmem(modulation),
            in_vmem(qkv_slice),
            in_vmem(out_slice),
            in_vmem(norm_gain),
            *stale_rows,
            table,
        )
        return pl.pallas_call(
            functools.partial(section_kernel, tick, (tok_dev, head_dim)),
            out_shape=(
                jax.ShapeDtypeStruct(partial_shape, jnp.bfloat16),
                jax.ShapeDtypeStruct(table.shape, jnp.bfloat16),
            ),
            in_specs=[smem] + [vmem] * (len(operands) - 1),
            out_specs=(vmem, vmem),
            input_output_aliases={len(operands) - 1: 1},
            compiler_params=pltpu.CompilerParams(vmem_limit_bytes=24 * 1024 * 1024),
        )(*operands)

    def small(kernel, in_specs, *out_shapes):
        return pl.pallas_call(
            kernel,
            out_shape=tuple(jax.ShapeDtypeStruct(shape, jnp.bfloat16) for shape in out_shapes),
            in_specs=in_specs,
            out_specs=(vmem,) * len(out_shapes),
            compiler_params=pltpu.CompilerParams(vmem_limit_bytes=8 * 1024 * 1024),
        )

    ticks = GROUPS + section_count - 1
    closing_shape = (2, half, slice_count, block_rows, block_cols)
    features = lax.all_to_all(spread, "seq", 0, 0, axis_index_groups=in_slices)[None]
    for tick in range(ticks - 1):
        partial_out, table = attend(tick, features, table, spread_shape)
        parts = exchange(partial_out)
        if tick < ticks - 2:
            streams, spread = small(
                functools.partial(settle_kernel, min(tick + 1, GROUPS - 1)),
                [vmem] * 3,
                stream_shape,
                spread_shape,
            )(parts, streams, in_vmem(sources))
        else:
            (spread,) = small(
                functools.partial(settle_last_kernel, in_group), [vmem] * 2, spread_shape
            )(parts, streams)
        features = exchange(spread)
    closing, table = attend(ticks - 1, features, table, closing_shape)
    closing = lax.all_to_all(
        closing.reshape((-1,) + closing_shape[3:]),
        ("cfg", "pipe", "seq"),
        0,
        0,
        axis_index_groups=closing_peers,
    ).reshape(closing_shape)
    guided, table = pl.pallas_call(
        guide_kernel,
        out_shape=(
            jax.ShapeDtypeStruct((tok_dev, model_width // 2), jnp.bfloat16),
            jax.ShapeDtypeStruct(table.shape, jnp.bfloat16),
        ),
        in_specs=[smem, vmem, vmem],
        out_specs=(vmem, hbm),
        scratch_shapes=[pltpu.SemaphoreType.DMA],
        compiler_params=pltpu.CompilerParams(vmem_limit_bytes=8 * 1024 * 1024),
    )(where, closing, table)
    return (guided[None], table.reshape(stale_kv.shape))


def solution(mesh):
    placed = (
        P(None, "seq", None),
        P("pipe", "cfg", None, None),
        P("pipe", None, "seq"),
        P("pipe", "seq", None),
        P("pipe", None, None),
        P("pipe", "cfg", None, None, "seq", None, None, None),
    )
    return jax.shard_map(
        local,
        mesh=mesh,
        in_specs=placed,
        out_specs=(P("pipe", "seq", "cfg"), P("pipe", "cfg", None, None, "seq", None, None, None)),
        check_vma=False,
    )
```

```python
import functools
import math

import jax
import jax.numpy as jnp
from jax import lax
from jax.experimental import pallas as pl
from jax.experimental.pallas import tpu as pltpu
from jax.sharding import PartitionSpec as P

GUIDANCE_SCALE = 6.0
EPSILON = 1e-06
GROUPS = 2


def swapped(value, axis, bit):
    return lax.ppermute(value, axis, [(i, i ^ 1 << bit) for i in range(lax.axis_size(axis))])


def head_norm(values, gain_row):
    return (
        values * lax.rsqrt(jnp.mean(values * values, axis=-1, keepdims=True) + EPSILON) * gain_row
    )


def join_pair(is_upper, mine, theirs, axis_dim):
    return jnp.where(
        is_upper,
        jnp.concatenate((theirs, mine), axis_dim),
        jnp.concatenate((mine, theirs), axis_dim),
    )


def section_kernel(tick, closing, sizes, where_ref, rows_ref, mod_ref, qkv_ref, out_ref, gain_ref, *refs):
    if closing:
        *refs, held_ref, sems = refs
    *stale_refs, old_table_ref, partial_ref, table_ref = refs
    tok_dev, head_dim = sizes
    blocks, slices, block_rows, block_cols = rows_ref.shape
    rows = slices * block_rows
    width = blocks * block_cols
    in_group = block_rows // tok_dev
    group_rows = slices * tok_dev
    groups, local_width = old_table_ref.shape[1], old_table_ref.shape[3]
    heads = local_width // head_dim
    section, own_member, own_slice = where_ref[0], where_ref[1], where_ref[2]
    group = tick - section
    parts = [rows_ref[q].reshape(rows, block_cols).astype(jnp.float32) for q in range(blocks)]
    mean = sum(jnp.sum(x, axis=-1, keepdims=True) for x in parts) / width
    parts = [x - mean for x in parts]
    spread = sum(jnp.sum(x * x, axis=-1, keepdims=True) for x in parts) / width
    inverse = lax.rsqrt(spread + EPSILON)
    modulated = []
    for q, x in enumerate(parts):
        at = slice(q * block_cols, (q + 1) * block_cols)
        modulated.append(
            (x * inverse * (1.0 + mod_ref[1, :, at]) + mod_ref[0, :, at]).astype(jnp.bfloat16)
        )
    modulated = jnp.concatenate(modulated, axis=1)
    pair = 2 if heads % 2 == 0 else 1
    pair_width = 3 * pair * head_dim
    mixed = [
        jnp.dot(
            modulated,
            qkv_ref[:, at * pair_width : (at + 1) * pair_width],
            preferred_element_type=jnp.float32,
        )
        for at in range(heads // pair)
    ]

    def by_patch(values):
        values = values.reshape(slices, in_group, tok_dev, head_dim).swapaxes(0, 1)
        return values.reshape(rows, head_dim).astype(jnp.bfloat16)

    def query_patch(shape):
        return lax.broadcasted_iota(jnp.int32, shape, 0) // tok_dev % in_group

    fresh_shape, old_shape = (rows, rows), (rows, groups * rows)
    fresh_patch = lax.broadcasted_iota(jnp.int32, fresh_shape, 1) // group_rows
    old_patch = lax.broadcasted_iota(jnp.int32, old_shape, 1) // group_rows - group * in_group
    masks = [
        (fresh_patch <= query_patch(fresh_shape)).astype(jnp.float32),
        jnp.logical_or(old_patch < 0, old_patch > query_patch(old_shape)).astype(jnp.float32),
    ]
    for ref in stale_refs:
        at = lax.broadcasted_iota(jnp.int32, (rows, ref.shape[1]), 1)
        masks.append((at // (groups * rows) != own_member).astype(jnp.float32))
    mask = jnp.concatenate(masks, axis=1)

    def column(head, kind):
        at = (3 * (head % pair) + kind) * head_dim
        return mixed[head // pair][:, at : at + head_dim]

    at_head = [slice(head * head_dim, (head + 1) * head_dim) for head in range(heads)]
    fresh = []

    def attend(head):
        at = at_head[head]
        query = head_norm(column(head, 0), gain_ref[0:1, :]).astype(jnp.bfloat16)
        key = by_patch(head_norm(column(head, 1), gain_ref[1:2, :]))
        fresh.append((key, by_patch(column(head, 2))))

        def entries(kind):
            old = old_table_ref[kind, :, :, at].reshape(groups * rows, head_dim)
            return jnp.concatenate([fresh[head][kind], old] + [ref[kind, :, at] for ref in stale_refs])

        scores = lax.dot_general(
            query, entries(0), (((1,), (1,)), ((), ())), preferred_element_type=jnp.float32
        )
        weights = mask * jnp.exp(scores / math.sqrt(head_dim))
        total = jnp.sum(weights, axis=-1, keepdims=True)
        summed = jnp.dot(
            weights.astype(jnp.bfloat16), entries(1), preferred_element_type=jnp.float32
        )
        return (summed / total).astype(jnp.bfloat16)

    attended = [attend(head) for head in range(heads)]

    def fresh_rows(kind):
        return jnp.concatenate([entry[kind] for entry in fresh], axis=1)

    copies = []
    if closing:
        last = groups - 1
        for kind in range(2):
            held_ref[kind] = jnp.where(group == last, fresh_rows(kind), old_table_ref[kind, last])
        copies = [
            pltpu.make_async_copy(held_ref, table_ref.at[:, last], sems.at[0]),
            pltpu.make_async_copy(
                old_table_ref.at[:, pl.ds(0, last)], table_ref.at[:, pl.ds(0, last)], sems.at[1]
            ),
        ]
        for copy in copies:
            copy.start()
    projected = 0.0
    for at in range(heads // pair):
        projected = projected + jnp.dot(
            jnp.concatenate(attended[at * pair : (at + 1) * pair], axis=1),
            out_ref[at * pair * head_dim : (at + 1) * pair * head_dim, :],
            preferred_element_type=jnp.float32,
        )
    projected = mod_ref[2] * projected
    if closing:
        close_into(partial_ref, projected, rows_ref, section, own_slice, in_group)
    else:
        out_cols = partial_ref.shape[3]
        for q in range(partial_ref.shape[0]):
            piece = projected[:, q * out_cols : (q + 1) * out_cols].astype(jnp.bfloat16)
            partial_ref[q] = piece.reshape(slices, block_rows, out_cols)

    for copy in copies:
        copy.wait()
    for at in range(0 if closing else groups):

        @pl.when(group == at)
        def _():
            for kind in range(2):
                table_ref[kind, at] = fresh_rows(kind)

        @pl.when(group != at)
        def _():
            for kind in range(2):
                table_ref[kind, at] = old_table_ref[kind, at]


def close_into(closing_ref, projected, rows_ref, section, own_slice, in_group):
    branches, patches, slices = closing_ref.shape[:3]
    blocks, _, block_rows, block_cols = rows_ref.shape
    tok_dev = block_rows // in_group
    per_branch = blocks // branches

    @pl.when(section >= patches)
    def _():
        for piece in range(slices):
            own = (own_slice == piece).astype(jnp.float32)
            by_block = []
            for q in range(blocks):
                rows = projected[
                    piece * block_rows : (piece + 1) * block_rows,
                    q * block_cols : (q + 1) * block_cols,
                ]
                rows = rows + own * rows_ref[q, piece].astype(jnp.float32)
                by_block.append(rows.reshape(in_group, tok_dev, block_cols))
            for branch in range(branches):
                for patch in range(patches):
                    held = [by_block[branch * per_branch + k][patch] for k in range(per_branch)]
                    closing_ref[branch, patch, piece] = jnp.concatenate(held).astype(jnp.bfloat16)

    @pl.when(section < patches)
    def _():
        finished = [rows_ref[q, own_slice].astype(jnp.float32)[:tok_dev] for q in range(blocks)]
        for branch in range(branches):
            held = jnp.concatenate(finished[branch * per_branch : (branch + 1) * per_branch])
            held = held.astype(jnp.bfloat16)
            for patch in range(patches):
                for piece in range(slices):
                    closing_ref[branch, patch, piece] = held


def start_kernel(where_ref, latent_ref, qkv_ref, out_ref, *refs):
    del qkv_ref, out_ref
    loads = (len(refs) - 4) // 2
    from_refs, to_refs = refs[:loads], refs[loads : 2 * loads]
    sources_to, streams_to, spread_to, sems = refs[2 * loads :]
    sections, _, block_cols = streams_to.shape
    own_cols = pl.ds(pl.multiple_of(where_ref[0] * block_cols, block_cols), block_cols)
    pairs = [(latent_ref.at[0], spread_to.at[piece]) for piece in range(spread_to.shape[0])]
    pairs.append((latent_ref.at[:, :, own_cols], sources_to))
    pairs.extend(zip(from_refs, to_refs))
    copies = [
        pltpu.make_async_copy(from_ref, to_ref, sems.at[at])
        for at, (from_ref, to_ref) in enumerate(pairs)
    ]
    for copy in copies:
        copy.start()
    for section in range(1, sections):
        streams_to[section] = jnp.zeros(streams_to.shape[1:], streams_to.dtype)
    for copy in copies:
        copy.wait()
    streams_to[0] = sources_to[0]


def added(parts_ref, streams_ref, section):
    total = streams_ref[section].astype(jnp.float32)
    for piece in range(parts_ref.shape[1]):
        total = total + parts_ref[section, piece].astype(jnp.float32)
    return total


def settle_kernel(entering, parts_ref, streams_ref, sources_ref, streams_to, spread_to):
    count, slices = parts_ref.shape[:2]
    for section in range(count):
        if section == 0:
            held = sources_ref[entering]
        else:
            held = added(parts_ref, streams_ref, section - 1).astype(jnp.bfloat16)
        streams_to[section] = held
        for piece in range(slices):
            spread_to[section, piece] = held


def settle_last_kernel(in_group, parts_ref, streams_ref, spread_to):
    count, slices = parts_ref.shape[:2]
    finished = added(parts_ref, streams_ref, count - 1)
    tok_dev = finished.shape[0] // in_group
    last = added(parts_ref, streams_ref, count - 2).astype(jnp.bfloat16)
    for section in range(count):
        held = last
        if section < in_group:
            held = finished[section * tok_dev : (section + 1) * tok_dev]
            held = jnp.concatenate([held] * in_group).astype(jnp.bfloat16)
        for piece in range(slices):
            spread_to[section, piece] = held


def guide_kernel(where_ref, closing_ref, guided_ref):
    branches, patches, slices, block_rows, block_cols = closing_ref.shape
    tok_dev = guided_ref.shape[0]
    section, own_slice = where_ref[0], where_ref[2]

    def combine(pair):
        conditional, unconditional = pair
        rows = unconditional + GUIDANCE_SCALE * (conditional - unconditional)
        for at in range(block_rows // tok_dev):
            guided_ref[:, at * block_cols : (at + 1) * block_cols] = rows[
                at * tok_dev : (at + 1) * tok_dev
            ].astype(jnp.bfloat16)

    @pl.when(section >= patches)
    def _():
        pair = []
        for branch in range(branches):
            total = 0.0
            for piece in range(slices):
                total = total + closing_ref[branch, patches - 1, piece].astype(jnp.float32)
            pair.append(total.astype(jnp.bfloat16).astype(jnp.float32))
        combine(pair)

    @pl.when(section < patches)
    def _():
        combine(
            [closing_ref[branch, section, own_slice].astype(jnp.float32) for branch in range(branches)]
        )


def local(latent, modulation, qkv_weight, out_weight, norm_gain, stale_kv):
    seq_count = lax.axis_size("seq")
    seq_rank = lax.axis_index("seq")
    section_count = lax.axis_size("pipe")
    section_rank = lax.axis_index("pipe")
    patches, tok_dev, model_width = latent.shape
    head_dim = norm_gain.shape[2]
    slice_count = min(seq_count, 8)
    member_count = seq_count // slice_count
    member_bits = member_count.bit_length() - 1
    own_member = seq_rank % member_count
    local_width = stale_kv.shape[7]
    group_rows = slice_count * tok_dev
    own_cache = stale_kv[0, 0].reshape(2, patches, group_rows, local_width)
    group_cache = own_cache[None]
    qkv_slice = qkv_weight[0]
    out_slice = out_weight[0]
    for level_index in range(member_bits):
        got_qkv, got_out, got_cache = (
            swapped(qkv_slice, "seq", level_index),
            swapped(out_slice, "seq", level_index),
            swapped(group_cache, "seq", level_index),
        )
        is_upper = own_member >> level_index & 1 == 1
        qkv_slice = join_pair(is_upper, qkv_slice, got_qkv, 1)
        out_slice = join_pair(is_upper, out_slice, got_out, 0)
        group_cache = join_pair(is_upper, group_cache, got_cache, 0)
    homes = section_count * slice_count
    in_group = patches // GROUPS
    block_rows = in_group * tok_dev
    block_cols = model_width // section_count
    rows = slice_count * block_rows
    half = section_count // 2
    groups_of = range(member_count)
    in_slices = [[a + member_count * b for b in range(slice_count)] for a in groups_of]
    peers = [[q * seq_count + at for q in range(section_count) for at in g] for g in in_slices]
    closing_peers = [
        [
            (c * section_count + q) * seq_count + at
            for c in range(2)
            for q in range(h * half, (h + 1) * half)
            for at in g
        ]
        for h in range(2)
        for g in in_slices
    ]

    def exchange(value):
        value = value.reshape(homes, block_rows, block_cols)
        value = lax.all_to_all(value, ("pipe", "seq"), 0, 0, axis_index_groups=peers)
        return value.reshape(section_count, slice_count, block_rows, block_cols)

    vmem = pl.BlockSpec(memory_space=pltpu.VMEM)
    smem = pl.BlockSpec(memory_space=pltpu.SMEM)
    hbm = pl.BlockSpec(memory_space=pltpu.HBM)
    in_hbm = functools.partial(pltpu.with_memory_space_constraint, memory_space=pltpu.HBM)
    in_vmem = functools.partial(pltpu.with_memory_space_constraint, memory_space=pltpu.VMEM)
    where = jnp.stack((section_rank, own_member, seq_rank // member_count)).astype(jnp.int32)
    sources = latent.reshape(GROUPS, block_rows, model_width)
    stream_shape = (section_count, block_rows, block_cols)
    spread_shape = (section_count, slice_count, block_rows, block_cols)
    loads = (
        modulation.reshape(3, 1, model_width),
        norm_gain[0],
        own_cache.reshape(2, GROUPS, rows, local_width),
    )
    modulation, norm_gain, table, sources, streams, spread = pl.pallas_call(
        start_kernel,
        out_shape=tuple(pltpu.VMEM(value.shape, value.dtype) for value in loads)
        + (
            pltpu.VMEM((GROUPS, block_rows, block_cols), jnp.bfloat16),
            jax.ShapeDtypeStruct(stream_shape, jnp.bfloat16),
            jax.ShapeDtypeStruct((slice_count, block_rows, model_width), jnp.bfloat16),
        ),
        in_specs=[smem] + [hbm] * (len(loads) + 3),
        out_specs=(vmem,) * (len(loads) + 3),
        scratch_shapes=[pltpu.SemaphoreType.DMA((len(loads) + slice_count + 1,))],
        compiler_params=pltpu.CompilerParams(vmem_limit_bytes=4 * 1024 * 1024),
    )(where, in_hbm(sources), in_hbm(qkv_slice), in_hbm(out_slice), *map(in_hbm, loads))
    stale_rows = []
    if member_count > 1:
        stale_rows = [group_cache.swapaxes(0, 1).reshape(2, -1, local_width)]

    ticks = GROUPS + section_count - 1

    def attend(tick, features, table, partial_shape):
        operands = (
            where,
            features,
            in_vmem(modulation),
            in_vmem(qkv_slice),
            in_vmem(out_slice),
            in_vmem(norm_gain),
            *stale_rows,
            table,
        )
        closing = tick == ticks - 1
        scratch = []
        if closing:
            scratch = [pltpu.VMEM((2, rows, local_width), jnp.bfloat16), pltpu.SemaphoreType.DMA((2,))]
        return pl.pallas_call(
            functools.partial(section_kernel, tick, closing, (tok_dev, head_dim)),
            out_shape=(
                jax.ShapeDtypeStruct(partial_shape, jnp.bfloat16),
                jax.ShapeDtypeStruct(table.shape, jnp.bfloat16),
            ),
            in_specs=[smem] + [vmem] * (len(operands) - 1),
            out_specs=(vmem, hbm if closing else vmem),
            scratch_shapes=scratch,
            input_output_aliases={} if closing else {len(operands) - 1: 1},
            compiler_params=pltpu.CompilerParams(vmem_limit_bytes=24 * 1024 * 1024),
        )(*operands)

    def small(kernel, in_specs, *out_shapes):
        return pl.pallas_call(
            kernel,
            out_shape=tuple(jax.ShapeDtypeStruct(shape, jnp.bfloat16) for shape in out_shapes),
            in_specs=in_specs,
            out_specs=(vmem,) * len(out_shapes),
            compiler_params=pltpu.CompilerParams(vmem_limit_bytes=8 * 1024 * 1024),
        )

    closing_shape = (2, half, slice_count, block_rows, block_cols)
    features = lax.all_to_all(spread, "seq", 0, 0, axis_index_groups=in_slices)[None]
    for tick in range(ticks - 1):
        partial_out, table = attend(tick, features, table, spread_shape)
        parts = exchange(partial_out)
        if tick < ticks - 2:
            streams, spread = small(
                functools.partial(settle_kernel, min(tick + 1, GROUPS - 1)),
                [vmem] * 3,
                stream_shape,
                spread_shape,
            )(parts, streams, in_vmem(sources))
        else:
            (spread,) = small(
                functools.partial(settle_last_kernel, in_group), [vmem] * 2, spread_shape
            )(parts, streams)
        features = exchange(spread)
    closing, table = attend(ticks - 1, features, table, closing_shape)
    closing = lax.all_to_all(
        closing.reshape((-1,) + closing_shape[3:]),
        ("cfg", "pipe", "seq"),
        0,
        0,
        axis_index_groups=closing_peers,
    ).reshape(closing_shape)
    (guided,) = small(guide_kernel, [smem, vmem], (tok_dev, model_width // 2))(where, closing)
    return (guided[None], table.reshape(stale_kv.shape))


def solution(mesh):
    placed = (
        P(None, "seq", None),
        P("pipe", "cfg", None, None),
        P("pipe", None, "seq"),
        P("pipe", "seq", None),
        P("pipe", None, None),
        P("pipe", "cfg", None, None, "seq", None, None, None),
    )
    return jax.shard_map(
        local,
        mesh=mesh,
        in_specs=placed,
        out_specs=(P("pipe", "seq", "cfg"), P("pipe", "cfg", None, None, "seq", None, None, None)),
        check_vma=False,
    )
```

```python
import functools
import math

import jax
import jax.numpy as jnp
from jax import lax
from jax.experimental import pallas as pl
from jax.experimental.pallas import tpu as pltpu
from jax.sharding import PartitionSpec as P

GUIDANCE_SCALE = 6.0
EPSILON = 1e-06
GROUPS = 2


def swapped(value, axis, bit):
    return lax.ppermute(value, axis, [(i, i ^ 1 << bit) for i in range(lax.axis_size(axis))])


def head_norm(values, gain_row):
    return (
        values * lax.rsqrt(jnp.mean(values * values, axis=-1, keepdims=True) + EPSILON) * gain_row
    )


def join_pair(is_upper, mine, theirs, axis_dim):
    return jnp.where(
        is_upper,
        jnp.concatenate((theirs, mine), axis_dim),
        jnp.concatenate((mine, theirs), axis_dim),
    )


def section_kernel(tick, sizes, where_ref, rows_ref, mod_ref, qkv_ref, out_ref, gain_ref, *refs):
    *stale_refs, old_table_ref, partial_ref, table_ref = refs
    closing = len(partial_ref.shape) == 5
    tok_dev, head_dim = sizes
    blocks, slices, block_rows, block_cols = rows_ref.shape
    rows = slices * block_rows
    width = blocks * block_cols
    in_group = block_rows // tok_dev
    group_rows = slices * tok_dev
    groups, local_width = table_ref.shape[1], table_ref.shape[3]
    heads = local_width // head_dim
    section, own_member, own_slice = where_ref[0], where_ref[1], where_ref[2]
    group = tick - section
    parts = [rows_ref[q].reshape(rows, block_cols).astype(jnp.float32) for q in range(blocks)]
    mean = jnp.sum(sum(parts), axis=-1, keepdims=True) * (1.0 / width)
    parts = [x - mean for x in parts]
    spread = jnp.sum(sum(x * x for x in parts), axis=-1, keepdims=True) * (1.0 / width)
    inverse = lax.rsqrt(spread + EPSILON)
    modulated = []
    for q, x in enumerate(parts):
        at = slice(q * block_cols, (q + 1) * block_cols)
        modulated.append(
            (x * inverse * (1.0 + mod_ref[1, :, at]) + mod_ref[0, :, at]).astype(jnp.bfloat16)
        )
    modulated = jnp.concatenate(modulated, axis=1)
    mixed = jnp.dot(modulated, qkv_ref[...], preferred_element_type=jnp.float32)

    def stacked(kind):
        at = [(3 * head + kind) * head_dim for head in range(heads)]
        return jnp.stack([mixed[:, start : start + head_dim] for start in at])

    def by_patch(values):
        values = values.reshape(heads, slices, in_group, tok_dev, head_dim).swapaxes(1, 2)
        return values.reshape(heads, rows, head_dim).astype(jnp.bfloat16)

    def query_patch(shape):
        return lax.broadcasted_iota(jnp.int32, shape, 0) // tok_dev % in_group

    fresh_shape, old_shape = (rows, rows), (rows, groups * rows)
    fresh_patch = lax.broadcasted_iota(jnp.int32, fresh_shape, 1) // group_rows
    old_patch = lax.broadcasted_iota(jnp.int32, old_shape, 1) // group_rows - group * in_group
    masks = [
        (fresh_patch <= query_patch(fresh_shape)).astype(jnp.float32),
        jnp.logical_or(old_patch < 0, old_patch > query_patch(old_shape)).astype(jnp.float32),
    ]
    for ref in stale_refs:
        at = lax.broadcasted_iota(jnp.int32, (rows, ref.shape[1]), 1)
        masks.append((at // (groups * rows) != own_member).astype(jnp.float32))
    mask = jnp.concatenate(masks, axis=1)

    queries = head_norm(stacked(0), gain_ref[0:1, :]).astype(jnp.bfloat16)
    fresh = (by_patch(head_norm(stacked(1), gain_ref[1:2, :])), by_patch(stacked(2)))

    def entries(head, kind):
        at = slice(head * head_dim, (head + 1) * head_dim)
        old = old_table_ref[kind, :, :, at].reshape(groups * rows, head_dim)
        return jnp.concatenate([fresh[kind][head], old] + [ref[kind, :, at] for ref in stale_refs])

    scores = [
        lax.dot_general(
            queries[head],
            entries(head, 0),
            (((1,), (1,)), ((), ())),
            preferred_element_type=jnp.float32,
        )
        for head in range(heads)
    ]
    weights = mask[None] * jnp.exp(jnp.stack(scores) * (1.0 / math.sqrt(head_dim)))
    inverse = 1.0 / jnp.sum(weights, axis=-1, keepdims=True)
    weights = weights.astype(jnp.bfloat16)
    summed = [
        jnp.dot(weights[head], entries(head, 1), preferred_element_type=jnp.float32)
        for head in range(heads)
    ]
    attended = (jnp.stack(summed) * inverse).astype(jnp.bfloat16)
    attended = jnp.concatenate([attended[head] for head in range(heads)], axis=1)

    projected = jnp.dot(attended, out_ref[...], preferred_element_type=jnp.float32)
    projected = mod_ref[2] * projected
    if closing:
        close_into(partial_ref, projected, rows_ref, section, own_slice, in_group)
    else:
        out_cols = partial_ref.shape[3]
        for q in range(partial_ref.shape[0]):
            piece = projected[:, q * out_cols : (q + 1) * out_cols].astype(jnp.bfloat16)
            partial_ref[q] = piece.reshape(slices, block_rows, out_cols)

    for at in range(groups):

        @pl.when(group == at)
        def _():
            for j in range(2):
                table_ref[j, at] = jnp.concatenate([fresh[j][head] for head in range(heads)], axis=1)

        @pl.when(group != at)
        def _():
            for j in range(2):
                table_ref[j, at] = old_table_ref[j, at]


def close_into(closing_ref, projected, rows_ref, section, own_slice, in_group):
    branches, patches, slices = closing_ref.shape[:3]
    blocks, _, block_rows, block_cols = rows_ref.shape
    tok_dev = block_rows // in_group
    per_branch = blocks // branches

    @pl.when(section >= patches)
    def _():
        for piece in range(slices):
            own = (own_slice == piece).astype(jnp.float32)
            by_block = []
            for q in range(blocks):
                rows = projected[
                    piece * block_rows : (piece + 1) * block_rows,
                    q * block_cols : (q + 1) * block_cols,
                ]
                rows = rows + own * rows_ref[q, piece].astype(jnp.float32)
                by_block.append(rows.reshape(in_group, tok_dev, block_cols))
            for branch in range(branches):
                for patch in range(patches):
                    held = [by_block[branch * per_branch + k][patch] for k in range(per_branch)]
                    closing_ref[branch, patch, piece] = jnp.concatenate(held).astype(jnp.bfloat16)

    @pl.when(section < patches)
    def _():
        finished = [rows_ref[q, own_slice].astype(jnp.float32)[:tok_dev] for q in range(blocks)]
        for branch in range(branches):
            held = jnp.concatenate(finished[branch * per_branch : (branch + 1) * per_branch])
            held = held.astype(jnp.bfloat16)
            for patch in range(patches):
                for piece in range(slices):
                    closing_ref[branch, patch, piece] = held


def start_kernel(where_ref, latent_ref, qkv_ref, out_ref, *refs):
    del qkv_ref, out_ref
    loads = (len(refs) - 4) // 2
    from_refs, to_refs = refs[:loads], refs[loads : 2 * loads]
    sources_to, streams_to, spread_to, sems = refs[2 * loads :]
    sections, _, block_cols = streams_to.shape
    own_cols = pl.ds(pl.multiple_of(where_ref[0] * block_cols, block_cols), block_cols)
    pairs = [(latent_ref.at[0], spread_to.at[piece]) for piece in range(spread_to.shape[0])]
    pairs.append((latent_ref.at[:, :, own_cols], sources_to))
    pairs.extend(zip(from_refs, to_refs))
    copies = [
        pltpu.make_async_copy(from_ref, to_ref, sems.at[at])
        for at, (from_ref, to_ref) in enumerate(pairs)
    ]
    for copy in copies:
        copy.start()
    for section in range(1, sections):
        streams_to[section] = jnp.zeros(streams_to.shape[1:], streams_to.dtype)
    for copy in copies:
        copy.wait()
    streams_to[0] = sources_to[0]


def added(parts_ref, streams_ref, section):
    total = streams_ref[section].astype(jnp.float32)
    for piece in range(parts_ref.shape[1]):
        total = total + parts_ref[section, piece].astype(jnp.float32)
    return total


def settle_kernel(entering, parts_ref, streams_ref, sources_ref, streams_to, spread_to):
    count, slices = parts_ref.shape[:2]
    for section in range(count):
        if section == 0:
            held = sources_ref[entering]
        else:
            held = added(parts_ref, streams_ref, section - 1).astype(jnp.bfloat16)
        streams_to[section] = held
        for piece in range(slices):
            spread_to[section, piece] = held


def settle_last_kernel(in_group, parts_ref, streams_ref, spread_to):
    count, slices = parts_ref.shape[:2]
    finished = added(parts_ref, streams_ref, count - 1)
    tok_dev = finished.shape[0] // in_group
    last = added(parts_ref, streams_ref, count - 2).astype(jnp.bfloat16)
    for section in range(count):
        held = last
        if section < in_group:
            held = finished[section * tok_dev : (section + 1) * tok_dev]
            held = jnp.concatenate([held] * in_group).astype(jnp.bfloat16)
        for piece in range(slices):
            spread_to[section, piece] = held


def guide_kernel(where_ref, closing_ref, table_ref, guided_ref, table_to, sem):
    copy = pltpu.make_async_copy(table_ref, table_to, sem)
    copy.start()
    branches, patches, slices, block_rows, block_cols = closing_ref.shape
    tok_dev = guided_ref.shape[0]
    section, own_slice = where_ref[0], where_ref[2]

    def combine(pair):
        conditional, unconditional = pair
        rows = unconditional + GUIDANCE_SCALE * (conditional - unconditional)
        for at in range(block_rows // tok_dev):
            guided_ref[:, at * block_cols : (at + 1) * block_cols] = rows[
                at * tok_dev : (at + 1) * tok_dev
            ].astype(jnp.bfloat16)

    @pl.when(section >= patches)
    def _():
        pair = []
        for branch in range(branches):
            total = 0.0
            for piece in range(slices):
                total = total + closing_ref[branch, patches - 1, piece].astype(jnp.float32)
            pair.append(total.astype(jnp.bfloat16).astype(jnp.float32))
        combine(pair)

    @pl.when(section < patches)
    def _():
        combine(
            [closing_ref[branch, section, own_slice].astype(jnp.float32) for branch in range(branches)]
        )

    copy.wait()


def local(latent, modulation, qkv_weight, out_weight, norm_gain, stale_kv):
    seq_count = lax.axis_size("seq")
    seq_rank = lax.axis_index("seq")
    section_count = lax.axis_size("pipe")
    section_rank = lax.axis_index("pipe")
    patches, tok_dev, model_width = latent.shape
    head_dim = norm_gain.shape[2]
    slice_count = min(seq_count, 8)
    member_count = seq_count // slice_count
    member_bits = member_count.bit_length() - 1
    own_member = seq_rank % member_count
    local_width = stale_kv.shape[7]
    group_rows = slice_count * tok_dev
    own_cache = stale_kv[0, 0].reshape(2, patches, group_rows, local_width)
    group_cache = own_cache[None]
    qkv_slice = qkv_weight[0]
    out_slice = out_weight[0]
    for level_index in range(member_bits):
        got_qkv, got_out, got_cache = (
            swapped(qkv_slice, "seq", level_index),
            swapped(out_slice, "seq", level_index),
            swapped(group_cache, "seq", level_index),
        )
        is_upper = own_member >> level_index & 1 == 1
        qkv_slice = join_pair(is_upper, qkv_slice, got_qkv, 1)
        out_slice = join_pair(is_upper, out_slice, got_out, 0)
        group_cache = join_pair(is_upper, group_cache, got_cache, 0)
    homes = section_count * slice_count
    in_group = patches // GROUPS
    block_rows = in_group * tok_dev
    block_cols = model_width // section_count
    rows = slice_count * block_rows
    half = section_count // 2
    groups_of = range(member_count)
    in_slices = [[a + member_count * b for b in range(slice_count)] for a in groups_of]
    peers = [[q * seq_count + at for q in range(section_count) for at in g] for g in in_slices]
    closing_peers = [
        [
            (c * section_count + q) * seq_count + at
            for c in range(2)
            for q in range(h * half, (h + 1) * half)
            for at in g
        ]
        for h in range(2)
        for g in in_slices
    ]

    def exchange(value):
        value = value.reshape(homes, block_rows, block_cols)
        value = lax.all_to_all(value, ("pipe", "seq"), 0, 0, axis_index_groups=peers)
        return value.reshape(section_count, slice_count, block_rows, block_cols)

    vmem = pl.BlockSpec(memory_space=pltpu.VMEM)
    smem = pl.BlockSpec(memory_space=pltpu.SMEM)
    hbm = pl.BlockSpec(memory_space=pltpu.HBM)
    in_hbm = functools.partial(pltpu.with_memory_space_constraint, memory_space=pltpu.HBM)
    in_vmem = functools.partial(pltpu.with_memory_space_constraint, memory_space=pltpu.VMEM)
    where = jnp.stack((section_rank, own_member, seq_rank // member_count)).astype(jnp.int32)
    sources = latent.reshape(GROUPS, block_rows, model_width)
    stream_shape = (section_count, block_rows, block_cols)
    spread_shape = (section_count, slice_count, block_rows, block_cols)
    loads = (
        modulation.reshape(3, 1, model_width),
        norm_gain[0],
        own_cache.reshape(2, GROUPS, rows, local_width),
    )
    modulation, norm_gain, table, sources, streams, spread = pl.pallas_call(
        start_kernel,
        out_shape=tuple(pltpu.VMEM(value.shape, value.dtype) for value in loads)
        + (
            pltpu.VMEM((GROUPS, block_rows, block_cols), jnp.bfloat16),
            jax.ShapeDtypeStruct(stream_shape, jnp.bfloat16),
            jax.ShapeDtypeStruct((slice_count, block_rows, model_width), jnp.bfloat16),
        ),
        in_specs=[smem] + [hbm] * (len(loads) + 3),
        out_specs=(vmem,) * (len(loads) + 3),
        scratch_shapes=[pltpu.SemaphoreType.DMA((len(loads) + slice_count + 1,))],
        compiler_params=pltpu.CompilerParams(vmem_limit_bytes=4 * 1024 * 1024),
    )(where, in_hbm(sources), in_hbm(qkv_slice), in_hbm(out_slice), *map(in_hbm, loads))
    stale_rows = []
    if member_count > 1:
        stale_rows = [group_cache.swapaxes(0, 1).reshape(2, -1, local_width)]

    def attend(tick, features, table, partial_shape):
        operands = (
            where,
            features,
            in_vmem(modulation),
            in_vmem(qkv_slice),
            in_vmem(out_slice),
            in_vmem(norm_gain),
            *stale_rows,
            table,
        )
        return pl.pallas_call(
            functools.partial(section_kernel, tick, (tok_dev, head_dim)),
            out_shape=(
                jax.ShapeDtypeStruct(partial_shape, jnp.bfloat16),
                jax.ShapeDtypeStruct(table.shape, jnp.bfloat16),
            ),
            in_specs=[smem] + [vmem] * (len(operands) - 1),
            out_specs=(vmem, vmem),
            input_output_aliases={len(operands) - 1: 1},
            compiler_params=pltpu.CompilerParams(vmem_limit_bytes=24 * 1024 * 1024),
        )(*operands)

    def small(kernel, in_specs, *out_shapes):
        return pl.pallas_call(
            kernel,
            out_shape=tuple(jax.ShapeDtypeStruct(shape, jnp.bfloat16) for shape in out_shapes),
            in_specs=in_specs,
            out_specs=(vmem,) * len(out_shapes),
            compiler_params=pltpu.CompilerParams(vmem_limit_bytes=8 * 1024 * 1024),
        )

    ticks = GROUPS + section_count - 1
    closing_shape = (2, half, slice_count, block_rows, block_cols)
    features = lax.all_to_all(spread, "seq", 0, 0, axis_index_groups=in_slices)[None]
    for tick in range(ticks - 1):
        partial_out, table = attend(tick, features, table, spread_shape)
        parts = exchange(partial_out)
        if tick < ticks - 2:
            streams, spread = small(
                functools.partial(settle_kernel, min(tick + 1, GROUPS - 1)),
                [vmem] * 3,
                stream_shape,
                spread_shape,
            )(parts, streams, in_vmem(sources))
        else:
            (spread,) = small(
                functools.partial(settle_last_kernel, in_group), [vmem] * 2, spread_shape
            )(parts, streams)
        features = exchange(spread)
    closing, table = attend(ticks - 1, features, table, closing_shape)
    closing = lax.all_to_all(
        closing.reshape((-1,) + closing_shape[3:]),
        ("cfg", "pipe", "seq"),
        0,
        0,
        axis_index_groups=closing_peers,
    ).reshape(closing_shape)
    guided, table = pl.pallas_call(
        guide_kernel,
        out_shape=(
            jax.ShapeDtypeStruct((tok_dev, model_width // 2), jnp.bfloat16),
            jax.ShapeDtypeStruct(table.shape, jnp.bfloat16),
        ),
        in_specs=[smem, vmem, vmem],
        out_specs=(vmem, hbm),
        scratch_shapes=[pltpu.SemaphoreType.DMA],
        compiler_params=pltpu.CompilerParams(vmem_limit_bytes=8 * 1024 * 1024),
    )(where, closing, table)
    return (guided[None], table.reshape(stale_kv.shape))


def solution(mesh):
    placed = (
        P(None, "seq", None),
        P("pipe", "cfg", None, None),
        P("pipe", None, "seq"),
        P("pipe", "seq", None),
        P("pipe", None, None),
        P("pipe", "cfg", None, None, "seq", None, None, None),
    )
    return jax.shard_map(
        local,
        mesh=mesh,
        in_specs=placed,
        out_specs=(P("pipe", "seq", "cfg"), P("pipe", "cfg", None, None, "seq", None, None, None)),
        check_vma=False,
    )
```

```python
import functools
import math

import jax
import jax.numpy as jnp
from jax import lax
from jax.experimental import pallas as pl
from jax.experimental.pallas import tpu as pltpu
from jax.sharding import PartitionSpec as P

GUIDANCE_SCALE = 6.0
EPSILON = 1e-06
GROUPS = 2


def swapped(value, axis, bit):
    return lax.ppermute(value, axis, [(i, i ^ 1 << bit) for i in range(lax.axis_size(axis))])


def head_norm(values, gain_row):
    return (
        values * lax.rsqrt(jnp.mean(values * values, axis=-1, keepdims=True) + EPSILON) * gain_row
    )


def join_pair(is_upper, mine, theirs, axis_dim):
    return jnp.where(
        is_upper,
        jnp.concatenate((theirs, mine), axis_dim),
        jnp.concatenate((mine, theirs), axis_dim),
    )


def section_kernel(tick, sizes, where_ref, rows_ref, mod_ref, qkv_ref, out_ref, gain_ref, *refs):
    *stale_refs, old_table_ref, partial_ref, table_ref = refs
    closing = len(partial_ref.shape) == 5
    folding = tick == 1
    tok_dev, head_dim = sizes
    blocks, slices, block_rows, block_cols = rows_ref.shape
    rows = slices * block_rows
    width = blocks * block_cols
    in_group = block_rows // tok_dev
    group_rows = slices * tok_dev
    groups, local_width = table_ref.shape[1], table_ref.shape[3]
    heads = local_width // head_dim
    section, own_member, own_slice = where_ref[0], where_ref[1], where_ref[2]
    group = tick - section
    parts = [rows_ref[q].reshape(rows, block_cols).astype(jnp.float32) for q in range(blocks)]
    mean = jnp.sum(sum(parts), axis=-1, keepdims=True) * (1.0 / width)
    parts = [x - mean for x in parts]
    spread = jnp.sum(sum(x * x for x in parts), axis=-1, keepdims=True) * (1.0 / width)
    inverse = lax.rsqrt(spread + EPSILON)
    modulated = []
    for q, x in enumerate(parts):
        at = slice(q * block_cols, (q + 1) * block_cols)
        modulated.append(
            (x * inverse * (1.0 + mod_ref[1, :, at]) + mod_ref[0, :, at]).astype(jnp.bfloat16)
        )
    modulated = jnp.concatenate(modulated, axis=1)
    mixed = jnp.dot(modulated, qkv_ref[...], preferred_element_type=jnp.float32)

    def stacked(kind):
        at = [(3 * head + kind) * head_dim for head in range(heads)]
        return jnp.stack([mixed[:, start : start + head_dim] for start in at])

    def by_patch(values):
        values = values.reshape(heads, slices, in_group, tok_dev, head_dim).swapaxes(1, 2)
        return values.reshape(heads, rows, head_dim).astype(jnp.bfloat16)

    def query_patch(shape):
        return lax.broadcasted_iota(jnp.int32, shape, 0) // tok_dev % in_group

    fresh_shape, old_shape = (rows, rows), (rows, groups * rows)
    fresh_patch = lax.broadcasted_iota(jnp.int32, fresh_shape, 1) // group_rows
    old_patch = lax.broadcasted_iota(jnp.int32, old_shape, 1) // group_rows - group * in_group
    masks = [
        (fresh_patch <= query_patch(fresh_shape)).astype(jnp.float32),
        jnp.logical_or(old_patch < 0, old_patch > query_patch(old_shape)).astype(jnp.float32),
    ]
    for ref in stale_refs:
        at = lax.broadcasted_iota(jnp.int32, (rows, ref.shape[1]), 1)
        masks.append((at // (groups * rows) != own_member).astype(jnp.float32))
    mask = jnp.concatenate(masks, axis=1)

    queries = head_norm(stacked(0), gain_ref[0:1, :]).astype(jnp.bfloat16)
    fresh = (by_patch(head_norm(stacked(1), gain_ref[1:2, :])), by_patch(stacked(2)))

    def entries(head, kind):
        at = slice(head * head_dim, (head + 1) * head_dim)
        old = old_table_ref[kind, :, :, at].reshape(groups * rows, head_dim)
        return jnp.concatenate([fresh[kind][head], old] + [ref[kind, :, at] for ref in stale_refs])

    scores = [
        lax.dot_general(
            queries[head],
            entries(head, 0),
            (((1,), (1,)), ((), ())),
            preferred_element_type=jnp.float32,
        )
        for head in range(heads)
    ]
    weights = mask[None] * jnp.exp(jnp.stack(scores) * (1.0 / math.sqrt(head_dim)))
    inverse = 1.0 / jnp.sum(weights, axis=-1, keepdims=True)
    weights = weights.astype(jnp.bfloat16)
    summed = [
        jnp.dot(weights[head], entries(head, 1), preferred_element_type=jnp.float32)
        for head in range(heads)
    ]
    attended = (jnp.stack(summed) * inverse).astype(jnp.bfloat16)
    attended = jnp.concatenate([attended[head] for head in range(heads)], axis=1)

    projected = jnp.dot(attended, out_ref[...], preferred_element_type=jnp.float32)
    projected = mod_ref[2] * projected
    if folding:
        at_slice = lax.broadcasted_iota(jnp.int32, (rows, 1), 0) // block_rows
        own = (at_slice == own_slice).astype(jnp.float32)
        projected = projected + own * jnp.concatenate(
            [rows_ref[q].reshape(rows, block_cols).astype(jnp.float32) for q in range(blocks)],
            axis=1,
        )
    if closing:
        close_into(partial_ref, projected, rows_ref, section, own_slice, in_group)
    else:
        out_cols = partial_ref.shape[3]
        for q in range(partial_ref.shape[0]):
            piece = projected[:, q * out_cols : (q + 1) * out_cols].astype(jnp.bfloat16)
            partial_ref[q] = piece.reshape(slices, block_rows, out_cols)

    for at in range(groups):

        @pl.when(group == at)
        def _():
            for j in range(2):
                table_ref[j, at] = jnp.concatenate([fresh[j][head] for head in range(heads)], axis=1)

        @pl.when(group != at)
        def _():
            for j in range(2):
                table_ref[j, at] = old_table_ref[j, at]


def close_into(closing_ref, projected, rows_ref, section, own_slice, in_group):
    branches, patches, slices = closing_ref.shape[:3]
    blocks, _, block_rows, block_cols = rows_ref.shape
    tok_dev = block_rows // in_group
    per_branch = blocks // branches

    @pl.when(section >= patches)
    def _():
        for piece in range(slices):
            own = (own_slice == piece).astype(jnp.float32)
            by_block = []
            for q in range(blocks):
                rows = projected[
                    piece * block_rows : (piece + 1) * block_rows,
                    q * block_cols : (q + 1) * block_cols,
                ]
                rows = rows + own * rows_ref[q, piece].astype(jnp.float32)
                by_block.append(rows.reshape(in_group, tok_dev, block_cols))
            for branch in range(branches):
                for patch in range(patches):
                    held = [by_block[branch * per_branch + k][patch] for k in range(per_branch)]
                    closing_ref[branch, patch, piece] = jnp.concatenate(held).astype(jnp.bfloat16)

    @pl.when(section < patches)
    def _():
        finished = [rows_ref[q, own_slice].astype(jnp.float32)[:tok_dev] for q in range(blocks)]
        for branch in range(branches):
            held = jnp.concatenate(finished[branch * per_branch : (branch + 1) * per_branch])
            held = held.astype(jnp.bfloat16)
            for patch in range(patches):
                for piece in range(slices):
                    closing_ref[branch, patch, piece] = held


def start_kernel(where_ref, latent_ref, qkv_ref, out_ref, *refs):
    del qkv_ref, out_ref
    loads = (len(refs) - 3) // 2
    from_refs, to_refs = refs[:loads], refs[loads : 2 * loads]
    sources_to, spread_to, sems = refs[2 * loads :]
    half_cols = sources_to.shape[2]
    own_cols = pl.ds(pl.multiple_of(where_ref[0] % 2 * half_cols, half_cols), half_cols)
    pairs = [(latent_ref.at[0], spread_to.at[piece]) for piece in range(spread_to.shape[0])]
    pairs.append((latent_ref.at[:, :, own_cols], sources_to))
    pairs.extend(zip(from_refs, to_refs))
    copies = [
        pltpu.make_async_copy(from_ref, to_ref, sems.at[at])
        for at, (from_ref, to_ref) in enumerate(pairs)
    ]
    for copy in copies:
        copy.start()
    for copy in copies:
        copy.wait()


def added(parts_ref, section, *streams_refs):
    total = sum(parts_ref[section, piece].astype(jnp.float32) for piece in range(parts_ref.shape[1]))
    for ref in streams_refs:
        total = total + ref[section].astype(jnp.float32)
    return total


def settle_first_kernel(parts_ref, sources_ref, spread_to):
    first = added(parts_ref, 0, sources_ref).astype(jnp.bfloat16)
    for piece in range(parts_ref.shape[1]):
        spread_to[0, piece] = sources_ref[1]
        spread_to[1, piece] = first


def settle_kernel(parts_ref, *refs):
    *streams_refs, streams_to, spread_to = refs
    count, slices = parts_ref.shape[:2]
    for section in range(count):
        held = added(parts_ref, max(section - 1, 0), *streams_refs).astype(jnp.bfloat16)
        streams_to[section] = held
        for piece in range(slices):
            spread_to[section, piece] = held


def settle_last_kernel(in_group, parts_ref, streams_ref, spread_to):
    count, slices = parts_ref.shape[:2]
    finished = added(parts_ref, count - 1, streams_ref)
    tok_dev = finished.shape[0] // in_group
    last = added(parts_ref, count - 2, streams_ref).astype(jnp.bfloat16)
    for section in range(count):
        held = last
        if section < in_group:
            held = finished[section * tok_dev : (section + 1) * tok_dev]
            held = jnp.concatenate([held] * in_group).astype(jnp.bfloat16)
        for piece in range(slices):
            spread_to[section, piece] = held


def guide_kernel(where_ref, closing_ref, table_ref, guided_ref, table_to, sem):
    copy = pltpu.make_async_copy(table_ref, table_to, sem)
    copy.start()
    branches, patches, slices, block_rows, block_cols = closing_ref.shape
    tok_dev = guided_ref.shape[0]
    section, own_slice = where_ref[0], where_ref[2]

    def combine(pair):
        conditional, unconditional = pair
        rows = unconditional + GUIDANCE_SCALE * (conditional - unconditional)
        for at in range(block_rows // tok_dev):
            guided_ref[:, at * block_cols : (at + 1) * block_cols] = rows[
                at * tok_dev : (at + 1) * tok_dev
            ].astype(jnp.bfloat16)

    @pl.when(section >= patches)
    def _():
        pair = []
        for branch in range(branches):
            total = 0.0
            for piece in range(slices):
                total = total + closing_ref[branch, patches - 1, piece].astype(jnp.float32)
            pair.append(total.astype(jnp.bfloat16).astype(jnp.float32))
        combine(pair)

    @pl.when(section < patches)
    def _():
        combine(
            [closing_ref[branch, section, own_slice].astype(jnp.float32) for branch in range(branches)]
        )

    copy.wait()


def local(latent, modulation, qkv_weight, out_weight, norm_gain, stale_kv):
    seq_count = lax.axis_size("seq")
    seq_rank = lax.axis_index("seq")
    section_count = lax.axis_size("pipe")
    section_rank = lax.axis_index("pipe")
    patches, tok_dev, model_width = latent.shape
    head_dim = norm_gain.shape[2]
    slice_count = min(seq_count, 8)
    member_count = seq_count // slice_count
    member_bits = member_count.bit_length() - 1
    own_member = seq_rank % member_count
    local_width = stale_kv.shape[7]
    group_rows = slice_count * tok_dev
    own_cache = stale_kv[0, 0].reshape(2, patches, group_rows, local_width)
    group_cache = own_cache[None]
    qkv_slice = qkv_weight[0]
    out_slice = out_weight[0]
    for level_index in range(member_bits):
        got_qkv, got_out, got_cache = (
            swapped(qkv_slice, "seq", level_index),
            swapped(out_slice, "seq", level_index),
            swapped(group_cache, "seq", level_index),
        )
        is_upper = own_member >> level_index & 1 == 1
        qkv_slice = join_pair(is_upper, qkv_slice, got_qkv, 1)
        out_slice = join_pair(is_upper, out_slice, got_out, 0)
        group_cache = join_pair(is_upper, group_cache, got_cache, 0)
    homes = section_count * slice_count
    in_group = patches // GROUPS
    block_rows = in_group * tok_dev
    block_cols = model_width // section_count
    rows = slice_count * block_rows
    half = section_count // 2
    groups_of = range(member_count)
    in_slices = [[a + member_count * b for b in range(slice_count)] for a in groups_of]
    peers = [[q * seq_count + at for q in range(section_count) for at in g] for g in in_slices]
    closing_peers = [
        [
            (c * section_count + q) * seq_count + at
            for c in range(2)
            for q in range(h * half, (h + 1) * half)
            for at in g
        ]
        for h in range(2)
        for g in in_slices
    ]

    pair_peers = [
        [q * seq_count + at for q in range(first, first + 2) for at in g]
        for first in range(0, section_count, 2)
        for g in in_slices
    ]

    def exchange(value, among=peers):
        flat = value.reshape((-1,) + value.shape[2:])
        flat = lax.all_to_all(flat, ("pipe", "seq"), 0, 0, axis_index_groups=among)
        return flat.reshape(value.shape)

    vmem = pl.BlockSpec(memory_space=pltpu.VMEM)
    smem = pl.BlockSpec(memory_space=pltpu.SMEM)
    hbm = pl.BlockSpec(memory_space=pltpu.HBM)
    in_hbm = functools.partial(pltpu.with_memory_space_constraint, memory_space=pltpu.HBM)
    in_vmem = functools.partial(pltpu.with_memory_space_constraint, memory_space=pltpu.VMEM)
    where = jnp.stack((section_rank, own_member, seq_rank // member_count)).astype(jnp.int32)
    sources = latent.reshape(GROUPS, block_rows, model_width)
    stream_shape = (section_count, block_rows, block_cols)
    spread_shape = (section_count, slice_count, block_rows, block_cols)
    loads = (
        modulation.reshape(3, 1, model_width),
        norm_gain[0],
        own_cache.reshape(2, GROUPS, rows, local_width),
    )
    modulation, norm_gain, table, sources, spread = pl.pallas_call(
        start_kernel,
        out_shape=tuple(pltpu.VMEM(value.shape, value.dtype) for value in loads)
        + (
            pltpu.VMEM((GROUPS, block_rows, model_width // 2), jnp.bfloat16),
            jax.ShapeDtypeStruct((slice_count, block_rows, model_width), jnp.bfloat16),
        ),
        in_specs=[smem] + [hbm] * (len(loads) + 3),
        out_specs=(vmem,) * (len(loads) + 2),
        scratch_shapes=[pltpu.SemaphoreType.DMA((len(loads) + slice_count + 1,))],
        compiler_params=pltpu.CompilerParams(vmem_limit_bytes=4 * 1024 * 1024),
    )(where, in_hbm(sources), in_hbm(qkv_slice), in_hbm(out_slice), *map(in_hbm, loads))
    stale_rows = []
    if member_count > 1:
        stale_rows = [group_cache.swapaxes(0, 1).reshape(2, -1, local_width)]

    def attend(tick, features, table, partial_shape):
        operands = (
            where,
            features,
            in_vmem(modulation),
            in_vmem(qkv_slice),
            in_vmem(out_slice),
            in_vmem(norm_gain),
            *stale_rows,
            table,
        )
        return pl.pallas_call(
            functools.partial(section_kernel, tick, (tok_dev, head_dim)),
            out_shape=(
                jax.ShapeDtypeStruct(partial_shape, jnp.bfloat16),
                jax.ShapeDtypeStruct(table.shape, jnp.bfloat16),
            ),
            in_specs=[smem] + [vmem] * (len(operands) - 1),
            out_specs=(vmem, vmem),
            input_output_aliases={len(operands) - 1: 1},
            compiler_params=pltpu.CompilerParams(vmem_limit_bytes=24 * 1024 * 1024),
        )(*operands)

    def small(kernel, in_specs, *out_shapes):
        return pl.pallas_call(
            kernel,
            out_shape=tuple(jax.ShapeDtypeStruct(shape, jnp.bfloat16) for shape in out_shapes),
            in_specs=in_specs,
            out_specs=(vmem,) * len(out_shapes),
            compiler_params=pltpu.CompilerParams(vmem_limit_bytes=8 * 1024 * 1024),
        )

    ticks = GROUPS + section_count - 1
    closing_shape = (2, half, slice_count, block_rows, block_cols)
    features = lax.all_to_all(spread, "seq", 0, 0, axis_index_groups=in_slices)[None]
    pair_shape = (2, slice_count, block_rows, model_width // 2)
    partial_out, table = attend(0, features, table, pair_shape)
    parts = exchange(partial_out, pair_peers)
    (spread,) = small(settle_first_kernel, [vmem] * 2, pair_shape)(parts, in_vmem(sources))
    features = exchange(spread, pair_peers)
    streams = []
    for tick in range(1, ticks - 2):
        partial_out, table = attend(tick, features, table, spread_shape)
        held = [exchange(partial_out)] + streams
        stream, spread = small(settle_kernel, [vmem] * len(held), stream_shape, spread_shape)(*held)
        streams = [stream]
        features = exchange(spread)
    partial_out, table = attend(ticks - 2, features, table, spread_shape)
    (spread,) = small(
        functools.partial(settle_last_kernel, in_group), [vmem] * 2, spread_shape
    )(exchange(partial_out), *streams)
    features = exchange(spread)
    closing, table = attend(ticks - 1, features, table, closing_shape)
    closing = lax.all_to_all(
        closing.reshape((-1,) + closing_shape[3:]),
        ("cfg", "pipe", "seq"),
        0,
        0,
        axis_index_groups=closing_peers,
    ).reshape(closing_shape)
    guided, table = pl.pallas_call(
        guide_kernel,
        out_shape=(
            jax.ShapeDtypeStruct((tok_dev, model_width // 2), jnp.bfloat16),
            jax.ShapeDtypeStruct(table.shape, jnp.bfloat16),
        ),
        in_specs=[smem, vmem, vmem],
        out_specs=(vmem, hbm),
        scratch_shapes=[pltpu.SemaphoreType.DMA],
        compiler_params=pltpu.CompilerParams(vmem_limit_bytes=8 * 1024 * 1024),
    )(where, closing, table)
    return (guided[None], table.reshape(stale_kv.shape))


def solution(mesh):
    placed = (
        P(None, "seq", None),
        P("pipe", "cfg", None, None),
        P("pipe", None, "seq"),
        P("pipe", "seq", None),
        P("pipe", None, None),
        P("pipe", "cfg", None, None, "seq", None, None, None),
    )
    return jax.shard_map(
        local,
        mesh=mesh,
        in_specs=placed,
        out_specs=(P("pipe", "seq", "cfg"), P("pipe", "cfg", None, None, "seq", None, None, None)),
        check_vma=False,
    )
```

```python
import functools
import math

import jax
import jax.numpy as jnp
from jax import lax
from jax.experimental import pallas as pl
from jax.experimental.pallas import tpu as pltpu
from jax.sharding import PartitionSpec as P

GUIDANCE_SCALE = 6.0
EPSILON = 1e-06
GROUPS = 2


def swapped(value, axis, bit):
    return lax.ppermute(value, axis, [(i, i ^ 1 << bit) for i in range(lax.axis_size(axis))])


def head_norm(values, gain_row):
    return (
        values * lax.rsqrt(jnp.mean(values * values, axis=-1, keepdims=True) + EPSILON) * gain_row
    )


def join_pair(is_upper, mine, theirs, axis_dim):
    return jnp.where(
        is_upper,
        jnp.concatenate((theirs, mine), axis_dim),
        jnp.concatenate((mine, theirs), axis_dim),
    )


def section_kernel(tick, sizes, where_ref, rows_ref, mod_ref, qkv_ref, out_ref, gain_ref, *refs):
    *stale_refs, old_table_ref, partial_ref, table_ref = refs
    closing = len(partial_ref.shape) == 5
    folding = tick == 1
    tok_dev, head_dim = sizes
    blocks, slices, block_rows, block_cols = rows_ref.shape
    rows = slices * block_rows
    width = blocks * block_cols
    in_group = block_rows // tok_dev
    group_rows = slices * tok_dev
    groups, local_width = table_ref.shape[1], table_ref.shape[3]
    heads = local_width // head_dim
    section, own_member, own_slice = where_ref[0], where_ref[1], where_ref[2]
    group = tick - section
    parts = [rows_ref[q].reshape(rows, block_cols).astype(jnp.float32) for q in range(blocks)]
    mean = jnp.sum(sum(parts), axis=-1, keepdims=True) * (1.0 / width)
    parts = [x - mean for x in parts]
    spread = jnp.sum(sum(x * x for x in parts), axis=-1, keepdims=True) * (1.0 / width)
    inverse = lax.rsqrt(spread + EPSILON)
    modulated = []
    for q, x in enumerate(parts):
        at = slice(q * block_cols, (q + 1) * block_cols)
        modulated.append(
            (x * inverse * (1.0 + mod_ref[1, :, at]) + mod_ref[0, :, at]).astype(jnp.bfloat16)
        )
    modulated = jnp.concatenate(modulated, axis=1)
    mixed = jnp.dot(modulated, qkv_ref[...], preferred_element_type=jnp.float32)

    def stacked(kind):
        at = [(3 * head + kind) * head_dim for head in range(heads)]
        return jnp.stack([mixed[:, start : start + head_dim] for start in at])

    def by_patch(values):
        values = values.reshape(heads, slices, in_group, tok_dev, head_dim).swapaxes(1, 2)
        return values.reshape(heads, rows, head_dim).astype(jnp.bfloat16)

    def query_patch(shape):
        return lax.broadcasted_iota(jnp.int32, shape, 0) // tok_dev % in_group

    fresh_shape, old_shape = (rows, rows), (rows, groups * rows)
    fresh_patch = lax.broadcasted_iota(jnp.int32, fresh_shape, 1) // group_rows
    old_patch = lax.broadcasted_iota(jnp.int32, old_shape, 1) // group_rows - group * in_group
    masks = [
        (fresh_patch <= query_patch(fresh_shape)).astype(jnp.float32),
        jnp.logical_or(old_patch < 0, old_patch > query_patch(old_shape)).astype(jnp.float32),
    ]
    for ref in stale_refs:
        at = lax.broadcasted_iota(jnp.int32, (rows, ref.shape[1]), 1)
        masks.append((at // (groups * rows) != own_member).astype(jnp.float32))
    mask = jnp.concatenate(masks, axis=1)

    queries = head_norm(stacked(0), gain_ref[0:1, :]).astype(jnp.bfloat16)
    fresh = (by_patch(head_norm(stacked(1), gain_ref[1:2, :])), by_patch(stacked(2)))

    def entries(head, kind):
        at = slice(head * head_dim, (head + 1) * head_dim)
        old = old_table_ref[kind, :, :, at].reshape(groups * rows, head_dim)
        return jnp.concatenate([fresh[kind][head], old] + [ref[kind, :, at] for ref in stale_refs])

    scores = [
        lax.dot_general(
            queries[head],
            entries(head, 0),
            (((1,), (1,)), ((), ())),
            preferred_element_type=jnp.float32,
        )
        for head in range(heads)
    ]
    weights = mask[None] * jnp.exp(jnp.stack(scores) * (1.0 / math.sqrt(head_dim)))
    inverse = 1.0 / jnp.sum(weights, axis=-1, keepdims=True)
    weights = weights.astype(jnp.bfloat16)
    summed = [
        jnp.dot(weights[head], entries(head, 1), preferred_element_type=jnp.float32)
        for head in range(heads)
    ]
    attended = (jnp.stack(summed) * inverse).astype(jnp.bfloat16)
    attended = jnp.concatenate([attended[head] for head in range(heads)], axis=1)

    projected = jnp.dot(attended, out_ref[...], preferred_element_type=jnp.float32)
    projected = mod_ref[2] * projected
    if folding:
        at_slice = lax.broadcasted_iota(jnp.int32, (rows, 1), 0) // block_rows
        own = (at_slice == own_slice).astype(jnp.float32)
        projected = projected + own * jnp.concatenate(
            [rows_ref[q].reshape(rows, block_cols).astype(jnp.float32) for q in range(blocks)],
            axis=1,
        )
    if closing:
        close_into(partial_ref, projected, rows_ref, section, own_slice, in_group)
    else:
        out_cols = partial_ref.shape[3]
        for q in range(partial_ref.shape[0]):
            piece = projected[:, q * out_cols : (q + 1) * out_cols].astype(jnp.bfloat16)
            partial_ref[q] = piece.reshape(slices, block_rows, out_cols)

    for at in range(groups):

        @pl.when(group == at)
        def _():
            for j in range(2):
                table_ref[j, at] = jnp.concatenate([fresh[j][head] for head in range(heads)], axis=1)

        @pl.when(group != at)
        def _():
            for j in range(2):
                table_ref[j, at] = old_table_ref[j, at]


def close_into(closing_ref, projected, rows_ref, section, own_slice, in_group):
    branches, patches, slices = closing_ref.shape[:3]
    blocks, _, block_rows, block_cols = rows_ref.shape
    tok_dev = block_rows // in_group
    per_branch = blocks // branches

    @pl.when(section >= patches)
    def _():
        for piece in range(slices):
            own = (own_slice == piece).astype(jnp.float32)
            by_block = []
            for q in range(blocks):
                rows = projected[
                    piece * block_rows : (piece + 1) * block_rows,
                    q * block_cols : (q + 1) * block_cols,
                ]
                rows = rows + own * rows_ref[q, piece].astype(jnp.float32)
                by_block.append(rows.reshape(in_group, tok_dev, block_cols))
            for branch in range(branches):
                for patch in range(patches):
                    held = [by_block[branch * per_branch + k][patch] for k in range(per_branch)]
                    closing_ref[branch, patch, piece] = jnp.concatenate(held).astype(jnp.bfloat16)

    @pl.when(section < patches)
    def _():
        finished = [rows_ref[q, own_slice].astype(jnp.float32)[:tok_dev] for q in range(blocks)]
        for branch in range(branches):
            held = jnp.concatenate(finished[branch * per_branch : (branch + 1) * per_branch])
            held = held.astype(jnp.bfloat16)
            for patch in range(patches):
                for piece in range(slices):
                    closing_ref[branch, patch, piece] = held


def start_kernel(where_ref, latent_ref, *refs):
    del where_ref
    spread_to, sems = refs[-2:]
    copies = [
        pltpu.make_async_copy(latent_ref.at[0], spread_to.at[piece], sems.at[piece])
        for piece in range(spread_to.shape[0])
    ]
    for copy in copies:
        copy.start()
    for copy in copies:
        copy.wait()


def added(parts_ref, section, *streams_refs):
    total = sum(parts_ref[section, piece].astype(jnp.float32) for piece in range(parts_ref.shape[1]))
    for ref in streams_refs:
        total = total + ref[section].astype(jnp.float32)
    return total


def settle_first_kernel(where_ref, parts_ref, latent_ref, spread_to):
    first = added(parts_ref, 0)
    half_cols = first.shape[1]
    for half in range(2):

        @pl.when(where_ref[0] % 2 == half)
        def _():
            at = slice(half * half_cols, (half + 1) * half_cols)
            held = (first + latent_ref[0, :, at].astype(jnp.float32)).astype(jnp.bfloat16)
            for piece in range(parts_ref.shape[1]):
                spread_to[0, piece] = latent_ref[1, :, at]
                spread_to[1, piece] = held


def settle_kernel(parts_ref, *refs):
    *streams_refs, streams_to, spread_to = refs
    count, slices = parts_ref.shape[:2]
    for section in range(count):
        held = added(parts_ref, max(section - 1, 0), *streams_refs).astype(jnp.bfloat16)
        streams_to[section] = held
        for piece in range(slices):
            spread_to[section, piece] = held


def settle_last_kernel(in_group, parts_ref, streams_ref, spread_to):
    count, slices = parts_ref.shape[:2]
    finished = added(parts_ref, count - 1, streams_ref)
    tok_dev = finished.shape[0] // in_group
    last = added(parts_ref, count - 2, streams_ref).astype(jnp.bfloat16)
    for section in range(count):
        held = last
        if section < in_group:
            held = finished[section * tok_dev : (section + 1) * tok_dev]
            held = jnp.concatenate([held] * in_group).astype(jnp.bfloat16)
        for piece in range(slices):
            spread_to[section, piece] = held


def guide_kernel(where_ref, closing_ref, table_ref, guided_ref, table_to, sem):
    copy = pltpu.make_async_copy(table_ref, table_to, sem)
    copy.start()
    branches, patches, slices, block_rows, block_cols = closing_ref.shape
    tok_dev = guided_ref.shape[0]
    section, own_slice = where_ref[0], where_ref[2]

    def combine(pair):
        conditional, unconditional = pair
        rows = unconditional + GUIDANCE_SCALE * (conditional - unconditional)
        for at in range(block_rows // tok_dev):
            guided_ref[:, at * block_cols : (at + 1) * block_cols] = rows[
                at * tok_dev : (at + 1) * tok_dev
            ].astype(jnp.bfloat16)

    @pl.when(section >= patches)
    def _():
        pair = []
        for branch in range(branches):
            total = 0.0
            for piece in range(slices):
                total = total + closing_ref[branch, patches - 1, piece].astype(jnp.float32)
            pair.append(total.astype(jnp.bfloat16).astype(jnp.float32))
        combine(pair)

    @pl.when(section < patches)
    def _():
        combine(
            [closing_ref[branch, section, own_slice].astype(jnp.float32) for branch in range(branches)]
        )

    copy.wait()


def local(latent, modulation, qkv_weight, out_weight, norm_gain, stale_kv):
    seq_count = lax.axis_size("seq")
    seq_rank = lax.axis_index("seq")
    section_count = lax.axis_size("pipe")
    section_rank = lax.axis_index("pipe")
    patches, tok_dev, model_width = latent.shape
    head_dim = norm_gain.shape[2]
    slice_count = min(seq_count, 8)
    member_count = seq_count // slice_count
    member_bits = member_count.bit_length() - 1
    own_member = seq_rank % member_count
    local_width = stale_kv.shape[7]
    group_rows = slice_count * tok_dev
    own_cache = stale_kv[0, 0].reshape(2, patches, group_rows, local_width)
    group_cache = own_cache[None]
    qkv_slice = qkv_weight[0]
    out_slice = out_weight[0]
    for level_index in range(member_bits):
        got_qkv, got_out, got_cache = (
            swapped(qkv_slice, "seq", level_index),
            swapped(out_slice, "seq", level_index),
            swapped(group_cache, "seq", level_index),
        )
        is_upper = own_member >> level_index & 1 == 1
        qkv_slice = join_pair(is_upper, qkv_slice, got_qkv, 1)
        out_slice = join_pair(is_upper, out_slice, got_out, 0)
        group_cache = join_pair(is_upper, group_cache, got_cache, 0)
    homes = section_count * slice_count
    in_group = patches // GROUPS
    block_rows = in_group * tok_dev
    block_cols = model_width // section_count
    rows = slice_count * block_rows
    half = section_count // 2
    groups_of = range(member_count)
    in_slices = [[a + member_count * b for b in range(slice_count)] for a in groups_of]
    peers = [[q * seq_count + at for q in range(section_count) for at in g] for g in in_slices]
    closing_peers = [
        [
            (c * section_count + q) * seq_count + at
            for c in range(2)
            for q in range(h * half, (h + 1) * half)
            for at in g
        ]
        for h in range(2)
        for g in in_slices
    ]

    pair_peers = [
        [q * seq_count + at for q in range(first, first + 2) for at in g]
        for first in range(0, section_count, 2)
        for g in in_slices
    ]

    def exchange(value, among=peers):
        flat = value.reshape((-1,) + value.shape[2:])
        flat = lax.all_to_all(flat, ("pipe", "seq"), 0, 0, axis_index_groups=among)
        return flat.reshape(value.shape)

    vmem = pl.BlockSpec(memory_space=pltpu.VMEM)
    smem = pl.BlockSpec(memory_space=pltpu.SMEM)
    hbm = pl.BlockSpec(memory_space=pltpu.HBM)
    in_hbm = functools.partial(pltpu.with_memory_space_constraint, memory_space=pltpu.HBM)
    in_vmem = functools.partial(pltpu.with_memory_space_constraint, memory_space=pltpu.VMEM)
    where = jnp.stack((section_rank, own_member, seq_rank // member_count)).astype(jnp.int32)
    sources = latent.reshape(GROUPS, block_rows, model_width)
    stream_shape = (section_count, block_rows, block_cols)
    spread_shape = (section_count, slice_count, block_rows, block_cols)
    modulation = modulation.reshape(3, 1, model_width)
    norm_gain = norm_gain[0]
    table = own_cache.reshape(2, GROUPS, rows, local_width)
    named = (sources, qkv_slice, out_slice, modulation, norm_gain, table)
    spread = pl.pallas_call(
        start_kernel,
        out_shape=jax.ShapeDtypeStruct((slice_count, block_rows, model_width), jnp.bfloat16),
        in_specs=[smem] + [hbm] * len(named),
        out_specs=vmem,
        scratch_shapes=[pltpu.SemaphoreType.DMA((slice_count,))],
        compiler_params=pltpu.CompilerParams(vmem_limit_bytes=4 * 1024 * 1024),
    )(where, *map(in_hbm, named))
    stale_rows = []
    if member_count > 1:
        stale_rows = [group_cache.swapaxes(0, 1).reshape(2, -1, local_width)]

    def attend(tick, features, table, partial_shape):
        operands = (
            where,
            features,
            in_vmem(modulation),
            in_vmem(qkv_slice),
            in_vmem(out_slice),
            in_vmem(norm_gain),
            *stale_rows,
            in_vmem(table),
        )
        return pl.pallas_call(
            functools.partial(section_kernel, tick, (tok_dev, head_dim)),
            out_shape=(
                jax.ShapeDtypeStruct(partial_shape, jnp.bfloat16),
                jax.ShapeDtypeStruct(table.shape, jnp.bfloat16),
            ),
            in_specs=[smem] + [vmem] * (len(operands) - 1),
            out_specs=(vmem, vmem),
            compiler_params=pltpu.CompilerParams(vmem_limit_bytes=24 * 1024 * 1024),
        )(*operands)

    def small(kernel, in_specs, *out_shapes):
        return pl.pallas_call(
            kernel,
            out_shape=tuple(jax.ShapeDtypeStruct(shape, jnp.bfloat16) for shape in out_shapes),
            in_specs=in_specs,
            out_specs=(vmem,) * len(out_shapes),
            compiler_params=pltpu.CompilerParams(vmem_limit_bytes=8 * 1024 * 1024),
        )

    ticks = GROUPS + section_count - 1
    closing_shape = (2, half, slice_count, block_rows, block_cols)
    features = lax.all_to_all(spread, "seq", 0, 0, axis_index_groups=in_slices)[None]
    pair_shape = (2, slice_count, block_rows, model_width // 2)
    partial_out, table = attend(0, features, table, pair_shape)
    parts = exchange(partial_out, pair_peers)
    (spread,) = small(settle_first_kernel, [smem, vmem, vmem], pair_shape)(
        where, parts, in_vmem(sources)
    )
    features = exchange(spread, pair_peers)
    streams = []
    for tick in range(1, ticks - 2):
        partial_out, table = attend(tick, features, table, spread_shape)
        held = [exchange(partial_out)] + streams
        stream, spread = small(settle_kernel, [vmem] * len(held), stream_shape, spread_shape)(*held)
        streams = [stream]
        features = exchange(spread)
    partial_out, table = attend(ticks - 2, features, table, spread_shape)
    (spread,) = small(
        functools.partial(settle_last_kernel, in_group), [vmem] * 2, spread_shape
    )(exchange(partial_out), *streams)
    features = exchange(spread)
    closing, table = attend(ticks - 1, features, table, closing_shape)
    closing = lax.all_to_all(
        closing.reshape((-1,) + closing_shape[3:]),
        ("cfg", "pipe", "seq"),
        0,
        0,
        axis_index_groups=closing_peers,
    ).reshape(closing_shape)
    guided, table = pl.pallas_call(
        guide_kernel,
        out_shape=(
            jax.ShapeDtypeStruct((tok_dev, model_width // 2), jnp.bfloat16),
            jax.ShapeDtypeStruct(table.shape, jnp.bfloat16),
        ),
        in_specs=[smem, vmem, vmem],
        out_specs=(vmem, hbm),
        scratch_shapes=[pltpu.SemaphoreType.DMA],
        compiler_params=pltpu.CompilerParams(vmem_limit_bytes=8 * 1024 * 1024),
    )(where, closing, table)
    return (guided[None], table.reshape(stale_kv.shape))


def solution(mesh):
    placed = (
        P(None, "seq", None),
        P("pipe", "cfg", None, None),
        P("pipe", None, "seq"),
        P("pipe", "seq", None),
        P("pipe", None, None),
        P("pipe", "cfg", None, None, "seq", None, None, None),
    )
    return jax.shard_map(
        local,
        mesh=mesh,
        in_specs=placed,
        out_specs=(P("pipe", "seq", "cfg"), P("pipe", "cfg", None, None, "seq", None, None, None)),
        check_vma=False,
    )
```

```python
import functools
import math

import jax
import jax.numpy as jnp
from jax import lax
from jax.experimental import pallas as pl
from jax.experimental.pallas import tpu as pltpu
from jax.sharding import PartitionSpec as P

GUIDANCE_SCALE = 6.0
EPSILON = 1e-06
GROUPS = 2


def swapped(value, axis, bit):
    return lax.ppermute(value, axis, [(i, i ^ 1 << bit) for i in range(lax.axis_size(axis))])


def head_norm(values, gain_row):
    return (
        values * lax.rsqrt(jnp.mean(values * values, axis=-1, keepdims=True) + EPSILON) * gain_row
    )


def join_pair(is_upper, mine, theirs, axis_dim):
    return jnp.where(
        is_upper,
        jnp.concatenate((theirs, mine), axis_dim),
        jnp.concatenate((mine, theirs), axis_dim),
    )


def position(members):
    rank = lax.axis_index("seq")
    return lax.axis_index("pipe"), rank % members, rank // members


def section_kernel(tick, sizes, rows_ref, mod_ref, qkv_ref, out_ref, gain_ref, *refs):
    *stale_refs, old_table_ref, partial_ref, table_ref = refs
    closing = len(partial_ref.shape) == 5
    folding = tick == 1
    tok_dev, head_dim, members = sizes
    blocks, slices, block_rows, block_cols = rows_ref.shape
    rows = slices * block_rows
    width = blocks * block_cols
    in_group = block_rows // tok_dev
    group_rows = slices * tok_dev
    groups, local_width = table_ref.shape[1], table_ref.shape[3]
    heads = local_width // head_dim
    section, own_member, own_slice = position(members)
    group = tick - section
    parts = [rows_ref[q].reshape(rows, block_cols).astype(jnp.float32) for q in range(blocks)]
    mean = jnp.sum(sum(parts), axis=-1, keepdims=True) * (1.0 / width)
    parts = [x - mean for x in parts]
    spread = jnp.sum(sum(x * x for x in parts), axis=-1, keepdims=True) * (1.0 / width)
    inverse = lax.rsqrt(spread + EPSILON)
    modulated = []
    for q, x in enumerate(parts):
        at = slice(q * block_cols, (q + 1) * block_cols)
        modulated.append(
            (x * inverse * (1.0 + mod_ref[1, :, at]) + mod_ref[0, :, at]).astype(jnp.bfloat16)
        )
    modulated = jnp.concatenate(modulated, axis=1)
    mixed = jnp.dot(modulated, qkv_ref[...], preferred_element_type=jnp.float32)

    def stacked(kind):
        at = [(3 * head + kind) * head_dim for head in range(heads)]
        return jnp.stack([mixed[:, start : start + head_dim] for start in at])

    def by_patch(values):
        values = values.reshape(heads, slices, in_group, tok_dev, head_dim).swapaxes(1, 2)
        return values.reshape(heads, rows, head_dim).astype(jnp.bfloat16)

    def query_patch(shape):
        return lax.broadcasted_iota(jnp.int32, shape, 0) // tok_dev % in_group

    fresh_shape, old_shape = (rows, rows), (rows, groups * rows)
    fresh_patch = lax.broadcasted_iota(jnp.int32, fresh_shape, 1) // group_rows
    old_patch = lax.broadcasted_iota(jnp.int32, old_shape, 1) // group_rows - group * in_group
    masks = [
        (fresh_patch <= query_patch(fresh_shape)).astype(jnp.float32),
        jnp.logical_or(old_patch < 0, old_patch > query_patch(old_shape)).astype(jnp.float32),
    ]
    for ref in stale_refs:
        at = lax.broadcasted_iota(jnp.int32, (rows, ref.shape[1]), 1)
        masks.append((at // (groups * rows) != own_member).astype(jnp.float32))
    mask = jnp.concatenate(masks, axis=1)

    queries = head_norm(stacked(0), gain_ref[0:1, :]).astype(jnp.bfloat16)
    fresh = (by_patch(head_norm(stacked(1), gain_ref[1:2, :])), by_patch(stacked(2)))

    def entries(head, kind):
        at = slice(head * head_dim, (head + 1) * head_dim)
        old = old_table_ref[kind, :, :, at].reshape(groups * rows, head_dim)
        return jnp.concatenate([fresh[kind][head], old] + [ref[kind, :, at] for ref in stale_refs])

    scores = [
        lax.dot_general(
            queries[head],
            entries(head, 0),
            (((1,), (1,)), ((), ())),
            preferred_element_type=jnp.float32,
        )
        for head in range(heads)
    ]
    weights = mask[None] * jnp.exp(jnp.stack(scores) * (1.0 / math.sqrt(head_dim)))
    inverse = 1.0 / jnp.sum(weights, axis=-1, keepdims=True)
    weights = weights.astype(jnp.bfloat16)
    summed = [
        jnp.dot(weights[head], entries(head, 1), preferred_element_type=jnp.float32)
        for head in range(heads)
    ]
    attended = (jnp.stack(summed) * inverse).astype(jnp.bfloat16)
    attended = jnp.concatenate([attended[head] for head in range(heads)], axis=1)

    projected = jnp.dot(attended, out_ref[...], preferred_element_type=jnp.float32)
    projected = mod_ref[2] * projected
    if folding:
        at_slice = lax.broadcasted_iota(jnp.int32, (rows, 1), 0) // block_rows
        own = (at_slice == own_slice).astype(jnp.float32)
        projected = projected + own * jnp.concatenate(
            [rows_ref[q].reshape(rows, block_cols).astype(jnp.float32) for q in range(blocks)],
            axis=1,
        )
    if closing:
        close_into(partial_ref, projected, rows_ref, section, own_slice, in_group)
    else:
        out_cols = partial_ref.shape[3]
        for q in range(partial_ref.shape[0]):
            piece = projected[:, q * out_cols : (q + 1) * out_cols].astype(jnp.bfloat16)
            partial_ref[q] = piece.reshape(slices, block_rows, out_cols)

    for at in range(groups):

        @pl.when(group == at)
        def _():
            for j in range(2):
                table_ref[j, at] = jnp.concatenate([fresh[j][head] for head in range(heads)], axis=1)

        @pl.when(group != at)
        def _():
            for j in range(2):
                table_ref[j, at] = old_table_ref[j, at]


def close_into(closing_ref, projected, rows_ref, section, own_slice, in_group):
    branches, patches, slices = closing_ref.shape[:3]
    blocks, _, block_rows, block_cols = rows_ref.shape
    tok_dev = block_rows // in_group
    per_branch = blocks // branches

    @pl.when(section >= patches)
    def _():
        for piece in range(slices):
            own = (own_slice == piece).astype(jnp.float32)
            by_block = []
            for q in range(blocks):
                rows = projected[
                    piece * block_rows : (piece + 1) * block_rows,
                    q * block_cols : (q + 1) * block_cols,
                ]
                rows = rows + own * rows_ref[q, piece].astype(jnp.float32)
                by_block.append(rows.reshape(in_group, tok_dev, block_cols))
            for branch in range(branches):
                for patch in range(patches):
                    held = [by_block[branch * per_branch + k][patch] for k in range(per_branch)]
                    closing_ref[branch, patch, piece] = jnp.concatenate(held).astype(jnp.bfloat16)

    @pl.when(section < patches)
    def _():
        finished = [rows_ref[q, own_slice].astype(jnp.float32)[:tok_dev] for q in range(blocks)]
        for branch in range(branches):
            held = jnp.concatenate(finished[branch * per_branch : (branch + 1) * per_branch])
            held = held.astype(jnp.bfloat16)
            for patch in range(patches):
                for piece in range(slices):
                    closing_ref[branch, patch, piece] = held


def start_kernel(latent_ref, *refs):
    spread_to = refs[-1]
    for piece in range(spread_to.shape[0]):
        spread_to[piece] = latent_ref[0]


def added(parts_ref, section, *streams_refs):
    total = sum(parts_ref[section, piece].astype(jnp.float32) for piece in range(parts_ref.shape[1]))
    for ref in streams_refs:
        total = total + ref[section].astype(jnp.float32)
    return total


def settle_first_kernel(parts_ref, latent_ref, spread_to):
    first = added(parts_ref, 0)
    half_cols = first.shape[1]
    for half in range(2):

        @pl.when(lax.axis_index("pipe") % 2 == half)
        def _():
            at = slice(half * half_cols, (half + 1) * half_cols)
            held = (first + latent_ref[0, :, at].astype(jnp.float32)).astype(jnp.bfloat16)
            for piece in range(parts_ref.shape[1]):
                spread_to[0, piece] = latent_ref[1, :, at]
                spread_to[1, piece] = held


def settle_kernel(parts_ref, *refs):
    *streams_refs, streams_to, spread_to = refs
    count, slices = parts_ref.shape[:2]
    for section in range(count):
        held = added(parts_ref, max(section - 1, 0), *streams_refs).astype(jnp.bfloat16)
        streams_to[section] = held
        for piece in range(slices):
            spread_to[section, piece] = held


def settle_last_kernel(in_group, parts_ref, streams_ref, spread_to):
    count, slices = parts_ref.shape[:2]
    finished = added(parts_ref, count - 1, streams_ref)
    tok_dev = finished.shape[0] // in_group
    last = added(parts_ref, count - 2, streams_ref).astype(jnp.bfloat16)
    for section in range(count):
        held = last
        if section < in_group:
            held = finished[section * tok_dev : (section + 1) * tok_dev]
            held = jnp.concatenate([held] * in_group).astype(jnp.bfloat16)
        for piece in range(slices):
            spread_to[section, piece] = held


def guide_kernel(members, closing_ref, table_ref, guided_ref, table_to, sem):
    copy = pltpu.make_async_copy(table_ref, table_to, sem)
    copy.start()
    branches, patches, slices, block_rows, block_cols = closing_ref.shape
    tok_dev = guided_ref.shape[0]
    section, _, own_slice = position(members)

    def combine(pair):
        conditional, unconditional = pair
        rows = unconditional + GUIDANCE_SCALE * (conditional - unconditional)
        for at in range(block_rows // tok_dev):
            guided_ref[:, at * block_cols : (at + 1) * block_cols] = rows[
                at * tok_dev : (at + 1) * tok_dev
            ].astype(jnp.bfloat16)

    @pl.when(section >= patches)
    def _():
        pair = []
        for branch in range(branches):
            total = 0.0
            for piece in range(slices):
                total = total + closing_ref[branch, patches - 1, piece].astype(jnp.float32)
            pair.append(total.astype(jnp.bfloat16).astype(jnp.float32))
        combine(pair)

    @pl.when(section < patches)
    def _():
        combine(
            [closing_ref[branch, section, own_slice].astype(jnp.float32) for branch in range(branches)]
        )

    copy.wait()


def local(latent, modulation, qkv_weight, out_weight, norm_gain, stale_kv):
    seq_count = lax.axis_size("seq")
    seq_rank = lax.axis_index("seq")
    section_count = lax.axis_size("pipe")
    patches, tok_dev, model_width = latent.shape
    head_dim = norm_gain.shape[2]
    slice_count = min(seq_count, 8)
    member_count = seq_count // slice_count
    member_bits = member_count.bit_length() - 1
    own_member = seq_rank % member_count
    local_width = stale_kv.shape[7]
    group_rows = slice_count * tok_dev
    own_cache = stale_kv[0, 0].reshape(2, patches, group_rows, local_width)
    group_cache = own_cache[None]
    qkv_slice = qkv_weight[0]
    out_slice = out_weight[0]
    for level_index in range(member_bits):
        got_qkv, got_out, got_cache = (
            swapped(qkv_slice, "seq", level_index),
            swapped(out_slice, "seq", level_index),
            swapped(group_cache, "seq", level_index),
        )
        is_upper = own_member >> level_index & 1 == 1
        qkv_slice = join_pair(is_upper, qkv_slice, got_qkv, 1)
        out_slice = join_pair(is_upper, out_slice, got_out, 0)
        group_cache = join_pair(is_upper, group_cache, got_cache, 0)
    homes = section_count * slice_count
    in_group = patches // GROUPS
    block_rows = in_group * tok_dev
    block_cols = model_width // section_count
    rows = slice_count * block_rows
    half = section_count // 2
    groups_of = range(member_count)
    in_slices = [[a + member_count * b for b in range(slice_count)] for a in groups_of]
    peers = [[q * seq_count + at for q in range(section_count) for at in g] for g in in_slices]
    closing_peers = [
        [
            (c * section_count + q) * seq_count + at
            for c in range(2)
            for q in range(h * half, (h + 1) * half)
            for at in g
        ]
        for h in range(2)
        for g in in_slices
    ]

    pair_peers = [
        [q * seq_count + at for q in range(first, first + 2) for at in g]
        for first in range(0, section_count, 2)
        for g in in_slices
    ]

    def exchange(value, among=peers):
        flat = value.reshape((-1,) + value.shape[2:])
        flat = lax.all_to_all(flat, ("pipe", "seq"), 0, 0, axis_index_groups=among)
        return flat.reshape(value.shape)

    vmem = pl.BlockSpec(memory_space=pltpu.VMEM)
    hbm = pl.BlockSpec(memory_space=pltpu.HBM)
    in_hbm = functools.partial(pltpu.with_memory_space_constraint, memory_space=pltpu.HBM)
    in_vmem = functools.partial(pltpu.with_memory_space_constraint, memory_space=pltpu.VMEM)
    sources = latent.reshape(GROUPS, block_rows, model_width)
    stream_shape = (section_count, block_rows, block_cols)
    spread_shape = (section_count, slice_count, block_rows, block_cols)
    modulation = modulation.reshape(3, 1, model_width)
    norm_gain = norm_gain[0]
    table = own_cache.reshape(2, GROUPS, rows, local_width)
    named = (qkv_slice, out_slice, modulation, norm_gain, table)
    spread = pl.pallas_call(
        start_kernel,
        out_shape=jax.ShapeDtypeStruct((slice_count, block_rows, model_width), jnp.bfloat16),
        in_specs=[vmem] + [hbm] * len(named),
        out_specs=vmem,
        compiler_params=pltpu.CompilerParams(vmem_limit_bytes=4 * 1024 * 1024),
    )(in_vmem(sources), *map(in_hbm, named))
    stale_rows = []
    if member_count > 1:
        stale_rows = [group_cache.swapaxes(0, 1).reshape(2, -1, local_width)]

    def attend(tick, features, table, partial_shape):
        operands = (
            features,
            in_vmem(modulation),
            in_vmem(qkv_slice),
            in_vmem(out_slice),
            in_vmem(norm_gain),
            *stale_rows,
            in_vmem(table),
        )
        return pl.pallas_call(
            functools.partial(section_kernel, tick, (tok_dev, head_dim, member_count)),
            out_shape=(
                jax.ShapeDtypeStruct(partial_shape, jnp.bfloat16),
                jax.ShapeDtypeStruct(table.shape, jnp.bfloat16),
            ),
            in_specs=[vmem] * len(operands),
            out_specs=(vmem, vmem),
            compiler_params=pltpu.CompilerParams(vmem_limit_bytes=24 * 1024 * 1024),
        )(*operands)

    def small(kernel, in_specs, *out_shapes):
        return pl.pallas_call(
            kernel,
            out_shape=tuple(jax.ShapeDtypeStruct(shape, jnp.bfloat16) for shape in out_shapes),
            in_specs=in_specs,
            out_specs=(vmem,) * len(out_shapes),
            compiler_params=pltpu.CompilerParams(vmem_limit_bytes=8 * 1024 * 1024),
        )

    ticks = GROUPS + section_count - 1
    closing_shape = (2, half, slice_count, block_rows, block_cols)
    features = lax.all_to_all(spread, "seq", 0, 0, axis_index_groups=in_slices)[None]
    pair_shape = (2, slice_count, block_rows, model_width // 2)
    partial_out, table = attend(0, features, table, pair_shape)
    parts = exchange(partial_out, pair_peers)
    (spread,) = small(settle_first_kernel, [vmem] * 2, pair_shape)(parts, in_vmem(sources))
    features = exchange(spread, pair_peers)
    streams = []
    for tick in range(1, ticks - 2):
        partial_out, table = attend(tick, features, table, spread_shape)
        held = [exchange(partial_out)] + streams
        stream, spread = small(settle_kernel, [vmem] * len(held), stream_shape, spread_shape)(*held)
        streams = [stream]
        features = exchange(spread)
    partial_out, table = attend(ticks - 2, features, table, spread_shape)
    (spread,) = small(
        functools.partial(settle_last_kernel, in_group), [vmem] * 2, spread_shape
    )(exchange(partial_out), *streams)
    features = exchange(spread)
    closing, table = attend(ticks - 1, features, table, closing_shape)
    closing = lax.all_to_all(
        closing.reshape((-1,) + closing_shape[3:]),
        ("cfg", "pipe", "seq"),
        0,
        0,
        axis_index_groups=closing_peers,
    ).reshape(closing_shape)
    guided, table = pl.pallas_call(
        functools.partial(guide_kernel, member_count),
        out_shape=(
            jax.ShapeDtypeStruct((tok_dev, model_width // 2), jnp.bfloat16),
            jax.ShapeDtypeStruct(table.shape, jnp.bfloat16),
        ),
        in_specs=[vmem, vmem],
        out_specs=(vmem, hbm),
        scratch_shapes=[pltpu.SemaphoreType.DMA],
        compiler_params=pltpu.CompilerParams(vmem_limit_bytes=8 * 1024 * 1024),
    )(closing, table)
    return (guided[None], table.reshape(stale_kv.shape))


def solution(mesh):
    placed = (
        P(None, "seq", None),
        P("pipe", "cfg", None, None),
        P("pipe", None, "seq"),
        P("pipe", "seq", None),
        P("pipe", None, None),
        P("pipe", "cfg", None, None, "seq", None, None, None),
    )
    return jax.shard_map(
        local,
        mesh=mesh,
        in_specs=placed,
        out_specs=(P("pipe", "seq", "cfg"), P("pipe", "cfg", None, None, "seq", None, None, None)),
        check_vma=False,
    )
```

```python
import functools
import math

import jax
import jax.numpy as jnp
from jax import lax
from jax.experimental import pallas as pl
from jax.experimental.pallas import tpu as pltpu
from jax.sharding import PartitionSpec as P

GUIDANCE_SCALE = 6.0
EPSILON = 1e-06
GROUPS = 2


def swapped(value, axis, bit):
    return lax.ppermute(value, axis, [(i, i ^ 1 << bit) for i in range(lax.axis_size(axis))])


def head_norm(values, gain_row):
    return (
        values * lax.rsqrt(jnp.mean(values * values, axis=-1, keepdims=True) + EPSILON) * gain_row
    )


def join_pair(is_upper, mine, theirs, axis_dim):
    return jnp.where(
        is_upper,
        jnp.concatenate((theirs, mine), axis_dim),
        jnp.concatenate((mine, theirs), axis_dim),
    )


def position(members):
    rank = lax.axis_index("seq")
    return lax.axis_index("pipe"), rank % members, rank // members


def section_kernel(tick, sizes, rows_ref, mod_ref, qkv_ref, out_ref, gain_ref, *refs):
    *stale_refs, old_table_ref, partial_ref, table_ref = refs
    closing = len(partial_ref.shape) == 5
    folding = tick == 1
    tok_dev, head_dim, members = sizes
    blocks, slices, block_rows, block_cols = rows_ref.shape
    rows = slices * block_rows
    width = blocks * block_cols
    in_group = block_rows // tok_dev
    group_rows = slices * tok_dev
    groups, local_width = table_ref.shape[1], table_ref.shape[3]
    heads = local_width // head_dim
    section, own_member, own_slice = position(members)
    group = tick - section
    parts = [rows_ref[q].reshape(rows, block_cols).astype(jnp.float32) for q in range(blocks)]
    mean = jnp.sum(sum(parts), axis=-1, keepdims=True) * (1.0 / width)
    parts = [x - mean for x in parts]
    spread = jnp.sum(sum(x * x for x in parts), axis=-1, keepdims=True) * (1.0 / width)
    inverse = lax.rsqrt(spread + EPSILON)
    modulated = []
    for q, x in enumerate(parts):
        at = slice(q * block_cols, (q + 1) * block_cols)
        modulated.append(
            (x * inverse * (1.0 + mod_ref[1, :, at]) + mod_ref[0, :, at]).astype(jnp.bfloat16)
        )
    modulated = jnp.concatenate(modulated, axis=1)
    mixed = jnp.dot(modulated, qkv_ref[...], preferred_element_type=jnp.float32)

    def stacked(kind):
        at = [(3 * head + kind) * head_dim for head in range(heads)]
        return jnp.stack([mixed[:, start : start + head_dim] for start in at])

    def by_patch(values):
        values = values.reshape(heads, slices, in_group, tok_dev, head_dim).swapaxes(1, 2)
        return values.reshape(heads, rows, head_dim).astype(jnp.bfloat16)

    def query_patch(shape):
        return lax.broadcasted_iota(jnp.int32, shape, 0) // tok_dev % in_group

    fresh_shape, old_shape = (rows, rows), (rows, groups * rows)
    fresh_patch = lax.broadcasted_iota(jnp.int32, fresh_shape, 1) // group_rows
    old_patch = lax.broadcasted_iota(jnp.int32, old_shape, 1) // group_rows - group * in_group
    masks = [
        (fresh_patch <= query_patch(fresh_shape)).astype(jnp.float32),
        jnp.logical_or(old_patch < 0, old_patch > query_patch(old_shape)).astype(jnp.float32),
    ]
    for ref in stale_refs:
        at = lax.broadcasted_iota(jnp.int32, (rows, ref.shape[1]), 1)
        masks.append((at // (groups * rows) != own_member).astype(jnp.float32))
    mask = jnp.concatenate(masks, axis=1)

    queries = head_norm(stacked(0), gain_ref[0:1, :]).astype(jnp.bfloat16)
    fresh = (by_patch(head_norm(stacked(1), gain_ref[1:2, :])), by_patch(stacked(2)))

    def entries(head, kind):
        at = slice(head * head_dim, (head + 1) * head_dim)
        old = old_table_ref[kind, :, :, at].reshape(groups * rows, head_dim)
        return jnp.concatenate([fresh[kind][head], old] + [ref[kind, :, at] for ref in stale_refs])

    scores = [
        lax.dot_general(
            queries[head],
            entries(head, 0),
            (((1,), (1,)), ((), ())),
            preferred_element_type=jnp.float32,
        )
        for head in range(heads)
    ]
    weights = mask[None] * jnp.exp(jnp.stack(scores) * (1.0 / math.sqrt(head_dim)))
    inverse = 1.0 / jnp.sum(weights, axis=-1, keepdims=True)
    weights = weights.astype(jnp.bfloat16)
    summed = [
        jnp.dot(weights[head], entries(head, 1), preferred_element_type=jnp.float32)
        for head in range(heads)
    ]
    attended = (jnp.stack(summed) * inverse).astype(jnp.bfloat16)
    attended = jnp.concatenate([attended[head] for head in range(heads)], axis=1)

    projected = jnp.dot(attended, out_ref[...], preferred_element_type=jnp.float32)
    projected = mod_ref[2] * projected
    if folding:
        at_slice = lax.broadcasted_iota(jnp.int32, (rows, 1), 0) // block_rows
        own = (at_slice == own_slice).astype(jnp.float32)
        projected = projected + own * jnp.concatenate(
            [rows_ref[q].reshape(rows, block_cols).astype(jnp.float32) for q in range(blocks)],
            axis=1,
        )
    if closing:
        close_into(partial_ref, projected, rows_ref, section, own_slice, in_group)
    else:
        out_cols = partial_ref.shape[3]
        for q in range(partial_ref.shape[0]):
            piece = projected[:, q * out_cols : (q + 1) * out_cols].astype(jnp.bfloat16)
            partial_ref[q] = piece.reshape(slices, block_rows, out_cols)

    for kind in range(2):
        rows_of = jnp.concatenate([fresh[kind][head] for head in range(heads)], axis=1)
        for at in range(groups):
            table_ref[kind, at] = jnp.where(group == at, rows_of, old_table_ref[kind, at])


def close_into(closing_ref, projected, rows_ref, section, own_slice, in_group):
    branches, patches, slices = closing_ref.shape[:3]
    blocks, _, block_rows, block_cols = rows_ref.shape
    tok_dev = block_rows // in_group
    per_branch = blocks // branches

    @pl.when(section >= patches)
    def _():
        for piece in range(slices):
            own = (own_slice == piece).astype(jnp.float32)
            by_block = []
            for q in range(blocks):
                rows = projected[
                    piece * block_rows : (piece + 1) * block_rows,
                    q * block_cols : (q + 1) * block_cols,
                ]
                rows = rows + own * rows_ref[q, piece].astype(jnp.float32)
                by_block.append(rows.reshape(in_group, tok_dev, block_cols))
            for branch in range(branches):
                for patch in range(patches):
                    held = [by_block[branch * per_branch + k][patch] for k in range(per_branch)]
                    closing_ref[branch, patch, piece] = jnp.concatenate(held).astype(jnp.bfloat16)

    @pl.when(section < patches)
    def _():
        finished = [rows_ref[q, own_slice].astype(jnp.float32)[:tok_dev] for q in range(blocks)]
        for branch in range(branches):
            held = jnp.concatenate(finished[branch * per_branch : (branch + 1) * per_branch])
            held = held.astype(jnp.bfloat16)
            for patch in range(patches):
                for piece in range(slices):
                    closing_ref[branch, patch, piece] = held


def start_kernel(latent_ref, *refs):
    spread_to = refs[-1]
    half_cols = spread_to.shape[3]
    for half in range(2):

        @pl.when(lax.axis_index("pipe") % 2 == half)
        def _():
            held = latent_ref[0, :, half * half_cols : (half + 1) * half_cols]
            for line in range(2):
                for piece in range(spread_to.shape[1]):
                    spread_to[line, piece] = held


def added(parts_ref, section, *streams_refs):
    total = sum(parts_ref[section, piece].astype(jnp.float32) for piece in range(parts_ref.shape[1]))
    for ref in streams_refs:
        total = total + ref[section].astype(jnp.float32)
    return total


def settle_first_kernel(parts_ref, latent_ref, spread_to):
    first = added(parts_ref, 0)
    half_cols = first.shape[1]
    for half in range(2):

        @pl.when(lax.axis_index("pipe") % 2 == half)
        def _():
            at = slice(half * half_cols, (half + 1) * half_cols)
            held = (first + latent_ref[0, :, at].astype(jnp.float32)).astype(jnp.bfloat16)
            for piece in range(parts_ref.shape[1]):
                spread_to[0, piece] = latent_ref[1, :, at]
                spread_to[1, piece] = held


def settle_kernel(parts_ref, *refs):
    *streams_refs, streams_to, spread_to = refs
    count, slices = parts_ref.shape[:2]
    for section in range(count):
        held = added(parts_ref, max(section - 1, 0), *streams_refs).astype(jnp.bfloat16)
        streams_to[section] = held
        for piece in range(slices):
            spread_to[section, piece] = held


def settle_last_kernel(in_group, parts_ref, streams_ref, spread_to):
    count, slices = parts_ref.shape[:2]
    finished = added(parts_ref, count - 1, streams_ref)
    tok_dev = finished.shape[0] // in_group
    last = added(parts_ref, count - 2, streams_ref).astype(jnp.bfloat16)
    for section in range(count):
        held = last
        if section < in_group:
            held = finished[section * tok_dev : (section + 1) * tok_dev]
            held = jnp.concatenate([held] * in_group).astype(jnp.bfloat16)
        for piece in range(slices):
            spread_to[section, piece] = held


def guide_kernel(members, closing_ref, table_ref, guided_ref, table_to, sem):
    copy = pltpu.make_async_copy(table_ref, table_to, sem)
    copy.start()
    branches, patches, slices, block_rows, block_cols = closing_ref.shape
    tok_dev = guided_ref.shape[0]
    section, _, own_slice = position(members)

    def combine(pair):
        conditional, unconditional = pair
        rows = unconditional + GUIDANCE_SCALE * (conditional - unconditional)
        for at in range(block_rows // tok_dev):
            guided_ref[:, at * block_cols : (at + 1) * block_cols] = rows[
                at * tok_dev : (at + 1) * tok_dev
            ].astype(jnp.bfloat16)

    @pl.when(section >= patches)
    def _():
        pair = []
        for branch in range(branches):
            total = 0.0
            for piece in range(slices):
                total = total + closing_ref[branch, patches - 1, piece].astype(jnp.float32)
            pair.append(total.astype(jnp.bfloat16).astype(jnp.float32))
        combine(pair)

    @pl.when(section < patches)
    def _():
        combine(
            [closing_ref[branch, section, own_slice].astype(jnp.float32) for branch in range(branches)]
        )

    copy.wait()


def local(latent, modulation, qkv_weight, out_weight, norm_gain, stale_kv):
    seq_count = lax.axis_size("seq")
    seq_rank = lax.axis_index("seq")
    section_count = lax.axis_size("pipe")
    patches, tok_dev, model_width = latent.shape
    head_dim = norm_gain.shape[2]
    slice_count = min(seq_count, 8)
    member_count = seq_count // slice_count
    member_bits = member_count.bit_length() - 1
    own_member = seq_rank % member_count
    local_width = stale_kv.shape[7]
    group_rows = slice_count * tok_dev
    own_cache = stale_kv[0, 0].reshape(2, patches, group_rows, local_width)
    group_cache = own_cache[None]
    qkv_slice = qkv_weight[0]
    out_slice = out_weight[0]
    for level_index in range(member_bits):
        got_qkv, got_out, got_cache = (
            swapped(qkv_slice, "seq", level_index),
            swapped(out_slice, "seq", level_index),
            swapped(group_cache, "seq", level_index),
        )
        is_upper = own_member >> level_index & 1 == 1
        qkv_slice = join_pair(is_upper, qkv_slice, got_qkv, 1)
        out_slice = join_pair(is_upper, out_slice, got_out, 0)
        group_cache = join_pair(is_upper, group_cache, got_cache, 0)
    homes = section_count * slice_count
    in_group = patches // GROUPS
    block_rows = in_group * tok_dev
    block_cols = model_width // section_count
    rows = slice_count * block_rows
    half = section_count // 2
    groups_of = range(member_count)
    in_slices = [[a + member_count * b for b in range(slice_count)] for a in groups_of]
    peers = [[q * seq_count + at for q in range(section_count) for at in g] for g in in_slices]
    closing_peers = [
        [
            (c * section_count + q) * seq_count + at
            for c in range(2)
            for q in range(h * half, (h + 1) * half)
            for at in g
        ]
        for h in range(2)
        for g in in_slices
    ]

    pair_peers = [
        [q * seq_count + at for q in range(first, first + 2) for at in g]
        for first in range(0, section_count, 2)
        for g in in_slices
    ]

    def exchange(value, among=peers):
        flat = value.reshape((-1,) + value.shape[2:])
        flat = lax.all_to_all(flat, ("pipe", "seq"), 0, 0, axis_index_groups=among)
        return flat.reshape(value.shape)

    vmem = pl.BlockSpec(memory_space=pltpu.VMEM)
    hbm = pl.BlockSpec(memory_space=pltpu.HBM)
    in_hbm = functools.partial(pltpu.with_memory_space_constraint, memory_space=pltpu.HBM)
    in_vmem = functools.partial(pltpu.with_memory_space_constraint, memory_space=pltpu.VMEM)
    sources = latent.reshape(GROUPS, block_rows, model_width)
    stream_shape = (section_count, block_rows, block_cols)
    spread_shape = (section_count, slice_count, block_rows, block_cols)
    pair_shape = (2, slice_count, block_rows, model_width // 2)
    modulation = modulation.reshape(3, 1, model_width)
    norm_gain = norm_gain[0]
    table = own_cache.reshape(2, GROUPS, rows, local_width)
    named = (qkv_slice, out_slice, modulation, norm_gain, table)
    spread = pl.pallas_call(
        start_kernel,
        out_shape=jax.ShapeDtypeStruct(pair_shape, jnp.bfloat16),
        in_specs=[vmem] + [hbm] * len(named),
        out_specs=vmem,
        compiler_params=pltpu.CompilerParams(vmem_limit_bytes=4 * 1024 * 1024),
    )(in_vmem(sources), *map(in_hbm, named))
    stale_rows = []
    if member_count > 1:
        stale_rows = [group_cache.swapaxes(0, 1).reshape(2, -1, local_width)]

    def attend(tick, features, table, partial_shape):
        operands = (
            features,
            in_vmem(modulation),
            in_vmem(qkv_slice),
            in_vmem(out_slice),
            in_vmem(norm_gain),
            *stale_rows,
            in_vmem(table),
        )
        return pl.pallas_call(
            functools.partial(section_kernel, tick, (tok_dev, head_dim, member_count)),
            out_shape=(
                jax.ShapeDtypeStruct(partial_shape, jnp.bfloat16),
                jax.ShapeDtypeStruct(table.shape, jnp.bfloat16),
            ),
            in_specs=[vmem] * len(operands),
            out_specs=(vmem, vmem),
            compiler_params=pltpu.CompilerParams(vmem_limit_bytes=24 * 1024 * 1024),
        )(*operands)

    def small(kernel, in_specs, *out_shapes):
        return pl.pallas_call(
            kernel,
            out_shape=tuple(jax.ShapeDtypeStruct(shape, jnp.bfloat16) for shape in out_shapes),
            in_specs=in_specs,
            out_specs=(vmem,) * len(out_shapes),
            compiler_params=pltpu.CompilerParams(vmem_limit_bytes=8 * 1024 * 1024),
        )

    ticks = GROUPS + section_count - 1
    closing_shape = (2, half, slice_count, block_rows, block_cols)
    features = exchange(spread, pair_peers)
    partial_out, table = attend(0, features, table, pair_shape)
    parts = exchange(partial_out, pair_peers)
    (spread,) = small(settle_first_kernel, [vmem] * 2, pair_shape)(parts, in_vmem(sources))
    features = exchange(spread, pair_peers)
    streams = []
    for tick in range(1, ticks - 2):
        partial_out, table = attend(tick, features, table, spread_shape)
        held = [exchange(partial_out)] + streams
        stream, spread = small(settle_kernel, [vmem] * len(held), stream_shape, spread_shape)(*held)
        streams = [stream]
        features = exchange(spread)
    partial_out, table = attend(ticks - 2, features, table, spread_shape)
    (spread,) = small(
        functools.partial(settle_last_kernel, in_group), [vmem] * 2, spread_shape
    )(exchange(partial_out), *streams)
    features = exchange(spread)
    closing, table = attend(ticks - 1, features, table, closing_shape)
    closing = lax.all_to_all(
        closing.reshape((-1,) + closing_shape[3:]),
        ("cfg", "pipe", "seq"),
        0,
        0,
        axis_index_groups=closing_peers,
    ).reshape(closing_shape)
    guided, table = pl.pallas_call(
        functools.partial(guide_kernel, member_count),
        out_shape=(
            jax.ShapeDtypeStruct((tok_dev, model_width // 2), jnp.bfloat16),
            jax.ShapeDtypeStruct(table.shape, jnp.bfloat16),
        ),
        in_specs=[vmem, vmem],
        out_specs=(vmem, hbm),
        scratch_shapes=[pltpu.SemaphoreType.DMA],
        compiler_params=pltpu.CompilerParams(vmem_limit_bytes=8 * 1024 * 1024),
    )(closing, table)
    return (guided[None], table.reshape(stale_kv.shape))


def solution(mesh):
    placed = (
        P(None, "seq", None),
        P("pipe", "cfg", None, None),
        P("pipe", None, "seq"),
        P("pipe", "seq", None),
        P("pipe", None, None),
        P("pipe", "cfg", None, None, "seq", None, None, None),
    )
    return jax.shard_map(
        local,
        mesh=mesh,
        in_specs=placed,
        out_specs=(P("pipe", "seq", "cfg"), P("pipe", "cfg", None, None, "seq", None, None, None)),
        check_vma=False,
    )
```

```python
import functools
import math

import jax
import jax.numpy as jnp
from jax import lax
from jax.experimental import pallas as pl
from jax.experimental.pallas import tpu as pltpu
from jax.sharding import PartitionSpec as P

GUIDANCE_SCALE = 6.0
EPSILON = 1e-06
GROUPS = 2


def swapped(value, axis, bit):
    return lax.ppermute(value, axis, [(i, i ^ 1 << bit) for i in range(lax.axis_size(axis))])


def head_norm(values, gain_row):
    return (
        values * lax.rsqrt(jnp.mean(values * values, axis=-1, keepdims=True) + EPSILON) * gain_row
    )


def join_pair(is_upper, mine, theirs, axis_dim):
    return jnp.where(
        is_upper,
        jnp.concatenate((theirs, mine), axis_dim),
        jnp.concatenate((mine, theirs), axis_dim),
    )


def position(members):
    rank = lax.axis_index("seq")
    return lax.axis_index("pipe"), rank % members, rank // members


def section_kernel(tick, sizes, rows_ref, mod_ref, qkv_ref, out_ref, gain_ref, *refs):
    *stale_refs, old_table_ref, partial_ref, table_ref = refs
    closing = len(partial_ref.shape) == 5
    folding = tick == 1
    tok_dev, head_dim, members = sizes
    blocks, slices, block_rows, block_cols = rows_ref.shape
    rows = slices * block_rows
    width = blocks * block_cols
    in_group = block_rows // tok_dev
    group_rows = slices * tok_dev
    groups, local_width = table_ref.shape[1], table_ref.shape[3]
    heads = local_width // head_dim
    section, own_member, own_slice = position(members)
    group = tick - section
    parts = [rows_ref[q].reshape(rows, block_cols).astype(jnp.float32) for q in range(blocks)]
    mean = jnp.sum(sum(parts), axis=-1, keepdims=True) * (1.0 / width)
    parts = [x - mean for x in parts]
    spread = jnp.sum(sum(x * x for x in parts), axis=-1, keepdims=True) * (1.0 / width)
    inverse = lax.rsqrt(spread + EPSILON)
    modulated = []
    for q, x in enumerate(parts):
        at = slice(q * block_cols, (q + 1) * block_cols)
        modulated.append(
            (x * inverse * (1.0 + mod_ref[1, :, at]) + mod_ref[0, :, at]).astype(jnp.bfloat16)
        )
    modulated = jnp.concatenate(modulated, axis=1)
    mixed = jnp.dot(modulated, qkv_ref[...], preferred_element_type=jnp.float32)

    def stacked(kind):
        at = [(3 * head + kind) * head_dim for head in range(heads)]
        return jnp.stack([mixed[:, start : start + head_dim] for start in at])

    def by_patch(values):
        values = values.reshape(heads, slices, in_group, tok_dev, head_dim).swapaxes(1, 2)
        return values.reshape(heads, rows, head_dim).astype(jnp.bfloat16)

    def query_patch(shape):
        return lax.broadcasted_iota(jnp.int32, shape, 0) // tok_dev % in_group

    fresh_shape, old_shape = (rows, rows), (rows, groups * rows)
    fresh_patch = lax.broadcasted_iota(jnp.int32, fresh_shape, 1) // group_rows
    old_patch = lax.broadcasted_iota(jnp.int32, old_shape, 1) // group_rows - group * in_group
    masks = [
        (fresh_patch <= query_patch(fresh_shape)).astype(jnp.float32),
        jnp.logical_or(old_patch < 0, old_patch > query_patch(old_shape)).astype(jnp.float32),
    ]
    for ref in stale_refs:
        at = lax.broadcasted_iota(jnp.int32, (rows, ref.shape[1]), 1)
        masks.append((at // (groups * rows) != own_member).astype(jnp.float32))
    mask = jnp.concatenate(masks, axis=1)

    queries = head_norm(stacked(0), gain_ref[0:1, :]).astype(jnp.bfloat16)
    fresh = (by_patch(head_norm(stacked(1), gain_ref[1:2, :])), by_patch(stacked(2)))

    def entries(head, kind):
        at = slice(head * head_dim, (head + 1) * head_dim)
        old = old_table_ref[kind, :, :, at].reshape(groups * rows, head_dim)
        return jnp.concatenate([fresh[kind][head], old] + [ref[kind, :, at] for ref in stale_refs])

    scores = [
        lax.dot_general(
            queries[head],
            entries(head, 0),
            (((1,), (1,)), ((), ())),
            preferred_element_type=jnp.float32,
        )
        for head in range(heads)
    ]
    weights = mask[None] * jnp.exp(jnp.stack(scores) * (1.0 / math.sqrt(head_dim)))
    inverse = 1.0 / jnp.sum(weights, axis=-1, keepdims=True)
    weights = weights.astype(jnp.bfloat16)
    summed = [
        jnp.dot(weights[head], entries(head, 1), preferred_element_type=jnp.float32)
        for head in range(heads)
    ]
    attended = (jnp.stack(summed) * inverse).astype(jnp.bfloat16)
    attended = jnp.concatenate([attended[head] for head in range(heads)], axis=1)

    projected = jnp.dot(attended, out_ref[...], preferred_element_type=jnp.float32)
    projected = mod_ref[2] * projected
    if folding:
        at_slice = lax.broadcasted_iota(jnp.int32, (rows, 1), 0) // block_rows
        own = (at_slice == own_slice).astype(jnp.float32)
        projected = projected + own * jnp.concatenate(
            [rows_ref[q].reshape(rows, block_cols).astype(jnp.float32) for q in range(blocks)],
            axis=1,
        )
    if closing:
        close_into(partial_ref, projected, rows_ref, section, own_slice, in_group)
    else:
        out_cols = partial_ref.shape[3]
        for q in range(partial_ref.shape[0]):
            piece = projected[:, q * out_cols : (q + 1) * out_cols].astype(jnp.bfloat16)
            partial_ref[q] = piece.reshape(slices, block_rows, out_cols)

    for kind in range(2):
        rows_of = jnp.concatenate([fresh[kind][head] for head in range(heads)], axis=1)
        for at in range(groups):
            table_ref[kind, at] = jnp.where(group == at, rows_of, old_table_ref[kind, at])


def close_into(closing_ref, projected, rows_ref, section, own_slice, in_group):
    branches, patches, slices = closing_ref.shape[:3]
    blocks, _, block_rows, block_cols = rows_ref.shape
    tok_dev = block_rows // in_group
    per_branch = blocks // branches

    @pl.when(section >= patches)
    def _():
        for piece in range(slices):
            own = (own_slice == piece).astype(jnp.float32)
            by_block = []
            for q in range(blocks):
                rows = projected[
                    piece * block_rows : (piece + 1) * block_rows,
                    q * block_cols : (q + 1) * block_cols,
                ]
                rows = rows + own * rows_ref[q, piece].astype(jnp.float32)
                by_block.append(rows.reshape(in_group, tok_dev, block_cols))
            for branch in range(branches):
                for patch in range(patches):
                    held = [by_block[branch * per_branch + k][patch] for k in range(per_branch)]
                    closing_ref[branch, patch, piece] = jnp.concatenate(held).astype(jnp.bfloat16)

    @pl.when(section < patches)
    def _():
        finished = [rows_ref[q, own_slice].astype(jnp.float32)[:tok_dev] for q in range(blocks)]
        for branch in range(branches):
            held = jnp.concatenate(finished[branch * per_branch : (branch + 1) * per_branch])
            held = held.astype(jnp.bfloat16)
            for patch in range(patches):
                for piece in range(slices):
                    closing_ref[branch, patch, piece] = held


def start_kernel(latent_ref, *refs):
    refs[-1][...] = latent_ref[0]


def added(parts_ref, section, *streams_refs):
    total = sum(parts_ref[section, piece].astype(jnp.float32) for piece in range(parts_ref.shape[1]))
    for ref in streams_refs:
        total = total + ref[section].astype(jnp.float32)
    return total


def settle_first_kernel(parts_ref, latent_ref, spread_to):
    first = added(parts_ref, 0)
    half_cols = first.shape[1]
    for half in range(2):

        @pl.when(lax.axis_index("pipe") % 2 == half)
        def _():
            at = slice(half * half_cols, (half + 1) * half_cols)
            held = (first + latent_ref[0, :, at].astype(jnp.float32)).astype(jnp.bfloat16)
            for piece in range(parts_ref.shape[1]):
                spread_to[0, piece] = latent_ref[1, :, at]
                spread_to[1, piece] = held


def settle_kernel(parts_ref, *refs):
    *streams_refs, streams_to, spread_to = refs
    count, slices = parts_ref.shape[:2]
    for section in range(count):
        held = added(parts_ref, max(section - 1, 0), *streams_refs).astype(jnp.bfloat16)
        streams_to[section] = held
        for piece in range(slices):
            spread_to[section, piece] = held


def settle_last_kernel(in_group, parts_ref, streams_ref, spread_to):
    count, slices = parts_ref.shape[:2]
    finished = added(parts_ref, count - 1, streams_ref)
    tok_dev = finished.shape[0] // in_group
    last = added(parts_ref, count - 2, streams_ref).astype(jnp.bfloat16)
    for section in range(count):
        held = last
        if section < in_group:
            held = finished[section * tok_dev : (section + 1) * tok_dev]
            held = jnp.concatenate([held] * in_group).astype(jnp.bfloat16)
        for piece in range(slices):
            spread_to[section, piece] = held


def guide_kernel(members, closing_ref, table_ref, guided_ref, table_to, sem):
    copy = pltpu.make_async_copy(table_ref, table_to, sem)
    copy.start()
    branches, patches, slices, block_rows, block_cols = closing_ref.shape
    tok_dev = guided_ref.shape[0]
    section, _, own_slice = position(members)

    def combine(pair):
        conditional, unconditional = pair
        rows = unconditional + GUIDANCE_SCALE * (conditional - unconditional)
        for at in range(block_rows // tok_dev):
            guided_ref[:, at * block_cols : (at + 1) * block_cols] = rows[
                at * tok_dev : (at + 1) * tok_dev
            ].astype(jnp.bfloat16)

    @pl.when(section >= patches)
    def _():
        pair = []
        for branch in range(branches):
            total = 0.0
            for piece in range(slices):
                total = total + closing_ref[branch, patches - 1, piece].astype(jnp.float32)
            pair.append(total.astype(jnp.bfloat16).astype(jnp.float32))
        combine(pair)

    @pl.when(section < patches)
    def _():
        combine(
            [closing_ref[branch, section, own_slice].astype(jnp.float32) for branch in range(branches)]
        )

    copy.wait()


def local(latent, modulation, qkv_weight, out_weight, norm_gain, stale_kv):
    seq_count = lax.axis_size("seq")
    seq_rank = lax.axis_index("seq")
    section_count = lax.axis_size("pipe")
    patches, tok_dev, model_width = latent.shape
    head_dim = norm_gain.shape[2]
    slice_count = min(seq_count, 8)
    member_count = seq_count // slice_count
    member_bits = member_count.bit_length() - 1
    own_member = seq_rank % member_count
    local_width = stale_kv.shape[7]
    group_rows = slice_count * tok_dev
    own_cache = stale_kv[0, 0].reshape(2, patches, group_rows, local_width)
    group_cache = own_cache[None]
    qkv_slice = qkv_weight[0]
    out_slice = out_weight[0]
    for level_index in range(member_bits):
        got_qkv, got_out, got_cache = (
            swapped(qkv_slice, "seq", level_index),
            swapped(out_slice, "seq", level_index),
            swapped(group_cache, "seq", level_index),
        )
        is_upper = own_member >> level_index & 1 == 1
        qkv_slice = join_pair(is_upper, qkv_slice, got_qkv, 1)
        out_slice = join_pair(is_upper, out_slice, got_out, 0)
        group_cache = join_pair(is_upper, group_cache, got_cache, 0)
    homes = section_count * slice_count
    in_group = patches // GROUPS
    block_rows = in_group * tok_dev
    block_cols = model_width // section_count
    rows = slice_count * block_rows
    half = section_count // 2
    groups_of = range(member_count)
    in_slices = [[a + member_count * b for b in range(slice_count)] for a in groups_of]
    peers = [[q * seq_count + at for q in range(section_count) for at in g] for g in in_slices]
    closing_peers = [
        [
            (c * section_count + q) * seq_count + at
            for c in range(2)
            for q in range(h * half, (h + 1) * half)
            for at in g
        ]
        for h in range(2)
        for g in in_slices
    ]

    pair_peers = [
        [q * seq_count + at for q in range(first, first + 2) for at in g]
        for first in range(0, section_count, 2)
        for g in in_slices
    ]

    def exchange(value, among=peers):
        flat = value.reshape((-1,) + value.shape[2:])
        flat = lax.all_to_all(flat, ("pipe", "seq"), 0, 0, axis_index_groups=among)
        return flat.reshape(value.shape)

    vmem = pl.BlockSpec(memory_space=pltpu.VMEM)
    hbm = pl.BlockSpec(memory_space=pltpu.HBM)
    in_hbm = functools.partial(pltpu.with_memory_space_constraint, memory_space=pltpu.HBM)
    in_vmem = functools.partial(pltpu.with_memory_space_constraint, memory_space=pltpu.VMEM)
    sources = latent.reshape(GROUPS, block_rows, model_width)
    stream_shape = (section_count, block_rows, block_cols)
    spread_shape = (section_count, slice_count, block_rows, block_cols)
    pair_shape = (2, slice_count, block_rows, model_width // 2)
    modulation = modulation.reshape(3, 1, model_width)
    norm_gain = norm_gain[0]
    table = own_cache.reshape(2, GROUPS, rows, local_width)
    named = (qkv_slice, out_slice, modulation, norm_gain, table)
    own_rows = pl.pallas_call(
        start_kernel,
        out_shape=jax.ShapeDtypeStruct((block_rows, model_width), jnp.bfloat16),
        in_specs=[vmem] + [hbm] * len(named),
        out_specs=vmem,
        compiler_params=pltpu.CompilerParams(vmem_limit_bytes=4 * 1024 * 1024),
    )(in_vmem(sources), *map(in_hbm, named))
    stale_rows = []
    if member_count > 1:
        stale_rows = [group_cache.swapaxes(0, 1).reshape(2, -1, local_width)]

    def attend(tick, features, table, partial_shape):
        operands = (
            features,
            in_vmem(modulation),
            in_vmem(qkv_slice),
            in_vmem(out_slice),
            in_vmem(norm_gain),
            *stale_rows,
            in_vmem(table),
        )
        return pl.pallas_call(
            functools.partial(section_kernel, tick, (tok_dev, head_dim, member_count)),
            out_shape=(
                jax.ShapeDtypeStruct(partial_shape, jnp.bfloat16),
                jax.ShapeDtypeStruct(table.shape, jnp.bfloat16),
            ),
            in_specs=[vmem] * len(operands),
            out_specs=(vmem, vmem),
            compiler_params=pltpu.CompilerParams(vmem_limit_bytes=24 * 1024 * 1024),
        )(*operands)

    def small(kernel, in_specs, *out_shapes):
        return pl.pallas_call(
            kernel,
            out_shape=tuple(jax.ShapeDtypeStruct(shape, jnp.bfloat16) for shape in out_shapes),
            in_specs=in_specs,
            out_specs=(vmem,) * len(out_shapes),
            compiler_params=pltpu.CompilerParams(vmem_limit_bytes=8 * 1024 * 1024),
        )

    ticks = GROUPS + section_count - 1
    closing_shape = (2, half, slice_count, block_rows, block_cols)
    features = lax.all_gather(own_rows, "seq", axis_index_groups=in_slices)[None]
    partial_out, table = attend(0, features, table, pair_shape)
    parts = exchange(partial_out, pair_peers)
    (spread,) = small(settle_first_kernel, [vmem] * 2, pair_shape)(parts, in_vmem(sources))
    features = exchange(spread, pair_peers)
    streams = []
    for tick in range(1, ticks - 2):
        partial_out, table = attend(tick, features, table, spread_shape)
        held = [exchange(partial_out)] + streams
        stream, spread = small(settle_kernel, [vmem] * len(held), stream_shape, spread_shape)(*held)
        streams = [stream]
        features = exchange(spread)
    partial_out, table = attend(ticks - 2, features, table, spread_shape)
    (spread,) = small(
        functools.partial(settle_last_kernel, in_group), [vmem] * 2, spread_shape
    )(exchange(partial_out), *streams)
    features = exchange(spread)
    closing, table = attend(ticks - 1, features, table, closing_shape)
    closing = lax.all_to_all(
        closing.reshape((-1,) + closing_shape[3:]),
        ("cfg", "pipe", "seq"),
        0,
        0,
        axis_index_groups=closing_peers,
    ).reshape(closing_shape)
    guided, table = pl.pallas_call(
        functools.partial(guide_kernel, member_count),
        out_shape=(
            jax.ShapeDtypeStruct((tok_dev, model_width // 2), jnp.bfloat16),
            jax.ShapeDtypeStruct(table.shape, jnp.bfloat16),
        ),
        in_specs=[vmem, vmem],
        out_specs=(vmem, hbm),
        scratch_shapes=[pltpu.SemaphoreType.DMA],
        compiler_params=pltpu.CompilerParams(vmem_limit_bytes=8 * 1024 * 1024),
    )(closing, table)
    return (guided[None], table.reshape(stale_kv.shape))


def solution(mesh):
    placed = (
        P(None, "seq", None),
        P("pipe", "cfg", None, None),
        P("pipe", None, "seq"),
        P("pipe", "seq", None),
        P("pipe", None, None),
        P("pipe", "cfg", None, None, "seq", None, None, None),
    )
    return jax.shard_map(
        local,
        mesh=mesh,
        in_specs=placed,
        out_specs=(P("pipe", "seq", "cfg"), P("pipe", "cfg", None, None, "seq", None, None, None)),
        check_vma=False,
    )
```

```python
import functools
import math

import jax
import jax.numpy as jnp
from jax import lax
from jax.experimental import pallas as pl
from jax.experimental.pallas import tpu as pltpu
from jax.sharding import PartitionSpec as P

GUIDANCE_SCALE = 6.0
EPSILON = 1e-06
GROUPS = 2


def swapped(value, axis, bit):
    return lax.ppermute(value, axis, [(i, i ^ 1 << bit) for i in range(lax.axis_size(axis))])


def head_norm(values, gain_row):
    return (
        values * lax.rsqrt(jnp.mean(values * values, axis=-1, keepdims=True) + EPSILON) * gain_row
    )


def join_pair(is_upper, mine, theirs, axis_dim):
    return jnp.where(
        is_upper,
        jnp.concatenate((theirs, mine), axis_dim),
        jnp.concatenate((mine, theirs), axis_dim),
    )


def position(members):
    rank = lax.axis_index("seq")
    return lax.axis_index("pipe"), rank % members, rank // members


def section_kernel(tick, sizes, rows_ref, mod_ref, qkv_ref, out_ref, gain_ref, *refs):
    *stale_refs, old_table_ref, partial_ref, table_ref = refs
    closing = len(partial_ref.shape) == 5
    folding = tick == 1
    tok_dev, head_dim, members = sizes
    blocks, slices, block_rows, block_cols = rows_ref.shape
    rows = slices * block_rows
    width = blocks * block_cols
    in_group = block_rows // tok_dev
    group_rows = slices * tok_dev
    groups, local_width = table_ref.shape[1], table_ref.shape[3]
    heads = local_width // head_dim
    section, own_member, own_slice = position(members)
    group = tick - section
    parts = [rows_ref[q].reshape(rows, block_cols).astype(jnp.float32) for q in range(blocks)]
    mean = jnp.sum(sum(parts), axis=-1, keepdims=True) * (1.0 / width)
    parts = [x - mean for x in parts]
    spread = jnp.sum(sum(x * x for x in parts), axis=-1, keepdims=True) * (1.0 / width)
    inverse = lax.rsqrt(spread + EPSILON)
    modulated = []
    for q, x in enumerate(parts):
        at = slice(q * block_cols, (q + 1) * block_cols)
        modulated.append(
            (x * inverse * (1.0 + mod_ref[1, :, at]) + mod_ref[0, :, at]).astype(jnp.bfloat16)
        )
    modulated = jnp.concatenate(modulated, axis=1)
    mixed = jnp.dot(modulated, qkv_ref[...], preferred_element_type=jnp.float32)

    def stacked(kind):
        at = [(3 * head + kind) * head_dim for head in range(heads)]
        return jnp.stack([mixed[:, start : start + head_dim] for start in at])

    def by_patch(values):
        values = values.reshape(heads, slices, in_group, tok_dev, head_dim).swapaxes(1, 2)
        return values.reshape(heads, rows, head_dim).astype(jnp.bfloat16)

    def query_patch(shape):
        return lax.broadcasted_iota(jnp.int32, shape, 0) // tok_dev % in_group

    fresh_shape, old_shape = (rows, rows), (rows, groups * rows)
    fresh_patch = lax.broadcasted_iota(jnp.int32, fresh_shape, 1) // group_rows
    old_patch = lax.broadcasted_iota(jnp.int32, old_shape, 1) // group_rows - group * in_group
    masks = [
        (fresh_patch <= query_patch(fresh_shape)).astype(jnp.float32),
        jnp.logical_or(old_patch < 0, old_patch > query_patch(old_shape)).astype(jnp.float32),
    ]
    for ref in stale_refs:
        at = lax.broadcasted_iota(jnp.int32, (rows, ref.shape[1]), 1)
        masks.append((at // (groups * rows) != own_member).astype(jnp.float32))
    mask = jnp.concatenate(masks, axis=1)

    queries = head_norm(stacked(0), gain_ref[0:1, :]).astype(jnp.bfloat16)
    fresh = (by_patch(head_norm(stacked(1), gain_ref[1:2, :])), by_patch(stacked(2)))

    def entries(head, kind):
        at = slice(head * head_dim, (head + 1) * head_dim)
        old = old_table_ref[kind, :, :, at].reshape(groups * rows, head_dim)
        return jnp.concatenate([fresh[kind][head], old] + [ref[kind, :, at] for ref in stale_refs])

    scores = [
        lax.dot_general(
            queries[head],
            entries(head, 0),
            (((1,), (1,)), ((), ())),
            preferred_element_type=jnp.float32,
        )
        for head in range(heads)
    ]
    weights = mask[None] * jnp.exp(jnp.stack(scores) * (1.0 / math.sqrt(head_dim)))
    inverse = 1.0 / jnp.sum(weights, axis=-1, keepdims=True)
    weights = weights.astype(jnp.bfloat16)
    summed = [
        jnp.dot(weights[head], entries(head, 1), preferred_element_type=jnp.float32)
        for head in range(heads)
    ]
    attended = (jnp.stack(summed) * inverse).astype(jnp.bfloat16)
    attended = jnp.concatenate([attended[head] for head in range(heads)], axis=1)

    projected = jnp.dot(attended, out_ref[...], preferred_element_type=jnp.float32)
    projected = mod_ref[2] * projected
    if folding:
        at_slice = lax.broadcasted_iota(jnp.int32, (rows, 1), 0) // block_rows
        own = (at_slice == own_slice).astype(jnp.float32)
        projected = projected + own * jnp.concatenate(
            [rows_ref[q].reshape(rows, block_cols).astype(jnp.float32) for q in range(blocks)],
            axis=1,
        )
    if closing:
        close_into(partial_ref, projected, rows_ref, section, own_slice, in_group)
    else:
        out_cols = partial_ref.shape[3]
        for q in range(partial_ref.shape[0]):
            piece = projected[:, q * out_cols : (q + 1) * out_cols].astype(jnp.bfloat16)
            partial_ref[q] = piece.reshape(slices, block_rows, out_cols)

    for kind in range(2):
        rows_of = jnp.concatenate([fresh[kind][head] for head in range(heads)], axis=1)
        for at in range(groups):
            table_ref[kind, at] = jnp.where(group == at, rows_of, old_table_ref[kind, at])


def close_into(closing_ref, projected, rows_ref, section, own_slice, in_group):
    branches, patches, slices = closing_ref.shape[:3]
    blocks, _, block_rows, block_cols = rows_ref.shape
    tok_dev = block_rows // in_group
    per_branch = blocks // branches

    @pl.when(section >= patches)
    def _():
        for piece in range(slices):
            own = (own_slice == piece).astype(jnp.float32)
            by_block = []
            for q in range(blocks):
                rows = projected[
                    piece * block_rows : (piece + 1) * block_rows,
                    q * block_cols : (q + 1) * block_cols,
                ]
                rows = rows + own * rows_ref[q, piece].astype(jnp.float32)
                by_block.append(rows.reshape(in_group, tok_dev, block_cols))
            for branch in range(branches):
                for patch in range(patches):
                    held = [by_block[branch * per_branch + k][patch] for k in range(per_branch)]
                    closing_ref[branch, patch, piece] = jnp.concatenate(held).astype(jnp.bfloat16)

    @pl.when(section < patches)
    def _():
        finished = [rows_ref[q, own_slice].astype(jnp.float32)[:tok_dev] for q in range(blocks)]
        for branch in range(branches):
            held = jnp.concatenate(finished[branch * per_branch : (branch + 1) * per_branch])
            held = held.astype(jnp.bfloat16)
            for patch in range(patches):
                for piece in range(slices):
                    closing_ref[branch, patch, piece] = held


def start_kernel(latent_ref, *refs):
    spread_to = refs[-1]
    for piece in range(spread_to.shape[0]):
        spread_to[piece] = latent_ref[...]


def added(parts_ref, section, *streams_refs):
    total = sum(parts_ref[section, piece].astype(jnp.float32) for piece in range(parts_ref.shape[1]))
    for ref in streams_refs:
        total = total + ref[section].astype(jnp.float32)
    return total


def settle_first_kernel(parts_ref, latent_ref, spread_to):
    first = added(parts_ref, 0)
    half_cols = first.shape[1]
    for half in range(2):

        @pl.when(lax.axis_index("pipe") % 2 == half)
        def _():
            at = slice(half * half_cols, (half + 1) * half_cols)
            held = (first + latent_ref[0, :, at].astype(jnp.float32)).astype(jnp.bfloat16)
            for piece in range(parts_ref.shape[1]):
                spread_to[0, piece] = latent_ref[1, :, at]
                spread_to[1, piece] = held


def settle_kernel(parts_ref, *refs):
    *streams_refs, streams_to, spread_to = refs
    count, slices = parts_ref.shape[:2]
    for section in range(count):
        held = added(parts_ref, max(section - 1, 0), *streams_refs).astype(jnp.bfloat16)
        streams_to[section] = held
        for piece in range(slices):
            spread_to[section, piece] = held


def settle_last_kernel(in_group, parts_ref, streams_ref, spread_to):
    count, slices = parts_ref.shape[:2]
    finished = added(parts_ref, count - 1, streams_ref)
    tok_dev = finished.shape[0] // in_group
    last = added(parts_ref, count - 2, streams_ref).astype(jnp.bfloat16)
    for section in range(count):
        held = last
        if section < in_group:
            held = finished[section * tok_dev : (section + 1) * tok_dev]
            held = jnp.concatenate([held] * in_group).astype(jnp.bfloat16)
        for piece in range(slices):
            spread_to[section, piece] = held


def guide_kernel(members, closing_ref, table_ref, guided_ref, table_to, sem):
    copy = pltpu.make_async_copy(table_ref, table_to, sem)
    copy.start()
    branches, patches, slices, block_rows, block_cols = closing_ref.shape
    tok_dev = guided_ref.shape[0]
    section, _, own_slice = position(members)

    def combine(pair):
        conditional, unconditional = pair
        rows = unconditional + GUIDANCE_SCALE * (conditional - unconditional)
        for at in range(block_rows // tok_dev):
            guided_ref[:, at * block_cols : (at + 1) * block_cols] = rows[
                at * tok_dev : (at + 1) * tok_dev
            ].astype(jnp.bfloat16)

    @pl.when(section >= patches)
    def _():
        pair = []
        for branch in range(branches):
            total = 0.0
            for piece in range(slices):
                total = total + closing_ref[branch, patches - 1, piece].astype(jnp.float32)
            pair.append(total.astype(jnp.bfloat16).astype(jnp.float32))
        combine(pair)

    @pl.when(section < patches)
    def _():
        combine(
            [closing_ref[branch, section, own_slice].astype(jnp.float32) for branch in range(branches)]
        )

    copy.wait()


def local(latent, modulation, qkv_weight, out_weight, norm_gain, stale_kv):
    seq_count = lax.axis_size("seq")
    seq_rank = lax.axis_index("seq")
    section_count = lax.axis_size("pipe")
    patches, tok_dev, model_width = latent.shape
    head_dim = norm_gain.shape[2]
    slice_count = min(seq_count, 8)
    member_count = seq_count // slice_count
    member_bits = member_count.bit_length() - 1
    own_member = seq_rank % member_count
    local_width = stale_kv.shape[7]
    group_rows = slice_count * tok_dev
    own_cache = stale_kv[0, 0].reshape(2, patches, group_rows, local_width)
    group_cache = own_cache[None]
    qkv_slice = qkv_weight[0]
    out_slice = out_weight[0]
    for level_index in range(member_bits):
        got_qkv, got_out, got_cache = (
            swapped(qkv_slice, "seq", level_index),
            swapped(out_slice, "seq", level_index),
            swapped(group_cache, "seq", level_index),
        )
        is_upper = own_member >> level_index & 1 == 1
        qkv_slice = join_pair(is_upper, qkv_slice, got_qkv, 1)
        out_slice = join_pair(is_upper, out_slice, got_out, 0)
        group_cache = join_pair(is_upper, group_cache, got_cache, 0)
    homes = section_count * slice_count
    in_group = patches // GROUPS
    block_rows = in_group * tok_dev
    block_cols = model_width // section_count
    rows = slice_count * block_rows
    half = section_count // 2
    groups_of = range(member_count)
    in_slices = [[a + member_count * b for b in range(slice_count)] for a in groups_of]
    peers = [[q * seq_count + at for q in range(section_count) for at in g] for g in in_slices]
    closing_peers = [
        [
            (c * section_count + q) * seq_count + at
            for c in range(2)
            for q in range(h * half, (h + 1) * half)
            for at in g
        ]
        for h in range(2)
        for g in in_slices
    ]

    pair_peers = [
        [q * seq_count + at for q in range(first, first + 2) for at in g]
        for first in range(0, section_count, 2)
        for g in in_slices
    ]

    def exchange(value, among=peers):
        flat = value.reshape((-1,) + value.shape[2:])
        flat = lax.all_to_all(flat, ("pipe", "seq"), 0, 0, axis_index_groups=among)
        return flat.reshape(value.shape)

    vmem = pl.BlockSpec(memory_space=pltpu.VMEM)
    hbm = pl.BlockSpec(memory_space=pltpu.HBM)
    in_hbm = functools.partial(pltpu.with_memory_space_constraint, memory_space=pltpu.HBM)
    in_vmem = functools.partial(pltpu.with_memory_space_constraint, memory_space=pltpu.VMEM)
    sources = latent.reshape(GROUPS, block_rows, model_width)
    stream_shape = (section_count, block_rows, block_cols)
    spread_shape = (section_count, slice_count, block_rows, block_cols)
    modulation = modulation.reshape(3, 1, model_width)
    norm_gain = norm_gain[0]
    table = own_cache.reshape(2, GROUPS, rows, local_width)
    named = (qkv_slice, out_slice, modulation, norm_gain, table, sources)
    spread = pl.pallas_call(
        start_kernel,
        out_shape=jax.ShapeDtypeStruct((slice_count, block_rows, model_width), jnp.bfloat16),
        in_specs=[vmem] + [hbm] * len(named),
        out_specs=vmem,
        compiler_params=pltpu.CompilerParams(vmem_limit_bytes=4 * 1024 * 1024),
    )(sources[0], *map(in_hbm, named))
    stale_rows = []
    if member_count > 1:
        stale_rows = [group_cache.swapaxes(0, 1).reshape(2, -1, local_width)]

    def attend(tick, features, table, partial_shape):
        operands = (
            features,
            in_vmem(modulation),
            in_vmem(qkv_slice),
            in_vmem(out_slice),
            in_vmem(norm_gain),
            *stale_rows,
            in_vmem(table),
        )
        return pl.pallas_call(
            functools.partial(section_kernel, tick, (tok_dev, head_dim, member_count)),
            out_shape=(
                jax.ShapeDtypeStruct(partial_shape, jnp.bfloat16),
                jax.ShapeDtypeStruct(table.shape, jnp.bfloat16),
            ),
            in_specs=[vmem] * len(operands),
            out_specs=(vmem, vmem),
            compiler_params=pltpu.CompilerParams(vmem_limit_bytes=24 * 1024 * 1024),
        )(*operands)

    def small(kernel, in_specs, *out_shapes):
        return pl.pallas_call(
            kernel,
            out_shape=tuple(jax.ShapeDtypeStruct(shape, jnp.bfloat16) for shape in out_shapes),
            in_specs=in_specs,
            out_specs=(vmem,) * len(out_shapes),
            compiler_params=pltpu.CompilerParams(vmem_limit_bytes=8 * 1024 * 1024),
        )

    ticks = GROUPS + section_count - 1
    closing_shape = (2, half, slice_count, block_rows, block_cols)
    features = lax.all_to_all(spread, "seq", 0, 0, axis_index_groups=in_slices)[None]
    pair_shape = (2, slice_count, block_rows, model_width // 2)
    partial_out, table = attend(0, features, table, pair_shape)
    parts = exchange(partial_out, pair_peers)
    (spread,) = small(settle_first_kernel, [vmem] * 2, pair_shape)(parts, in_vmem(sources))
    features = exchange(spread, pair_peers)
    streams = []
    for tick in range(1, ticks - 2):
        partial_out, table = attend(tick, features, table, spread_shape)
        held = [exchange(partial_out)] + streams
        stream, spread = small(settle_kernel, [vmem] * len(held), stream_shape, spread_shape)(*held)
        streams = [stream]
        features = exchange(spread)
    partial_out, table = attend(ticks - 2, features, table, spread_shape)
    (spread,) = small(
        functools.partial(settle_last_kernel, in_group), [vmem] * 2, spread_shape
    )(exchange(partial_out), *streams)
    features = exchange(spread)
    closing, table = attend(ticks - 1, features, table, closing_shape)
    closing = lax.all_to_all(
        closing.reshape((-1,) + closing_shape[3:]),
        ("cfg", "pipe", "seq"),
        0,
        0,
        axis_index_groups=closing_peers,
    ).reshape(closing_shape)
    guided, table = pl.pallas_call(
        functools.partial(guide_kernel, member_count),
        out_shape=(
            jax.ShapeDtypeStruct((tok_dev, model_width // 2), jnp.bfloat16),
            jax.ShapeDtypeStruct(table.shape, jnp.bfloat16),
        ),
        in_specs=[vmem, vmem],
        out_specs=(vmem, hbm),
        scratch_shapes=[pltpu.SemaphoreType.DMA],
        compiler_params=pltpu.CompilerParams(vmem_limit_bytes=8 * 1024 * 1024),
    )(closing, table)
    return (guided[None], table.reshape(stale_kv.shape))


def solution(mesh):
    placed = (
        P(None, "seq", None),
        P("pipe", "cfg", None, None),
        P("pipe", None, "seq"),
        P("pipe", "seq", None),
        P("pipe", None, None),
        P("pipe", "cfg", None, None, "seq", None, None, None),
    )
    return jax.shard_map(
        local,
        mesh=mesh,
        in_specs=placed,
        out_specs=(P("pipe", "seq", "cfg"), P("pipe", "cfg", None, None, "seq", None, None, None)),
        check_vma=False,
    )
```

```python
import functools
import math

import jax
import jax.numpy as jnp
from jax import lax
from jax.experimental import pallas as pl
from jax.experimental.pallas import tpu as pltpu
from jax.sharding import PartitionSpec as P

GUIDANCE_SCALE = 6.0
EPSILON = 1e-06
GROUPS = 2


def swapped(value, axis, bit):
    return lax.ppermute(value, axis, [(i, i ^ 1 << bit) for i in range(lax.axis_size(axis))])


def head_norm(values, gain_row):
    return (
        values * lax.rsqrt(jnp.mean(values * values, axis=-1, keepdims=True) + EPSILON) * gain_row
    )


def join_pair(is_upper, mine, theirs, axis_dim):
    return jnp.where(
        is_upper,
        jnp.concatenate((theirs, mine), axis_dim),
        jnp.concatenate((mine, theirs), axis_dim),
    )


def position(members):
    rank = lax.axis_index("seq")
    return lax.axis_index("pipe"), rank % members, rank // members


def section_kernel(tick, sizes, rows_ref, mod_ref, qkv_ref, out_ref, gain_ref, *refs):
    *stale_refs, old_table_ref, partial_ref, table_ref = refs
    closing = len(partial_ref.shape) == 5
    folding = tick == 1
    tok_dev, head_dim, members = sizes
    slices, blocks, block_rows, block_cols = rows_ref.shape
    rows = slices * block_rows
    width = blocks * block_cols
    in_group = block_rows // tok_dev
    group_rows = slices * tok_dev
    groups, local_width = table_ref.shape[1], table_ref.shape[3]
    heads = local_width // head_dim
    section, own_member, own_slice = position(members)
    group = tick - section
    parts = [rows_ref[:, q].reshape(rows, block_cols).astype(jnp.float32) for q in range(blocks)]
    mean = jnp.sum(sum(parts), axis=-1, keepdims=True) * (1.0 / width)
    parts = [x - mean for x in parts]
    spread = jnp.sum(sum(x * x for x in parts), axis=-1, keepdims=True) * (1.0 / width)
    inverse = lax.rsqrt(spread + EPSILON)
    modulated = []
    for q, x in enumerate(parts):
        at = slice(q * block_cols, (q + 1) * block_cols)
        modulated.append(
            (x * inverse * (1.0 + mod_ref[1, :, at]) + mod_ref[0, :, at]).astype(jnp.bfloat16)
        )
    modulated = jnp.concatenate(modulated, axis=1)
    mixed = jnp.dot(modulated, qkv_ref[...], preferred_element_type=jnp.float32)

    def stacked(kind):
        at = [(3 * head + kind) * head_dim for head in range(heads)]
        return jnp.stack([mixed[:, start : start + head_dim] for start in at])

    def by_patch(values):
        values = values.reshape(heads, slices, in_group, tok_dev, head_dim).swapaxes(1, 2)
        return values.reshape(heads, rows, head_dim).astype(jnp.bfloat16)

    def query_patch(shape):
        return lax.broadcasted_iota(jnp.int32, shape, 0) // tok_dev % in_group

    fresh_shape, old_shape = (rows, rows), (rows, groups * rows)
    fresh_patch = lax.broadcasted_iota(jnp.int32, fresh_shape, 1) // group_rows
    old_patch = lax.broadcasted_iota(jnp.int32, old_shape, 1) // group_rows - group * in_group
    masks = [
        (fresh_patch <= query_patch(fresh_shape)).astype(jnp.float32),
        jnp.logical_or(old_patch < 0, old_patch > query_patch(old_shape)).astype(jnp.float32),
    ]
    for ref in stale_refs:
        at = lax.broadcasted_iota(jnp.int32, (rows, ref.shape[1]), 1)
        masks.append((at // (groups * rows) != own_member).astype(jnp.float32))
    mask = jnp.concatenate(masks, axis=1)

    queries = head_norm(stacked(0), gain_ref[0:1, :]).astype(jnp.bfloat16)
    fresh = (by_patch(head_norm(stacked(1), gain_ref[1:2, :])), by_patch(stacked(2)))

    def entries(head, kind):
        at = slice(head * head_dim, (head + 1) * head_dim)
        old = old_table_ref[kind, :, :, at].reshape(groups * rows, head_dim)
        return jnp.concatenate([fresh[kind][head], old] + [ref[kind, :, at] for ref in stale_refs])

    scores = [
        lax.dot_general(
            queries[head],
            entries(head, 0),
            (((1,), (1,)), ((), ())),
            preferred_element_type=jnp.float32,
        )
        for head in range(heads)
    ]
    weights = mask[None] * jnp.exp(jnp.stack(scores) * (1.0 / math.sqrt(head_dim)))
    inverse = 1.0 / jnp.sum(weights, axis=-1, keepdims=True)
    weights = weights.astype(jnp.bfloat16)
    summed = [
        jnp.dot(weights[head], entries(head, 1), preferred_element_type=jnp.float32)
        for head in range(heads)
    ]
    attended = (jnp.stack(summed) * inverse).astype(jnp.bfloat16)
    attended = jnp.concatenate([attended[head] for head in range(heads)], axis=1)

    projected = jnp.dot(attended, out_ref[...], preferred_element_type=jnp.float32)
    projected = mod_ref[2] * projected
    if folding:
        at_slice = lax.broadcasted_iota(jnp.int32, (rows, 1), 0) // block_rows
        own = (at_slice == own_slice).astype(jnp.float32)
        projected = projected + own * jnp.concatenate(
            [rows_ref[:, q].reshape(rows, block_cols).astype(jnp.float32) for q in range(blocks)],
            axis=1,
        )
    if closing:
        close_into(partial_ref, projected, rows_ref, section, own_slice, in_group)
    else:
        out_cols = partial_ref.shape[3]
        for q in range(partial_ref.shape[1]):
            piece = projected[:, q * out_cols : (q + 1) * out_cols].astype(jnp.bfloat16)
            partial_ref[:, q] = piece.reshape(slices, block_rows, out_cols)

    for kind in range(2):
        rows_of = jnp.concatenate([fresh[kind][head] for head in range(heads)], axis=1)
        for at in range(groups):
            table_ref[kind, at] = jnp.where(group == at, rows_of, old_table_ref[kind, at])


def close_into(closing_ref, projected, rows_ref, section, own_slice, in_group):
    branches, patches, slices = closing_ref.shape[:3]
    _, blocks, block_rows, block_cols = rows_ref.shape
    tok_dev = block_rows // in_group
    per_branch = blocks // branches

    @pl.when(section >= patches)
    def _():
        for piece in range(slices):
            own = (own_slice == piece).astype(jnp.float32)
            by_block = []
            for q in range(blocks):
                rows = projected[
                    piece * block_rows : (piece + 1) * block_rows,
                    q * block_cols : (q + 1) * block_cols,
                ]
                rows = rows + own * rows_ref[piece, q].astype(jnp.float32)
                by_block.append(rows.reshape(in_group, tok_dev, block_cols))
            for branch in range(branches):
                for patch in range(patches):
                    held = [by_block[branch * per_branch + k][patch] for k in range(per_branch)]
                    closing_ref[branch, patch, piece] = jnp.concatenate(held).astype(jnp.bfloat16)

    @pl.when(section < patches)
    def _():
        finished = [rows_ref[own_slice, q].astype(jnp.float32)[:tok_dev] for q in range(blocks)]
        for branch in range(branches):
            held = jnp.concatenate(finished[branch * per_branch : (branch + 1) * per_branch])
            held = held.astype(jnp.bfloat16)
            for patch in range(patches):
                for piece in range(slices):
                    closing_ref[branch, patch, piece] = held


def start_kernel(latent_ref, *refs):
    spread_to = refs[-1]
    for piece in range(spread_to.shape[0]):
        spread_to[piece] = latent_ref[...]


def added(parts_ref, section, *streams_refs):
    total = sum(parts_ref[piece, section].astype(jnp.float32) for piece in range(parts_ref.shape[0]))
    for ref in streams_refs:
        total = total + ref[section].astype(jnp.float32)
    return total


def settle_first_kernel(parts_ref, latent_ref, spread_to):
    first = added(parts_ref, 0)
    half_cols = first.shape[1]
    for half in range(2):

        @pl.when(lax.axis_index("pipe") % 2 == half)
        def _():
            at = slice(half * half_cols, (half + 1) * half_cols)
            held = (first + latent_ref[0, :, at].astype(jnp.float32)).astype(jnp.bfloat16)
            for piece in range(parts_ref.shape[0]):
                spread_to[piece, 0] = latent_ref[1, :, at]
                spread_to[piece, 1] = held


def settle_kernel(parts_ref, *refs):
    *streams_refs, streams_to, spread_to = refs
    slices, count = parts_ref.shape[:2]
    for section in range(count):
        held = added(parts_ref, max(section - 1, 0), *streams_refs).astype(jnp.bfloat16)
        streams_to[section] = held
        for piece in range(slices):
            spread_to[piece, section] = held


def settle_last_kernel(in_group, parts_ref, streams_ref, spread_to):
    slices, count = parts_ref.shape[:2]
    finished = added(parts_ref, count - 1, streams_ref)
    tok_dev = finished.shape[0] // in_group
    last = added(parts_ref, count - 2, streams_ref).astype(jnp.bfloat16)
    for section in range(count):
        held = last
        if section < in_group:
            held = finished[section * tok_dev : (section + 1) * tok_dev]
            held = jnp.concatenate([held] * in_group).astype(jnp.bfloat16)
        for piece in range(slices):
            spread_to[piece, section] = held


def guide_kernel(members, closing_ref, table_ref, guided_ref, table_to, sem):
    copy = pltpu.make_async_copy(table_ref, table_to, sem)
    copy.start()
    branches, patches, slices, block_rows, block_cols = closing_ref.shape
    tok_dev = guided_ref.shape[0]
    section, _, own_slice = position(members)

    def combine(pair):
        conditional, unconditional = pair
        rows = unconditional + GUIDANCE_SCALE * (conditional - unconditional)
        for at in range(block_rows // tok_dev):
            guided_ref[:, at * block_cols : (at + 1) * block_cols] = rows[
                at * tok_dev : (at + 1) * tok_dev
            ].astype(jnp.bfloat16)

    @pl.when(section >= patches)
    def _():
        pair = []
        for branch in range(branches):
            total = 0.0
            for piece in range(slices):
                total = total + closing_ref[branch, patches - 1, piece].astype(jnp.float32)
            pair.append(total.astype(jnp.bfloat16).astype(jnp.float32))
        combine(pair)

    @pl.when(section < patches)
    def _():
        combine(
            [closing_ref[branch, section, own_slice].astype(jnp.float32) for branch in range(branches)]
        )

    copy.wait()


def local(latent, modulation, qkv_weight, out_weight, norm_gain, stale_kv):
    seq_count = lax.axis_size("seq")
    seq_rank = lax.axis_index("seq")
    section_count = lax.axis_size("pipe")
    patches, tok_dev, model_width = latent.shape
    head_dim = norm_gain.shape[2]
    slice_count = min(seq_count, 8)
    member_count = seq_count // slice_count
    member_bits = member_count.bit_length() - 1
    own_member = seq_rank % member_count
    local_width = stale_kv.shape[7]
    group_rows = slice_count * tok_dev
    own_cache = stale_kv[0, 0].reshape(2, patches, group_rows, local_width)
    group_cache = own_cache[None]
    qkv_slice = qkv_weight[0]
    out_slice = out_weight[0]
    for level_index in range(member_bits):
        got_qkv, got_out, got_cache = (
            swapped(qkv_slice, "seq", level_index),
            swapped(out_slice, "seq", level_index),
            swapped(group_cache, "seq", level_index),
        )
        is_upper = own_member >> level_index & 1 == 1
        qkv_slice = join_pair(is_upper, qkv_slice, got_qkv, 1)
        out_slice = join_pair(is_upper, out_slice, got_out, 0)
        group_cache = join_pair(is_upper, group_cache, got_cache, 0)
    homes = section_count * slice_count
    in_group = patches // GROUPS
    block_rows = in_group * tok_dev
    block_cols = model_width // section_count
    rows = slice_count * block_rows
    half = section_count // 2
    groups_of = range(member_count)
    in_slices = [[a + member_count * b for b in range(slice_count)] for a in groups_of]
    peers = [[q * seq_count + at for at in g for q in range(section_count)] for g in in_slices]
    closing_peers = [
        [
            (c * section_count + q) * seq_count + at
            for c in range(2)
            for q in range(h * half, (h + 1) * half)
            for at in g
        ]
        for h in range(2)
        for g in in_slices
    ]

    pair_peers = [
        [q * seq_count + at for at in g for q in range(first, first + 2)]
        for first in range(0, section_count, 2)
        for g in in_slices
    ]

    def exchange(value, among=peers):
        flat = value.reshape((-1,) + value.shape[2:])
        flat = lax.all_to_all(flat, ("pipe", "seq"), 0, 0, axis_index_groups=among)
        return flat.reshape(value.shape)

    vmem = pl.BlockSpec(memory_space=pltpu.VMEM)
    hbm = pl.BlockSpec(memory_space=pltpu.HBM)
    in_hbm = functools.partial(pltpu.with_memory_space_constraint, memory_space=pltpu.HBM)
    in_vmem = functools.partial(pltpu.with_memory_space_constraint, memory_space=pltpu.VMEM)
    sources = latent.reshape(GROUPS, block_rows, model_width)
    stream_shape = (section_count, block_rows, block_cols)
    spread_shape = (slice_count, section_count, block_rows, block_cols)
    modulation = modulation.reshape(3, 1, model_width)
    norm_gain = norm_gain[0]
    table = own_cache.reshape(2, GROUPS, rows, local_width)
    named = (qkv_slice, out_slice, modulation, norm_gain, table, sources)
    spread = pl.pallas_call(
        start_kernel,
        out_shape=jax.ShapeDtypeStruct((slice_count, block_rows, model_width), jnp.bfloat16),
        in_specs=[vmem] + [hbm] * len(named),
        out_specs=vmem,
        compiler_params=pltpu.CompilerParams(vmem_limit_bytes=4 * 1024 * 1024),
    )(sources[0], *map(in_hbm, named))
    stale_rows = []
    if member_count > 1:
        stale_rows = [group_cache.swapaxes(0, 1).reshape(2, -1, local_width)]

    def attend(tick, features, table, partial_shape):
        operands = (
            features,
            in_vmem(modulation),
            in_vmem(qkv_slice),
            in_vmem(out_slice),
            in_vmem(norm_gain),
            *stale_rows,
            in_vmem(table),
        )
        return pl.pallas_call(
            functools.partial(section_kernel, tick, (tok_dev, head_dim, member_count)),
            out_shape=(
                jax.ShapeDtypeStruct(partial_shape, jnp.bfloat16),
                jax.ShapeDtypeStruct(table.shape, jnp.bfloat16),
            ),
            in_specs=[vmem] * len(operands),
            out_specs=(vmem, vmem),
            compiler_params=pltpu.CompilerParams(vmem_limit_bytes=24 * 1024 * 1024),
        )(*operands)

    def small(kernel, in_specs, *out_shapes):
        return pl.pallas_call(
            kernel,
            out_shape=tuple(jax.ShapeDtypeStruct(shape, jnp.bfloat16) for shape in out_shapes),
            in_specs=in_specs,
            out_specs=(vmem,) * len(out_shapes),
            compiler_params=pltpu.CompilerParams(vmem_limit_bytes=8 * 1024 * 1024),
        )

    ticks = GROUPS + section_count - 1
    closing_shape = (2, half, slice_count, block_rows, block_cols)
    features = lax.all_to_all(spread, "seq", 0, 0, axis_index_groups=in_slices)[:, None]
    pair_shape = (slice_count, 2, block_rows, model_width // 2)
    partial_out, table = attend(0, features, table, pair_shape)
    parts = exchange(partial_out, pair_peers)
    (spread,) = small(settle_first_kernel, [vmem] * 2, pair_shape)(parts, in_vmem(sources))
    features = exchange(spread, pair_peers)
    streams = []
    for tick in range(1, ticks - 2):
        partial_out, table = attend(tick, features, table, spread_shape)
        held = [exchange(partial_out)] + streams
        stream, spread = small(settle_kernel, [vmem] * len(held), stream_shape, spread_shape)(*held)
        streams = [stream]
        features = exchange(spread)
    partial_out, table = attend(ticks - 2, features, table, spread_shape)
    (spread,) = small(
        functools.partial(settle_last_kernel, in_group), [vmem] * 2, spread_shape
    )(exchange(partial_out), *streams)
    features = exchange(spread)
    closing, table = attend(ticks - 1, features, table, closing_shape)
    closing = lax.all_to_all(
        closing.reshape((-1,) + closing_shape[3:]),
        ("cfg", "pipe", "seq"),
        0,
        0,
        axis_index_groups=closing_peers,
    ).reshape(closing_shape)
    guided, table = pl.pallas_call(
        functools.partial(guide_kernel, member_count),
        out_shape=(
            jax.ShapeDtypeStruct((tok_dev, model_width // 2), jnp.bfloat16),
            jax.ShapeDtypeStruct(table.shape, jnp.bfloat16),
        ),
        in_specs=[vmem, vmem],
        out_specs=(vmem, hbm),
        scratch_shapes=[pltpu.SemaphoreType.DMA],
        compiler_params=pltpu.CompilerParams(vmem_limit_bytes=8 * 1024 * 1024),
    )(closing, table)
    return (guided[None], table.reshape(stale_kv.shape))


def solution(mesh):
    placed = (
        P(None, "seq", None),
        P("pipe", "cfg", None, None),
        P("pipe", None, "seq"),
        P("pipe", "seq", None),
        P("pipe", None, None),
        P("pipe", "cfg", None, None, "seq", None, None, None),
    )
    return jax.shard_map(
        local,
        mesh=mesh,
        in_specs=placed,
        out_specs=(P("pipe", "seq", "cfg"), P("pipe", "cfg", None, None, "seq", None, None, None)),
        check_vma=False,
    )
```

```python
import functools
import math

import jax
import jax.numpy as jnp
from jax import lax
from jax.experimental import pallas as pl
from jax.experimental.pallas import tpu as pltpu
from jax.sharding import PartitionSpec as P

GUIDANCE_SCALE = 6.0
EPSILON = 1e-06
GROUPS = 2


def swapped(value, axis, bit):
    return lax.ppermute(value, axis, [(i, i ^ 1 << bit) for i in range(lax.axis_size(axis))])


def head_norm(values, gain_row):
    return (
        values * lax.rsqrt(jnp.mean(values * values, axis=-1, keepdims=True) + EPSILON) * gain_row
    )


def join_pair(is_upper, mine, theirs, axis_dim):
    return jnp.where(
        is_upper,
        jnp.concatenate((theirs, mine), axis_dim),
        jnp.concatenate((mine, theirs), axis_dim),
    )


def position(members):
    rank = lax.axis_index("seq")
    return lax.axis_index("pipe"), rank % members, rank // members


def section_kernel(tick, sizes, rows_ref, mod_ref, qkv_ref, out_ref, gain_ref, *refs):
    *stale_refs, old_table_ref, partial_ref, table_ref = refs
    closing = len(partial_ref.shape) == 5
    folding = tick == 1
    tok_dev, head_dim, members = sizes
    blocks, slices, block_rows, block_cols = rows_ref.shape
    rows = slices * block_rows
    width = blocks * block_cols
    in_group = block_rows // tok_dev
    group_rows = slices * tok_dev
    groups, local_width = table_ref.shape[1], table_ref.shape[3]
    heads = local_width // head_dim
    section, own_member, own_slice = position(members)
    group = tick - section
    parts = [rows_ref[q].reshape(rows, block_cols).astype(jnp.float32) for q in range(blocks)]
    mean = jnp.sum(sum(parts), axis=-1, keepdims=True) * (1.0 / width)
    parts = [x - mean for x in parts]
    spread = jnp.sum(sum(x * x for x in parts), axis=-1, keepdims=True) * (1.0 / width)
    inverse = lax.rsqrt(spread + EPSILON)
    modulated = []
    for q, x in enumerate(parts):
        at = slice(q * block_cols, (q + 1) * block_cols)
        modulated.append(
            (x * inverse * (1.0 + mod_ref[1, :, at]) + mod_ref[0, :, at]).astype(jnp.bfloat16)
        )
    modulated = jnp.concatenate(modulated, axis=1)
    mixed = jnp.dot(modulated, qkv_ref[...], preferred_element_type=jnp.float32)

    def stacked(kind):
        at = [(3 * head + kind) * head_dim for head in range(heads)]
        return jnp.stack([mixed[:, start : start + head_dim] for start in at])

    def by_patch(values):
        values = values.reshape(heads, slices, in_group, tok_dev, head_dim).swapaxes(1, 2)
        return values.reshape(heads, rows, head_dim).astype(jnp.bfloat16)

    def query_patch(shape):
        return lax.broadcasted_iota(jnp.int32, shape, 0) // tok_dev % in_group

    fresh_shape, old_shape = (rows, rows), (rows, groups * rows)
    fresh_patch = lax.broadcasted_iota(jnp.int32, fresh_shape, 1) // group_rows
    old_patch = lax.broadcasted_iota(jnp.int32, old_shape, 1) // group_rows - group * in_group
    masks = [
        (fresh_patch <= query_patch(fresh_shape)).astype(jnp.float32),
        jnp.logical_or(old_patch < 0, old_patch > query_patch(old_shape)).astype(jnp.float32),
    ]
    for ref in stale_refs:
        at = lax.broadcasted_iota(jnp.int32, (rows, ref.shape[1]), 1)
        masks.append((at // (groups * rows) != own_member).astype(jnp.float32))
    mask = jnp.concatenate(masks, axis=1)

    queries = head_norm(stacked(0), gain_ref[0:1, :]).astype(jnp.bfloat16)
    fresh = (by_patch(head_norm(stacked(1), gain_ref[1:2, :])), by_patch(stacked(2)))

    def entries(head, kind):
        at = slice(head * head_dim, (head + 1) * head_dim)
        old = old_table_ref[kind, :, :, at].reshape(groups * rows, head_dim)
        return jnp.concatenate([fresh[kind][head], old] + [ref[kind, :, at] for ref in stale_refs])

    scores = [
        lax.dot_general(
            queries[head],
            entries(head, 0),
            (((1,), (1,)), ((), ())),
            preferred_element_type=jnp.float32,
        )
        for head in range(heads)
    ]
    weights = mask[None] * jnp.exp(jnp.stack(scores) * (1.0 / math.sqrt(head_dim)))
    inverse = 1.0 / jnp.sum(weights, axis=-1, keepdims=True)
    weights = weights.astype(jnp.bfloat16)
    summed = [
        jnp.dot(weights[head], entries(head, 1), preferred_element_type=jnp.float32)
        for head in range(heads)
    ]
    attended = (jnp.stack(summed) * inverse).astype(jnp.bfloat16)
    attended = jnp.concatenate([attended[head] for head in range(heads)], axis=1)

    projected = jnp.dot(attended, out_ref[...], preferred_element_type=jnp.float32)
    projected = mod_ref[2] * projected
    if folding:
        at_slice = lax.broadcasted_iota(jnp.int32, (rows, 1), 0) // block_rows
        own = (at_slice == own_slice).astype(jnp.float32)
        projected = projected + own * jnp.concatenate(
            [rows_ref[q].reshape(rows, block_cols).astype(jnp.float32) for q in range(blocks)],
            axis=1,
        )
    if closing:
        close_into(partial_ref, projected, rows_ref, section, own_slice, in_group)
    else:
        out_cols = partial_ref.shape[3]
        for q in range(partial_ref.shape[0]):
            piece = projected[:, q * out_cols : (q + 1) * out_cols].astype(jnp.bfloat16)
            partial_ref[q] = piece.reshape(slices, block_rows, out_cols)

    for kind in range(2):
        rows_of = jnp.concatenate([fresh[kind][head] for head in range(heads)], axis=1)
        for at in range(groups):
            table_ref[kind, at] = jnp.where(group == at, rows_of, old_table_ref[kind, at])


def tick_kernel(tick, sizes, *refs):
    old_table_ref, partial_ref, table_ref = refs[-3:]
    group = tick - lax.axis_index("pipe")
    active = jnp.logical_and(group >= 0, group < old_table_ref.shape[1])

    @pl.when(active)
    def _():
        section_kernel(tick, sizes, *refs)

    @pl.when(jnp.logical_not(active))
    def _():
        partial_ref[...] = jnp.zeros(partial_ref.shape, partial_ref.dtype)
        table_ref[...] = old_table_ref[...]


def close_into(closing_ref, projected, rows_ref, section, own_slice, in_group):
    branches, patches, slices = closing_ref.shape[:3]
    blocks, _, block_rows, block_cols = rows_ref.shape
    tok_dev = block_rows // in_group
    per_branch = blocks // branches

    @pl.when(section >= patches)
    def _():
        for piece in range(slices):
            own = (own_slice == piece).astype(jnp.float32)
            by_block = []
            for q in range(blocks):
                rows = projected[
                    piece * block_rows : (piece + 1) * block_rows,
                    q * block_cols : (q + 1) * block_cols,
                ]
                rows = rows + own * rows_ref[q, piece].astype(jnp.float32)
                by_block.append(rows.reshape(in_group, tok_dev, block_cols))
            for branch in range(branches):
                for patch in range(patches):
                    held = [by_block[branch * per_branch + k][patch] for k in range(per_branch)]
                    closing_ref[branch, patch, piece] = jnp.concatenate(held).astype(jnp.bfloat16)

    @pl.when(section < patches)
    def _():
        finished = [rows_ref[q, own_slice].astype(jnp.float32)[:tok_dev] for q in range(blocks)]
        for branch in range(branches):
            held = jnp.concatenate(finished[branch * per_branch : (branch + 1) * per_branch])
            held = held.astype(jnp.bfloat16)
            for patch in range(patches):
                for piece in range(slices):
                    closing_ref[branch, patch, piece] = held


def start_kernel(latent_ref, *refs):
    spread_to = refs[-1]
    for piece in range(spread_to.shape[0]):
        spread_to[piece] = latent_ref[...]


def added(parts_ref, section, *streams_refs):
    total = sum(parts_ref[section, piece].astype(jnp.float32) for piece in range(parts_ref.shape[1]))
    for ref in streams_refs:
        total = total + ref[section].astype(jnp.float32)
    return total


def settle_first_kernel(parts_ref, latent_ref, spread_to):
    first = added(parts_ref, 0)
    half_cols = first.shape[1]
    for half in range(2):

        @pl.when(lax.axis_index("pipe") % 2 == half)
        def _():
            at = slice(half * half_cols, (half + 1) * half_cols)
            held = (first + latent_ref[0, :, at].astype(jnp.float32)).astype(jnp.bfloat16)
            for piece in range(parts_ref.shape[1]):
                spread_to[0, piece] = latent_ref[1, :, at]
                spread_to[1, piece] = held


def settle_kernel(parts_ref, *refs):
    *streams_refs, streams_to, spread_to = refs
    count, slices = parts_ref.shape[:2]
    for section in range(count):
        held = added(parts_ref, max(section - 1, 0), *streams_refs).astype(jnp.bfloat16)
        streams_to[section] = held
        for piece in range(slices):
            spread_to[section, piece] = held


def settle_last_kernel(in_group, parts_ref, streams_ref, spread_to):
    count, slices = parts_ref.shape[:2]
    finished = added(parts_ref, count - 1, streams_ref)
    tok_dev = finished.shape[0] // in_group
    last = added(parts_ref, count - 2, streams_ref).astype(jnp.bfloat16)
    for section in range(count):
        held = last
        if section < in_group:
            held = finished[section * tok_dev : (section + 1) * tok_dev]
            held = jnp.concatenate([held] * in_group).astype(jnp.bfloat16)
        for piece in range(slices):
            spread_to[section, piece] = held


def guide_kernel(members, closing_ref, table_ref, guided_ref, table_to, sem):
    copy = pltpu.make_async_copy(table_ref, table_to, sem)
    copy.start()
    branches, patches, slices, block_rows, block_cols = closing_ref.shape
    tok_dev = guided_ref.shape[0]
    section, _, own_slice = position(members)

    def combine(pair):
        conditional, unconditional = pair
        rows = unconditional + GUIDANCE_SCALE * (conditional - unconditional)
        for at in range(block_rows // tok_dev):
            guided_ref[:, at * block_cols : (at + 1) * block_cols] = rows[
                at * tok_dev : (at + 1) * tok_dev
            ].astype(jnp.bfloat16)

    @pl.when(section >= patches)
    def _():
        pair = []
        for branch in range(branches):
            total = 0.0
            for piece in range(slices):
                total = total + closing_ref[branch, patches - 1, piece].astype(jnp.float32)
            pair.append(total.astype(jnp.bfloat16).astype(jnp.float32))
        combine(pair)

    @pl.when(section < patches)
    def _():
        combine(
            [closing_ref[branch, section, own_slice].astype(jnp.float32) for branch in range(branches)]
        )

    copy.wait()


def local(latent, modulation, qkv_weight, out_weight, norm_gain, stale_kv):
    seq_count = lax.axis_size("seq")
    seq_rank = lax.axis_index("seq")
    section_count = lax.axis_size("pipe")
    patches, tok_dev, model_width = latent.shape
    head_dim = norm_gain.shape[2]
    slice_count = min(seq_count, 8)
    member_count = seq_count // slice_count
    member_bits = member_count.bit_length() - 1
    own_member = seq_rank % member_count
    local_width = stale_kv.shape[7]
    group_rows = slice_count * tok_dev
    own_cache = stale_kv[0, 0].reshape(2, patches, group_rows, local_width)
    group_cache = own_cache[None]
    qkv_slice = qkv_weight[0]
    out_slice = out_weight[0]
    for level_index in range(member_bits):
        got_qkv, got_out, got_cache = (
            swapped(qkv_slice, "seq", level_index),
            swapped(out_slice, "seq", level_index),
            swapped(group_cache, "seq", level_index),
        )
        is_upper = own_member >> level_index & 1 == 1
        qkv_slice = join_pair(is_upper, qkv_slice, got_qkv, 1)
        out_slice = join_pair(is_upper, out_slice, got_out, 0)
        group_cache = join_pair(is_upper, group_cache, got_cache, 0)
    homes = section_count * slice_count
    in_group = patches // GROUPS
    block_rows = in_group * tok_dev
    block_cols = model_width // section_count
    rows = slice_count * block_rows
    half = section_count // 2
    groups_of = range(member_count)
    in_slices = [[a + member_count * b for b in range(slice_count)] for a in groups_of]
    peers = [[q * seq_count + at for q in range(section_count) for at in g] for g in in_slices]
    closing_peers = [
        [
            (c * section_count + q) * seq_count + at
            for c in range(2)
            for q in range(h * half, (h + 1) * half)
            for at in g
        ]
        for h in range(2)
        for g in in_slices
    ]

    pair_peers = [
        [q * seq_count + at for q in range(first, first + 2) for at in g]
        for first in range(0, section_count, 2)
        for g in in_slices
    ]

    def exchange(value, among=peers):
        flat = value.reshape((-1,) + value.shape[2:])
        flat = lax.all_to_all(flat, ("pipe", "seq"), 0, 0, axis_index_groups=among)
        return flat.reshape(value.shape)

    vmem = pl.BlockSpec(memory_space=pltpu.VMEM)
    hbm = pl.BlockSpec(memory_space=pltpu.HBM)
    in_hbm = functools.partial(pltpu.with_memory_space_constraint, memory_space=pltpu.HBM)
    in_vmem = functools.partial(pltpu.with_memory_space_constraint, memory_space=pltpu.VMEM)
    sources = latent.reshape(GROUPS, block_rows, model_width)
    stream_shape = (section_count, block_rows, block_cols)
    spread_shape = (section_count, slice_count, block_rows, block_cols)
    modulation = modulation.reshape(3, 1, model_width)
    norm_gain = norm_gain[0]
    table = own_cache.reshape(2, GROUPS, rows, local_width)
    named = (qkv_slice, out_slice, modulation, norm_gain, table, sources)
    spread = pl.pallas_call(
        start_kernel,
        out_shape=jax.ShapeDtypeStruct((slice_count, block_rows, model_width), jnp.bfloat16),
        in_specs=[vmem] + [hbm] * len(named),
        out_specs=vmem,
        compiler_params=pltpu.CompilerParams(vmem_limit_bytes=4 * 1024 * 1024),
    )(sources[0], *map(in_hbm, named))
    stale_rows = []
    if member_count > 1:
        stale_rows = [group_cache.swapaxes(0, 1).reshape(2, -1, local_width)]

    ticks = GROUPS + section_count - 1

    def attend(tick, features, table, partial_shape):
        operands = (
            features,
            in_vmem(modulation),
            in_vmem(qkv_slice),
            in_vmem(out_slice),
            in_vmem(norm_gain),
            *stale_rows,
            in_vmem(table),
        )
        return pl.pallas_call(
            functools.partial(
                section_kernel if tick == ticks - 1 else tick_kernel,
                tick,
                (tok_dev, head_dim, member_count),
            ),
            out_shape=(
                jax.ShapeDtypeStruct(partial_shape, jnp.bfloat16),
                jax.ShapeDtypeStruct(table.shape, jnp.bfloat16),
            ),
            in_specs=[vmem] * len(operands),
            out_specs=(vmem, vmem),
            compiler_params=pltpu.CompilerParams(vmem_limit_bytes=24 * 1024 * 1024),
        )(*operands)

    def small(kernel, in_specs, *out_shapes):
        return pl.pallas_call(
            kernel,
            out_shape=tuple(jax.ShapeDtypeStruct(shape, jnp.bfloat16) for shape in out_shapes),
            in_specs=in_specs,
            out_specs=(vmem,) * len(out_shapes),
            compiler_params=pltpu.CompilerParams(vmem_limit_bytes=8 * 1024 * 1024),
        )

    closing_shape = (2, half, slice_count, block_rows, block_cols)
    features = lax.all_to_all(spread, "seq", 0, 0, axis_index_groups=in_slices)[None]
    pair_shape = (2, slice_count, block_rows, model_width // 2)
    partial_out, table = attend(0, features, table, pair_shape)
    parts = exchange(partial_out, pair_peers)
    (spread,) = small(settle_first_kernel, [vmem] * 2, pair_shape)(parts, in_vmem(sources))
    features = exchange(spread, pair_peers)
    streams = []
    for tick in range(1, ticks - 2):
        partial_out, table = attend(tick, features, table, spread_shape)
        held = [exchange(partial_out)] + streams
        stream, spread = small(settle_kernel, [vmem] * len(held), stream_shape, spread_shape)(*held)
        streams = [stream]
        features = exchange(spread)
    partial_out, table = attend(ticks - 2, features, table, spread_shape)
    (spread,) = small(
        functools.partial(settle_last_kernel, in_group), [vmem] * 2, spread_shape
    )(exchange(partial_out), *streams)
    features = exchange(spread)
    closing, table = attend(ticks - 1, features, table, closing_shape)
    closing = lax.all_to_all(
        closing.reshape((-1,) + closing_shape[3:]),
        ("cfg", "pipe", "seq"),
        0,
        0,
        axis_index_groups=closing_peers,
    ).reshape(closing_shape)
    guided, table = pl.pallas_call(
        functools.partial(guide_kernel, member_count),
        out_shape=(
            jax.ShapeDtypeStruct((tok_dev, model_width // 2), jnp.bfloat16),
            jax.ShapeDtypeStruct(table.shape, jnp.bfloat16),
        ),
        in_specs=[vmem, vmem],
        out_specs=(vmem, hbm),
        scratch_shapes=[pltpu.SemaphoreType.DMA],
        compiler_params=pltpu.CompilerParams(vmem_limit_bytes=8 * 1024 * 1024),
    )(closing, table)
    return (guided[None], table.reshape(stale_kv.shape))


def solution(mesh):
    placed = (
        P(None, "seq", None),
        P("pipe", "cfg", None, None),
        P("pipe", None, "seq"),
        P("pipe", "seq", None),
        P("pipe", None, None),
        P("pipe", "cfg", None, None, "seq", None, None, None),
    )
    return jax.shard_map(
        local,
        mesh=mesh,
        in_specs=placed,
        out_specs=(P("pipe", "seq", "cfg"), P("pipe", "cfg", None, None, "seq", None, None, None)),
        check_vma=False,
    )
```

```python
import functools
import math

import jax
import jax.numpy as jnp
from jax import lax
from jax.experimental import pallas as pl
from jax.experimental.pallas import tpu as pltpu
from jax.sharding import PartitionSpec as P

GUIDANCE_SCALE = 6.0
EPSILON = 1e-06
GROUPS = 2


def swapped(value, axis, bit):
    return lax.ppermute(value, axis, [(i, i ^ 1 << bit) for i in range(lax.axis_size(axis))])


def head_norm(values, gain_row):
    return (
        values * lax.rsqrt(jnp.mean(values * values, axis=-1, keepdims=True) + EPSILON) * gain_row
    )


def join_pair(is_upper, mine, theirs, axis_dim):
    return jnp.where(
        is_upper,
        jnp.concatenate((theirs, mine), axis_dim),
        jnp.concatenate((mine, theirs), axis_dim),
    )


def position(members):
    rank = lax.axis_index("seq")
    return lax.axis_index("pipe"), rank % members, rank // members


def section_kernel(tick, sizes, rows_ref, mod_ref, qkv_ref, out_ref, gain_ref, *refs):
    *stale_refs, old_table_ref, partial_ref, table_ref = refs
    closing = len(partial_ref.shape) == 5
    folding = tick == 1
    tok_dev, head_dim, members = sizes
    blocks, slices, block_rows, block_cols = rows_ref.shape
    rows = slices * block_rows
    width = blocks * block_cols
    in_group = block_rows // tok_dev
    group_rows = slices * tok_dev
    groups, local_width = table_ref.shape[1], table_ref.shape[3]
    heads = local_width // head_dim
    section, own_member, own_slice = position(members)
    group = tick - section
    parts = [rows_ref[q].reshape(rows, block_cols).astype(jnp.float32) for q in range(blocks)]
    mean = jnp.sum(sum(parts), axis=-1, keepdims=True) * (1.0 / width)
    parts = [x - mean for x in parts]
    spread = jnp.sum(sum(x * x for x in parts), axis=-1, keepdims=True) * (1.0 / width)
    inverse = lax.rsqrt(spread + EPSILON)
    modulated = []
    for q, x in enumerate(parts):
        at = slice(q * block_cols, (q + 1) * block_cols)
        modulated.append(
            (x * inverse * (1.0 + mod_ref[1, :, at]) + mod_ref[0, :, at]).astype(jnp.bfloat16)
        )
    modulated = jnp.concatenate(modulated, axis=1)
    mixed = jnp.dot(modulated, qkv_ref[...], preferred_element_type=jnp.float32)

    def stacked(kind):
        at = [(3 * head + kind) * head_dim for head in range(heads)]
        return jnp.stack([mixed[:, start : start + head_dim] for start in at])

    def by_patch(values):
        values = values.reshape(heads, slices, in_group, tok_dev, head_dim).swapaxes(1, 2)
        return values.reshape(heads, rows, head_dim).astype(jnp.bfloat16)

    def query_patch(shape):
        return lax.broadcasted_iota(jnp.int32, shape, 0) // tok_dev % in_group

    fresh_shape, old_shape = (rows, rows), (rows, groups * rows)
    fresh_patch = lax.broadcasted_iota(jnp.int32, fresh_shape, 1) // group_rows
    old_patch = lax.broadcasted_iota(jnp.int32, old_shape, 1) // group_rows - group * in_group
    masks = [
        (fresh_patch <= query_patch(fresh_shape)).astype(jnp.float32),
        jnp.logical_or(old_patch < 0, old_patch > query_patch(old_shape)).astype(jnp.float32),
    ]
    for ref in stale_refs:
        at = lax.broadcasted_iota(jnp.int32, (rows, ref.shape[1]), 1)
        masks.append((at // (groups * rows) != own_member).astype(jnp.float32))
    mask = jnp.concatenate(masks, axis=1)

    queries = head_norm(stacked(0), gain_ref[0:1, :]).astype(jnp.bfloat16)
    fresh = (by_patch(head_norm(stacked(1), gain_ref[1:2, :])), by_patch(stacked(2)))

    def entries(head, kind):
        at = slice(head * head_dim, (head + 1) * head_dim)
        old = old_table_ref[kind, :, :, at].reshape(groups * rows, head_dim)
        return jnp.concatenate([fresh[kind][head], old] + [ref[kind, :, at] for ref in stale_refs])

    scores = [
        lax.dot_general(
            queries[head],
            entries(head, 0),
            (((1,), (1,)), ((), ())),
            preferred_element_type=jnp.float32,
        )
        for head in range(heads)
    ]
    weights = mask[None] * jnp.exp(jnp.stack(scores) * (1.0 / math.sqrt(head_dim)))
    inverse = 1.0 / jnp.sum(weights, axis=-1, keepdims=True)
    weights = weights.astype(jnp.bfloat16)
    summed = [
        jnp.dot(weights[head], entries(head, 1), preferred_element_type=jnp.float32)
        for head in range(heads)
    ]
    attended = (jnp.stack(summed) * inverse).astype(jnp.bfloat16)
    attended = jnp.concatenate([attended[head] for head in range(heads)], axis=1)

    projected = jnp.dot(attended, out_ref[...], preferred_element_type=jnp.float32)
    projected = mod_ref[2] * projected
    if folding:
        at_slice = lax.broadcasted_iota(jnp.int32, (rows, 1), 0) // block_rows
        own = (at_slice == own_slice).astype(jnp.float32)
        projected = projected + own * jnp.concatenate(
            [rows_ref[q].reshape(rows, block_cols).astype(jnp.float32) for q in range(blocks)],
            axis=1,
        )
    if closing:
        close_into(partial_ref, projected, rows_ref, section, own_slice, in_group)
    else:
        out_cols = partial_ref.shape[3]
        for q in range(partial_ref.shape[0]):
            piece = projected[:, q * out_cols : (q + 1) * out_cols].astype(jnp.bfloat16)
            partial_ref[q] = piece.reshape(slices, block_rows, out_cols)

    for kind in range(2):
        rows_of = jnp.concatenate([fresh[kind][head] for head in range(heads)], axis=1)
        for at in range(groups):
            table_ref[kind, at] = jnp.where(group == at, rows_of, old_table_ref[kind, at])


def close_finished(closing_ref, rows_ref, own_slice, tok_dev):
    branches, patches, slices = closing_ref.shape[:3]
    blocks = rows_ref.shape[0]
    per_branch = blocks // branches
    finished = [rows_ref[q, own_slice].astype(jnp.float32)[:tok_dev] for q in range(blocks)]
    for branch in range(branches):
        held = jnp.concatenate(finished[branch * per_branch : (branch + 1) * per_branch])
        held = held.astype(jnp.bfloat16)
        for patch in range(patches):
            for piece in range(slices):
                closing_ref[branch, patch, piece] = held


def tick_kernel(tick, sizes, *refs):
    old_table_ref, partial_ref, table_ref = refs[-3:]
    group = tick - lax.axis_index("pipe")
    active = jnp.logical_and(group >= 0, group < old_table_ref.shape[1])

    @pl.when(active)
    def _():
        section_kernel(tick, sizes, *refs)

    @pl.when(jnp.logical_not(active))
    def _():
        if len(partial_ref.shape) == 5:
            close_finished(partial_ref, refs[0], position(sizes[2])[2], sizes[0])
        else:
            partial_ref[...] = jnp.zeros(partial_ref.shape, partial_ref.dtype)
        table_ref[...] = old_table_ref[...]


def close_into(closing_ref, projected, rows_ref, section, own_slice, in_group):
    branches, patches, slices = closing_ref.shape[:3]
    blocks, _, block_rows, block_cols = rows_ref.shape
    tok_dev = block_rows // in_group
    per_branch = blocks // branches

    @pl.when(section >= patches)
    def _():
        for piece in range(slices):
            own = (own_slice == piece).astype(jnp.float32)
            by_block = []
            for q in range(blocks):
                rows = projected[
                    piece * block_rows : (piece + 1) * block_rows,
                    q * block_cols : (q + 1) * block_cols,
                ]
                rows = rows + own * rows_ref[q, piece].astype(jnp.float32)
                by_block.append(rows.reshape(in_group, tok_dev, block_cols))
            for branch in range(branches):
                for patch in range(patches):
                    held = [by_block[branch * per_branch + k][patch] for k in range(per_branch)]
                    closing_ref[branch, patch, piece] = jnp.concatenate(held).astype(jnp.bfloat16)

    @pl.when(section < patches)
    def _():
        close_finished(closing_ref, rows_ref, own_slice, tok_dev)


def start_kernel(latent_ref, *refs):
    spread_to = refs[-1]
    for piece in range(spread_to.shape[0]):
        spread_to[piece] = latent_ref[...]


def added(parts_ref, section, *streams_refs):
    total = sum(parts_ref[section, piece].astype(jnp.float32) for piece in range(parts_ref.shape[1]))
    for ref in streams_refs:
        total = total + ref[section].astype(jnp.float32)
    return total


def settle_first_kernel(parts_ref, latent_ref, spread_to):
    first = added(parts_ref, 0)
    half_cols = first.shape[1]
    for half in range(2):

        @pl.when(lax.axis_index("pipe") % 2 == half)
        def _():
            at = slice(half * half_cols, (half + 1) * half_cols)
            held = (first + latent_ref[0, :, at].astype(jnp.float32)).astype(jnp.bfloat16)
            for piece in range(parts_ref.shape[1]):
                spread_to[0, piece] = latent_ref[1, :, at]
                spread_to[1, piece] = held


def settle_kernel(parts_ref, *refs):
    *streams_refs, streams_to, spread_to = refs
    count, slices = parts_ref.shape[:2]
    for section in range(count):
        held = added(parts_ref, max(section - 1, 0), *streams_refs).astype(jnp.bfloat16)
        streams_to[section] = held
        for piece in range(slices):
            spread_to[section, piece] = held


def settle_last_kernel(in_group, parts_ref, streams_ref, spread_to):
    count, slices = parts_ref.shape[:2]
    finished = added(parts_ref, count - 1, streams_ref)
    tok_dev = finished.shape[0] // in_group
    last = added(parts_ref, count - 2, streams_ref).astype(jnp.bfloat16)
    for section in range(count):
        held = last
        if section < in_group:
            held = finished[section * tok_dev : (section + 1) * tok_dev]
            held = jnp.concatenate([held] * in_group).astype(jnp.bfloat16)
        for piece in range(slices):
            spread_to[section, piece] = held


def guide_kernel(members, closing_ref, table_ref, guided_ref, table_to, sem):
    copy = pltpu.make_async_copy(table_ref, table_to, sem)
    copy.start()
    branches, patches, slices, block_rows, block_cols = closing_ref.shape
    tok_dev = guided_ref.shape[0]
    section, _, own_slice = position(members)

    def combine(pair):
        conditional, unconditional = pair
        rows = unconditional + GUIDANCE_SCALE * (conditional - unconditional)
        for at in range(block_rows // tok_dev):
            guided_ref[:, at * block_cols : (at + 1) * block_cols] = rows[
                at * tok_dev : (at + 1) * tok_dev
            ].astype(jnp.bfloat16)

    @pl.when(section >= patches)
    def _():
        pair = []
        for branch in range(branches):
            total = 0.0
            for piece in range(slices):
                total = total + closing_ref[branch, patches - 1, piece].astype(jnp.float32)
            pair.append(total.astype(jnp.bfloat16).astype(jnp.float32))
        combine(pair)

    @pl.when(section < patches)
    def _():
        combine(
            [closing_ref[branch, section, own_slice].astype(jnp.float32) for branch in range(branches)]
        )

    copy.wait()


def local(latent, modulation, qkv_weight, out_weight, norm_gain, stale_kv):
    seq_count = lax.axis_size("seq")
    seq_rank = lax.axis_index("seq")
    section_count = lax.axis_size("pipe")
    patches, tok_dev, model_width = latent.shape
    head_dim = norm_gain.shape[2]
    slice_count = min(seq_count, 8)
    member_count = seq_count // slice_count
    member_bits = member_count.bit_length() - 1
    own_member = seq_rank % member_count
    local_width = stale_kv.shape[7]
    group_rows = slice_count * tok_dev
    own_cache = stale_kv[0, 0].reshape(2, patches, group_rows, local_width)
    group_cache = own_cache[None]
    qkv_slice = qkv_weight[0]
    out_slice = out_weight[0]
    for level_index in range(member_bits):
        got_qkv, got_out, got_cache = (
            swapped(qkv_slice, "seq", level_index),
            swapped(out_slice, "seq", level_index),
            swapped(group_cache, "seq", level_index),
        )
        is_upper = own_member >> level_index & 1 == 1
        qkv_slice = join_pair(is_upper, qkv_slice, got_qkv, 1)
        out_slice = join_pair(is_upper, out_slice, got_out, 0)
        group_cache = join_pair(is_upper, group_cache, got_cache, 0)
    homes = section_count * slice_count
    in_group = patches // GROUPS
    block_rows = in_group * tok_dev
    block_cols = model_width // section_count
    rows = slice_count * block_rows
    half = section_count // 2
    groups_of = range(member_count)
    in_slices = [[a + member_count * b for b in range(slice_count)] for a in groups_of]
    peers = [[q * seq_count + at for q in range(section_count) for at in g] for g in in_slices]
    closing_peers = [
        [
            (c * section_count + q) * seq_count + at
            for c in range(2)
            for q in range(h * half, (h + 1) * half)
            for at in g
        ]
        for h in range(2)
        for g in in_slices
    ]

    pair_peers = [
        [q * seq_count + at for q in range(first, first + 2) for at in g]
        for first in range(0, section_count, 2)
        for g in in_slices
    ]

    def exchange(value, among=peers):
        flat = value.reshape((-1,) + value.shape[2:])
        flat = lax.all_to_all(flat, ("pipe", "seq"), 0, 0, axis_index_groups=among)
        return flat.reshape(value.shape)

    vmem = pl.BlockSpec(memory_space=pltpu.VMEM)
    hbm = pl.BlockSpec(memory_space=pltpu.HBM)
    in_hbm = functools.partial(pltpu.with_memory_space_constraint, memory_space=pltpu.HBM)
    in_vmem = functools.partial(pltpu.with_memory_space_constraint, memory_space=pltpu.VMEM)
    sources = latent.reshape(GROUPS, block_rows, model_width)
    stream_shape = (section_count, block_rows, block_cols)
    spread_shape = (section_count, slice_count, block_rows, block_cols)
    modulation = modulation.reshape(3, 1, model_width)
    norm_gain = norm_gain[0]
    table = own_cache.reshape(2, GROUPS, rows, local_width)
    named = (qkv_slice, out_slice, modulation, norm_gain, table, sources)
    spread = pl.pallas_call(
        start_kernel,
        out_shape=jax.ShapeDtypeStruct((slice_count, block_rows, model_width), jnp.bfloat16),
        in_specs=[vmem] + [hbm] * len(named),
        out_specs=vmem,
        compiler_params=pltpu.CompilerParams(vmem_limit_bytes=4 * 1024 * 1024),
    )(sources[0], *map(in_hbm, named))
    stale_rows = []
    if member_count > 1:
        stale_rows = [group_cache.swapaxes(0, 1).reshape(2, -1, local_width)]

    ticks = GROUPS + section_count - 1

    def attend(tick, features, table, partial_shape):
        operands = (
            features,
            in_vmem(modulation),
            in_vmem(qkv_slice),
            in_vmem(out_slice),
            in_vmem(norm_gain),
            *stale_rows,
            in_vmem(table),
        )
        return pl.pallas_call(
            functools.partial(
                tick_kernel,
                tick,
                (tok_dev, head_dim, member_count),
            ),
            out_shape=(
                jax.ShapeDtypeStruct(partial_shape, jnp.bfloat16),
                jax.ShapeDtypeStruct(table.shape, jnp.bfloat16),
            ),
            in_specs=[vmem] * len(operands),
            out_specs=(vmem, vmem),
            compiler_params=pltpu.CompilerParams(vmem_limit_bytes=24 * 1024 * 1024),
        )(*operands)

    def small(kernel, in_specs, *out_shapes):
        return pl.pallas_call(
            kernel,
            out_shape=tuple(jax.ShapeDtypeStruct(shape, jnp.bfloat16) for shape in out_shapes),
            in_specs=in_specs,
            out_specs=(vmem,) * len(out_shapes),
            compiler_params=pltpu.CompilerParams(vmem_limit_bytes=8 * 1024 * 1024),
        )

    closing_shape = (2, half, slice_count, block_rows, block_cols)
    features = lax.all_to_all(spread, "seq", 0, 0, axis_index_groups=in_slices)[None]
    pair_shape = (2, slice_count, block_rows, model_width // 2)
    partial_out, table = attend(0, features, table, pair_shape)
    parts = exchange(partial_out, pair_peers)
    (spread,) = small(settle_first_kernel, [vmem] * 2, pair_shape)(parts, in_vmem(sources))
    features = exchange(spread, pair_peers)
    streams = []
    for tick in range(1, ticks - 2):
        partial_out, table = attend(tick, features, table, spread_shape)
        held = [exchange(partial_out)] + streams
        stream, spread = small(settle_kernel, [vmem] * len(held), stream_shape, spread_shape)(*held)
        streams = [stream]
        features = exchange(spread)
    partial_out, table = attend(ticks - 2, features, table, spread_shape)
    (spread,) = small(
        functools.partial(settle_last_kernel, in_group), [vmem] * 2, spread_shape
    )(exchange(partial_out), *streams)
    features = exchange(spread)
    closing, table = attend(ticks - 1, features, table, closing_shape)
    closing = lax.all_to_all(
        closing.reshape((-1,) + closing_shape[3:]),
        ("cfg", "pipe", "seq"),
        0,
        0,
        axis_index_groups=closing_peers,
    ).reshape(closing_shape)
    guided, table = pl.pallas_call(
        functools.partial(guide_kernel, member_count),
        out_shape=(
            jax.ShapeDtypeStruct((tok_dev, model_width // 2), jnp.bfloat16),
            jax.ShapeDtypeStruct(table.shape, jnp.bfloat16),
        ),
        in_specs=[vmem, vmem],
        out_specs=(vmem, hbm),
        scratch_shapes=[pltpu.SemaphoreType.DMA],
        compiler_params=pltpu.CompilerParams(vmem_limit_bytes=8 * 1024 * 1024),
    )(closing, table)
    return (guided[None], table.reshape(stale_kv.shape))


def solution(mesh):
    placed = (
        P(None, "seq", None),
        P("pipe", "cfg", None, None),
        P("pipe", None, "seq"),
        P("pipe", "seq", None),
        P("pipe", None, None),
        P("pipe", "cfg", None, None, "seq", None, None, None),
    )
    return jax.shard_map(
        local,
        mesh=mesh,
        in_specs=placed,
        out_specs=(P("pipe", "seq", "cfg"), P("pipe", "cfg", None, None, "seq", None, None, None)),
        check_vma=False,
    )
```

```python
import functools
import math

import jax
import jax.numpy as jnp
from jax import lax
from jax.experimental import pallas as pl
from jax.experimental.pallas import tpu as pltpu
from jax.sharding import PartitionSpec as P

GUIDANCE_SCALE = 6.0
EPSILON = 1e-06
GROUPS = 2


def swapped(value, axis, bit):
    return lax.ppermute(value, axis, [(i, i ^ 1 << bit) for i in range(lax.axis_size(axis))])


def head_norm(values, gain_row):
    return (
        values * lax.rsqrt(jnp.mean(values * values, axis=-1, keepdims=True) + EPSILON) * gain_row
    )


def join_pair(is_upper, mine, theirs, axis_dim):
    return jnp.where(
        is_upper,
        jnp.concatenate((theirs, mine), axis_dim),
        jnp.concatenate((mine, theirs), axis_dim),
    )


def position(members):
    rank = lax.axis_index("seq")
    return lax.axis_index("pipe"), rank % members, rank // members


def section_kernel(tick, sizes, rows_ref, mod_ref, qkv_ref, out_ref, gain_ref, *refs):
    *stale_refs, old_table_ref, partial_ref, table_ref = refs
    closing = len(partial_ref.shape) == 5
    folding = tick == 1
    tok_dev, head_dim, members = sizes
    blocks, slices, block_rows, block_cols = rows_ref.shape
    rows = slices * block_rows
    width = blocks * block_cols
    in_group = block_rows // tok_dev
    group_rows = slices * tok_dev
    groups, local_width = table_ref.shape[1], table_ref.shape[3]
    heads = local_width // head_dim
    section, own_member, own_slice = position(members)
    group = tick - section
    parts = [rows_ref[q].reshape(rows, block_cols).astype(jnp.float32) for q in range(blocks)]
    mean = jnp.sum(sum(parts), axis=-1, keepdims=True) * (1.0 / width)
    parts = [x - mean for x in parts]
    spread = jnp.sum(sum(x * x for x in parts), axis=-1, keepdims=True) * (1.0 / width)
    inverse = lax.rsqrt(spread + EPSILON)
    modulated = []
    for q, x in enumerate(parts):
        at = slice(q * block_cols, (q + 1) * block_cols)
        modulated.append(
            (x * inverse * (1.0 + mod_ref[1, :, at]) + mod_ref[0, :, at]).astype(jnp.bfloat16)
        )
    modulated = jnp.concatenate(modulated, axis=1)
    mixed = jnp.dot(modulated, qkv_ref[...], preferred_element_type=jnp.float32)

    def stacked(kind):
        at = [(3 * head + kind) * head_dim for head in range(heads)]
        return jnp.stack([mixed[:, start : start + head_dim] for start in at])

    def by_patch(values):
        values = values.reshape(heads, slices, in_group, tok_dev, head_dim).swapaxes(1, 2)
        return values.reshape(heads, rows, head_dim).astype(jnp.bfloat16)

    def query_patch(shape):
        return lax.broadcasted_iota(jnp.int32, shape, 0) // tok_dev % in_group

    fresh_shape, old_shape = (rows, rows), (rows, groups * rows)
    fresh_patch = lax.broadcasted_iota(jnp.int32, fresh_shape, 1) // group_rows
    old_patch = lax.broadcasted_iota(jnp.int32, old_shape, 1) // group_rows - group * in_group
    masks = [
        (fresh_patch <= query_patch(fresh_shape)).astype(jnp.float32),
        jnp.logical_or(old_patch < 0, old_patch > query_patch(old_shape)).astype(jnp.float32),
    ]
    for ref in stale_refs:
        at = lax.broadcasted_iota(jnp.int32, (rows, ref.shape[1]), 1)
        masks.append((at // (groups * rows) != own_member).astype(jnp.float32))
    mask = jnp.concatenate(masks, axis=1)

    queries = head_norm(stacked(0), gain_ref[0:1, :]).astype(jnp.bfloat16)
    fresh = (by_patch(head_norm(stacked(1), gain_ref[1:2, :])), by_patch(stacked(2)))

    def entries(head, kind):
        at = slice(head * head_dim, (head + 1) * head_dim)
        old = old_table_ref[kind, :, :, at].reshape(groups * rows, head_dim)
        return jnp.concatenate([fresh[kind][head], old] + [ref[kind, :, at] for ref in stale_refs])

    scores = [
        lax.dot_general(
            queries[head],
            entries(head, 0),
            (((1,), (1,)), ((), ())),
            preferred_element_type=jnp.float32,
        )
        for head in range(heads)
    ]
    weights = mask[None] * jnp.exp(jnp.stack(scores) * (1.0 / math.sqrt(head_dim)))
    inverse = 1.0 / jnp.sum(weights, axis=-1, keepdims=True)
    weights = weights.astype(jnp.bfloat16)
    summed = [
        jnp.dot(weights[head], entries(head, 1), preferred_element_type=jnp.float32)
        for head in range(heads)
    ]
    attended = (jnp.stack(summed) * inverse).astype(jnp.bfloat16)
    attended = jnp.concatenate([attended[head] for head in range(heads)], axis=1)

    projected = jnp.dot(attended, out_ref[...], preferred_element_type=jnp.float32)
    projected = mod_ref[2] * projected
    if folding:
        at_slice = lax.broadcasted_iota(jnp.int32, (rows, 1), 0) // block_rows
        own = (at_slice == own_slice).astype(jnp.float32)
        projected = projected + own * jnp.concatenate(
            [rows_ref[q].reshape(rows, block_cols).astype(jnp.float32) for q in range(blocks)],
            axis=1,
        )
    if closing:
        close_into(partial_ref, projected, rows_ref, section, own_slice, in_group)
    else:
        out_cols = partial_ref.shape[3]
        for q in range(partial_ref.shape[0]):
            piece = projected[:, q * out_cols : (q + 1) * out_cols].astype(jnp.bfloat16)
            partial_ref[q] = piece.reshape(slices, block_rows, out_cols)

    for kind in range(2):
        rows_of = jnp.concatenate([fresh[kind][head] for head in range(heads)], axis=1)
        for at in range(groups):
            table_ref[kind, at] = jnp.where(group == at, rows_of, old_table_ref[kind, at])


def close_finished(closing_ref, rows_ref, own_slice, tok_dev):
    branches, patches, slices = closing_ref.shape[:3]
    blocks = rows_ref.shape[0]
    per_branch = blocks // branches
    finished = [rows_ref[q, own_slice].astype(jnp.float32)[:tok_dev] for q in range(blocks)]
    for branch in range(branches):
        held = jnp.concatenate(finished[branch * per_branch : (branch + 1) * per_branch])
        held = held.astype(jnp.bfloat16)
        for patch in range(patches):
            for piece in range(slices):
                closing_ref[branch, patch, piece] = held


def tick_kernel(tick, sizes, *refs):
    old_table_ref, partial_ref, table_ref = refs[-3:]
    group = tick - lax.axis_index("pipe")
    active = jnp.logical_and(group >= 0, group < old_table_ref.shape[1])

    @pl.when(active)
    def _():
        section_kernel(tick, sizes, *refs)

    @pl.when(jnp.logical_not(active))
    def _():
        if len(partial_ref.shape) == 5:
            close_finished(partial_ref, refs[0], position(sizes[2])[2], sizes[0])
        else:
            partial_ref[...] = jnp.zeros(partial_ref.shape, partial_ref.dtype)
        table_ref[...] = old_table_ref[...]


def close_into(closing_ref, projected, rows_ref, section, own_slice, in_group):
    branches, patches, slices = closing_ref.shape[:3]
    blocks, _, block_rows, block_cols = rows_ref.shape
    tok_dev = block_rows // in_group
    per_branch = blocks // branches

    @pl.when(section >= patches)
    def _():
        for piece in range(slices):
            own = (own_slice == piece).astype(jnp.float32)
            by_block = []
            for q in range(blocks):
                rows = projected[
                    piece * block_rows : (piece + 1) * block_rows,
                    q * block_cols : (q + 1) * block_cols,
                ]
                rows = rows + own * rows_ref[q, piece].astype(jnp.float32)
                by_block.append(rows.reshape(in_group, tok_dev, block_cols))
            for branch in range(branches):
                for patch in range(patches):
                    held = [by_block[branch * per_branch + k][patch] for k in range(per_branch)]
                    closing_ref[branch, patch, piece] = jnp.concatenate(held).astype(jnp.bfloat16)

    @pl.when(section < patches)
    def _():
        close_finished(closing_ref, rows_ref, own_slice, tok_dev)


def start_kernel(latent_ref, *refs):
    spread_to, sem = refs[-2:]
    copy = pltpu.make_async_copy(latent_ref.at[0], spread_to.at[0], sem)
    copy.start()
    copy.wait()
    for piece in range(1, spread_to.shape[0]):
        spread_to[piece] = spread_to[0]


def added(parts_ref, section, *streams_refs):
    total = sum(parts_ref[section, piece].astype(jnp.float32) for piece in range(parts_ref.shape[1]))
    for ref in streams_refs:
        total = total + ref[section].astype(jnp.float32)
    return total


def settle_first_kernel(parts_ref, latent_ref, spread_to):
    first = added(parts_ref, 0)
    half_cols = first.shape[1]
    for half in range(2):

        @pl.when(lax.axis_index("pipe") % 2 == half)
        def _():
            at = slice(half * half_cols, (half + 1) * half_cols)
            held = (first + latent_ref[0, :, at].astype(jnp.float32)).astype(jnp.bfloat16)
            for piece in range(parts_ref.shape[1]):
                spread_to[0, piece] = latent_ref[1, :, at]
                spread_to[1, piece] = held


def settle_kernel(parts_ref, *refs):
    *streams_refs, streams_to, spread_to = refs
    count, slices = parts_ref.shape[:2]
    for section in range(count):
        held = added(parts_ref, max(section - 1, 0), *streams_refs).astype(jnp.bfloat16)
        streams_to[section] = held
        for piece in range(slices):
            spread_to[section, piece] = held


def settle_last_kernel(in_group, parts_ref, streams_ref, spread_to):
    count, slices = parts_ref.shape[:2]
    finished = added(parts_ref, count - 1, streams_ref)
    tok_dev = finished.shape[0] // in_group
    last = added(parts_ref, count - 2, streams_ref).astype(jnp.bfloat16)
    for section in range(count):
        held = last
        if section < in_group:
            held = finished[section * tok_dev : (section + 1) * tok_dev]
            held = jnp.concatenate([held] * in_group).astype(jnp.bfloat16)
        for piece in range(slices):
            spread_to[section, piece] = held


def guide_kernel(members, closing_ref, table_ref, guided_ref, table_to, sem):
    copy = pltpu.make_async_copy(table_ref, table_to, sem)
    copy.start()
    branches, patches, slices, block_rows, block_cols = closing_ref.shape
    tok_dev = guided_ref.shape[0]
    section, _, own_slice = position(members)

    def combine(pair):
        conditional, unconditional = pair
        rows = unconditional + GUIDANCE_SCALE * (conditional - unconditional)
        for at in range(block_rows // tok_dev):
            guided_ref[:, at * block_cols : (at + 1) * block_cols] = rows[
                at * tok_dev : (at + 1) * tok_dev
            ].astype(jnp.bfloat16)

    @pl.when(section >= patches)
    def _():
        pair = []
        for branch in range(branches):
            total = 0.0
            for piece in range(slices):
                total = total + closing_ref[branch, patches - 1, piece].astype(jnp.float32)
            pair.append(total.astype(jnp.bfloat16).astype(jnp.float32))
        combine(pair)

    @pl.when(section < patches)
    def _():
        combine(
            [closing_ref[branch, section, own_slice].astype(jnp.float32) for branch in range(branches)]
        )

    copy.wait()


def local(latent, modulation, qkv_weight, out_weight, norm_gain, stale_kv):
    seq_count = lax.axis_size("seq")
    seq_rank = lax.axis_index("seq")
    section_count = lax.axis_size("pipe")
    patches, tok_dev, model_width = latent.shape
    head_dim = norm_gain.shape[2]
    slice_count = min(seq_count, 8)
    member_count = seq_count // slice_count
    member_bits = member_count.bit_length() - 1
    own_member = seq_rank % member_count
    local_width = stale_kv.shape[7]
    group_rows = slice_count * tok_dev
    own_cache = stale_kv[0, 0].reshape(2, patches, group_rows, local_width)
    group_cache = own_cache[None]
    qkv_slice = qkv_weight[0]
    out_slice = out_weight[0]
    for level_index in range(member_bits):
        got_qkv, got_out, got_cache = (
            swapped(qkv_slice, "seq", level_index),
            swapped(out_slice, "seq", level_index),
            swapped(group_cache, "seq", level_index),
        )
        is_upper = own_member >> level_index & 1 == 1
        qkv_slice = join_pair(is_upper, qkv_slice, got_qkv, 1)
        out_slice = join_pair(is_upper, out_slice, got_out, 0)
        group_cache = join_pair(is_upper, group_cache, got_cache, 0)
    homes = section_count * slice_count
    in_group = patches // GROUPS
    block_rows = in_group * tok_dev
    block_cols = model_width // section_count
    rows = slice_count * block_rows
    half = section_count // 2
    groups_of = range(member_count)
    in_slices = [[a + member_count * b for b in range(slice_count)] for a in groups_of]
    peers = [[q * seq_count + at for q in range(section_count) for at in g] for g in in_slices]
    closing_peers = [
        [
            (c * section_count + q) * seq_count + at
            for c in range(2)
            for q in range(h * half, (h + 1) * half)
            for at in g
        ]
        for h in range(2)
        for g in in_slices
    ]

    pair_peers = [
        [q * seq_count + at for q in range(first, first + 2) for at in g]
        for first in range(0, section_count, 2)
        for g in in_slices
    ]

    def exchange(value, among=peers):
        flat = value.reshape((-1,) + value.shape[2:])
        flat = lax.all_to_all(flat, ("pipe", "seq"), 0, 0, axis_index_groups=among)
        return flat.reshape(value.shape)

    vmem = pl.BlockSpec(memory_space=pltpu.VMEM)
    hbm = pl.BlockSpec(memory_space=pltpu.HBM)
    in_hbm = functools.partial(pltpu.with_memory_space_constraint, memory_space=pltpu.HBM)
    in_vmem = functools.partial(pltpu.with_memory_space_constraint, memory_space=pltpu.VMEM)
    sources = latent.reshape(GROUPS, block_rows, model_width)
    stream_shape = (section_count, block_rows, block_cols)
    spread_shape = (section_count, slice_count, block_rows, block_cols)
    modulation = modulation.reshape(3, 1, model_width)
    norm_gain = norm_gain[0]
    table = own_cache.reshape(2, GROUPS, rows, local_width)
    named = (qkv_slice, out_slice, modulation, norm_gain, table)
    spread = pl.pallas_call(
        start_kernel,
        out_shape=jax.ShapeDtypeStruct((slice_count, block_rows, model_width), jnp.bfloat16),
        in_specs=[hbm] * (len(named) + 1),
        out_specs=vmem,
        scratch_shapes=[pltpu.SemaphoreType.DMA],
        compiler_params=pltpu.CompilerParams(vmem_limit_bytes=4 * 1024 * 1024),
    )(in_hbm(sources), *map(in_hbm, named))
    stale_rows = []
    if member_count > 1:
        stale_rows = [group_cache.swapaxes(0, 1).reshape(2, -1, local_width)]

    ticks = GROUPS + section_count - 1

    def attend(tick, features, table, partial_shape):
        operands = (
            features,
            in_vmem(modulation),
            in_vmem(qkv_slice),
            in_vmem(out_slice),
            in_vmem(norm_gain),
            *stale_rows,
            in_vmem(table),
        )
        return pl.pallas_call(
            functools.partial(
                tick_kernel,
                tick,
                (tok_dev, head_dim, member_count),
            ),
            out_shape=(
                jax.ShapeDtypeStruct(partial_shape, jnp.bfloat16),
                jax.ShapeDtypeStruct(table.shape, jnp.bfloat16),
            ),
            in_specs=[vmem] * len(operands),
            out_specs=(vmem, vmem),
            compiler_params=pltpu.CompilerParams(vmem_limit_bytes=24 * 1024 * 1024),
        )(*operands)

    def small(kernel, in_specs, *out_shapes):
        return pl.pallas_call(
            kernel,
            out_shape=tuple(jax.ShapeDtypeStruct(shape, jnp.bfloat16) for shape in out_shapes),
            in_specs=in_specs,
            out_specs=(vmem,) * len(out_shapes),
            compiler_params=pltpu.CompilerParams(vmem_limit_bytes=8 * 1024 * 1024),
        )

    closing_shape = (2, half, slice_count, block_rows, block_cols)
    features = lax.all_to_all(spread, "seq", 0, 0, axis_index_groups=in_slices)[None]
    pair_shape = (2, slice_count, block_rows, model_width // 2)
    partial_out, table = attend(0, features, table, pair_shape)
    parts = exchange(partial_out, pair_peers)
    (spread,) = small(settle_first_kernel, [vmem] * 2, pair_shape)(parts, in_vmem(sources))
    features = exchange(spread, pair_peers)
    streams = []
    for tick in range(1, ticks - 2):
        partial_out, table = attend(tick, features, table, spread_shape)
        held = [exchange(partial_out)] + streams
        stream, spread = small(settle_kernel, [vmem] * len(held), stream_shape, spread_shape)(*held)
        streams = [stream]
        features = exchange(spread)
    partial_out, table = attend(ticks - 2, features, table, spread_shape)
    (spread,) = small(
        functools.partial(settle_last_kernel, in_group), [vmem] * 2, spread_shape
    )(exchange(partial_out), *streams)
    features = exchange(spread)
    closing, table = attend(ticks - 1, features, table, closing_shape)
    closing = lax.all_to_all(
        closing.reshape((-1,) + closing_shape[3:]),
        ("cfg", "pipe", "seq"),
        0,
        0,
        axis_index_groups=closing_peers,
    ).reshape(closing_shape)
    guided, table = pl.pallas_call(
        functools.partial(guide_kernel, member_count),
        out_shape=(
            jax.ShapeDtypeStruct((tok_dev, model_width // 2), jnp.bfloat16),
            jax.ShapeDtypeStruct(table.shape, jnp.bfloat16),
        ),
        in_specs=[vmem, vmem],
        out_specs=(vmem, hbm),
        scratch_shapes=[pltpu.SemaphoreType.DMA],
        compiler_params=pltpu.CompilerParams(vmem_limit_bytes=8 * 1024 * 1024),
    )(closing, table)
    return (guided[None], table.reshape(stale_kv.shape))


def solution(mesh):
    placed = (
        P(None, "seq", None),
        P("pipe", "cfg", None, None),
        P("pipe", None, "seq"),
        P("pipe", "seq", None),
        P("pipe", None, None),
        P("pipe", "cfg", None, None, "seq", None, None, None),
    )
    return jax.shard_map(
        local,
        mesh=mesh,
        in_specs=placed,
        out_specs=(P("pipe", "seq", "cfg"), P("pipe", "cfg", None, None, "seq", None, None, None)),
        check_vma=False,
    )
```
